32 devices in a mesh: fsdp: 4 (over z), ctx: 4 (over y, x), tp: 2 (over core).
Axes of the slice: x: 2, y: 2, z: 4, core: 2. Of those that a mesh axis runs over, the one named last changes fastest.
Arguments:
- tokens: bfloat16 [4096, 2048], P(('fsdp', 'ctx')), may hold values from -6 to 6
- lengths: int32 [4], replicated, may hold values from 1024 to 1024, as said below
- dealing: int32 [4], replicated, may hold values from 0 to 3, as said below
- w_query: bfloat16 [2048, 2048], P(('fsdp', 'ctx'), 'tp'), may hold values from -0.25 to 0.25
- w_key: bfloat16 [2048, 2048], P(('fsdp', 'ctx'), 'tp'), may hold values from -0.125 to 0.125
- w_value: bfloat16 [2048, 2048], P(('fsdp', 'ctx'), 'tp'), may hold values from -0.125 to 0.125
- w_out: bfloat16 [2048, 2048], P(('fsdp', 'ctx'), 'tp'), may hold values from -1 to 1
- b_query: float32 [2048], P('tp'), may hold values from -3 to 3
- b_value: float32 [2048], P('tp'), may hold values from -0.3125 to 0.3125
- b_out: float32 [2048], replicated, may hold values from -1.25 to 1.25
- gain_mid: float32 [2048], replicated, may hold values from 0.25 to 1.75
- shift_mid: float32 [2048], replicated, may hold values from -1.25 to 1.25
- w_up: bfloat16 [2048, 8192], P(('fsdp', 'ctx'), 'tp'), may hold values from -0.125 to 0.125
- b_up: float32 [8192], P('tp'), may hold values from -1.25 to 1.25
- w_down: bfloat16 [2048, 8192], P(('fsdp', 'ctx'), 'tp'), may hold values from -0.0625 to 0.0625
- b_down: float32 [2048], replicated, may hold values from -1.25 to 1.25
- gain_end: float32 [2048], replicated, may hold values from 0.25 to 1.75
- shift_end: float32 [2048], replicated, may hold values from -1.25 to 1.25
- cotangent: bfloat16 [4096, 2048], P(('fsdp', 'ctx')), may hold values from -6 to 6
Outputs:
- output: bfloat16 [4096, 2048], P(('fsdp', 'ctx'))
- grad_tokens: bfloat16 [4096, 2048], P(('fsdp', 'ctx'))
- grad_query: float32 [2048, 2048], P(('fsdp', 'ctx'), 'tp')
- grad_key: float32 [2048, 2048], P(('fsdp', 'ctx'), 'tp')
- grad_value: float32 [2048, 2048], P(('fsdp', 'ctx'), 'tp')
- grad_out: float32 [2048, 2048], P(('fsdp', 'ctx'), 'tp')
- grad_bquery: float32 [2048], P('tp')
- grad_bvalue: float32 [2048], P('tp')
- grad_bout: float32 [2048], replicated
- grad_gmid: float32 [2048], replicated
- grad_smid: float32 [2048], replicated
- grad_up: float32 [2048, 8192], P(('fsdp', 'ctx'), 'tp')
- grad_bup: float32 [8192], P('tp')
- grad_down: float32 [2048, 8192], P(('fsdp', 'ctx'), 'tp')
- grad_bdown: float32 [2048], replicated
- grad_gend: float32 [2048], replicated
- grad_send: float32 [2048], replicated
The draws below stay inside these ranges and needn't reach their ends.
Inputs may be any that keep to these rules, and one draw needn't show every extreme that they name: `lengths`: in every draw some sequence has exactly 1024 live positions. `dealing`: A permutation: each sequence is held by exactly one group.
All inputs are finite; a program needn't handle non-finite values.
Results may differ from the reference program's by a relative error of at most 0.02.
The reference program's roundings to bfloat16 on the way count: a program that leaves them out, or rounds other values in their place, can miss the bound.
Values may be sent and summed in bfloat16 or wider, within the bound.
No kernel may reach another device: no remote copies, remote signals or barrier semaphores. Data moves between devices by JAX's collectives and lax.ppermute only.
A program may use at most 320 MiB of HBM per device.

```python
import math
import jax
import jax.numpy as jnp
from jax import lax

D = 2048
HEADS = 16
FF = 8192
HEAD = 128
MINLEN = 1024
GROUP_TOK = 1024
NSEQ = 4
TOKENS = 4096


def draw_lengths(key, part):
    sampled = jax.random.randint(jax.random.fold_in(key, 11), (NSEQ,), MINLEN, GROUP_TOK + 1, dtype=jnp.int32)
    longest = jax.random.randint(jax.random.fold_in(key, 12), (), 0, NSEQ, dtype=jnp.int32)
    return jnp.where(jnp.arange(NSEQ, dtype=jnp.int32) == longest, GROUP_TOK, sampled)


def draw_dealing(key, part):
    rotation = jax.random.randint(jax.random.fold_in(key, 21), (), 0, NSEQ, dtype=jnp.int32)
    group_ids = jnp.arange(NSEQ, dtype=jnp.int32)
    relative = (group_ids - rotation) % NSEQ
    half_way = NSEQ // 2
    mapped = jnp.where(relative == 0, NSEQ - 1, jnp.where(relative == NSEQ - 1, half_way - 1, jnp.where(relative == half_way - 1, half_way, jnp.where(relative == half_way, 0, relative))))
    return ((mapped + rotation) % NSEQ).astype(jnp.int32)


def level_of(rng, extent, shards, smallest, high):
    gain, own = 1.0, jax.random.fold_in(rng, 6)
    for position, parts in shards:
        heights = jnp.exp(jax.random.uniform(jax.random.fold_in(own, position), (parts,), jnp.float32, smallest / len(shards), high / len(shards)))
        gain = gain * jnp.repeat(heights, extent[position] // parts).reshape([-1 if axis == position else 1 for axis in range(len(extent))])
    return gain


def scatter_about(stream_key, dims, width, most, shards=(), kind=jnp.bfloat16):
    entries = jax.random.normal(stream_key, dims, jnp.float32) * width
    if len(shards) > 0:
        entries = level_of(stream_key, dims, shards, -0.22, 0.18) * entries
    return jnp.clip(entries, min=-most, max=most).astype(kind)


def setup_inputs(seed: int = 0) -> dict:
    keys = jax.random.split(jax.random.key(seed), 20)
    return {
        "tokens": scatter_about(keys[0], (TOKENS, D), 1.0, 6.0, ((0, 16),)),
        "lengths": draw_lengths(jax.random.fold_in(keys[19], 71), 0),
        "dealing": draw_dealing(jax.random.fold_in(keys[19], 71), 0),
        "w_query": scatter_about(keys[3], (D, D), (D // 4) ** -0.5, 0.25, ((0, 16), (1, 2))),
        "w_key": scatter_about(keys[4], (D, D), D ** -0.5, 0.125, ((0, 16), (1, 2))),
        "w_value": scatter_about(keys[5], (D, D), D ** -0.5, 0.125, ((0, 16), (1, 2))),
        "w_out": scatter_about(keys[6], (D, D), (D // 64) ** -0.5, 1.0, ((0, 16), (1, 2))),
        "b_query": scatter_about(keys[7], (D,), 0.5, 3.0, ((0, 2),), jnp.float32),
        "b_value": scatter_about(keys[8], (D,), 0.05, 0.3125, ((0, 2),), jnp.float32),
        "b_out": scatter_about(keys[9], (D,), 0.2, 1.25, (), jnp.float32),
        "gain_mid": jnp.clip(1.0 + 0.15 * jax.random.normal(keys[10], (D,), jnp.float32), 0.25, 1.75),
        "shift_mid": scatter_about(keys[11], (D,), 0.2, 1.25, (), jnp.float32),
        "w_up": scatter_about(keys[12], (D, FF), D ** -0.5, 0.125, ((0, 16), (1, 2))),
        "b_up": scatter_about(keys[13], (FF,), 0.2, 1.25, ((0, 2),), jnp.float32),
        "w_down": scatter_about(keys[14], (D, FF), FF ** -0.5, 0.0625, ((0, 16), (1, 2))),
        "b_down": scatter_about(keys[15], (D,), 0.2, 1.25, (), jnp.float32),
        "gain_end": jnp.clip(1.0 + 0.15 * jax.random.normal(keys[16], (D,), jnp.float32), 0.25, 1.75),
        "shift_end": scatter_about(keys[17], (D,), 0.2, 1.25, (), jnp.float32),
        "cotangent": scatter_about(keys[18], (TOKENS, D), 1.0, 6.0, ((0, 16),)),
    }


EPSILON = 1e-12
NEGATIVE = -1e+30
HIGH = lax.Precision.HIGHEST

@jax.custom_vjp
def low(v):
    return lax.optimization_barrier(v.astype(jnp.bfloat16)).astype(jnp.float32)

@jax.custom_vjp
def low_back(v):
    return v

def low_keep(v):
    return (low(v), None)

def low_pass(kept, grad):
    return (grad,)

def back_keep(v):
    return (v, None)

def back_low(kept, grad):
    return (low(grad),)
low.defvjp(low_keep, low_pass)
low_back.defvjp(back_keep, back_low)

def product(left, right):
    return jnp.dot(left, right, precision=HIGH, preferred_element_type=jnp.float32)

def layer_norm(inputs, gain_vec, shift_vec):
    row_mean = lax.optimization_barrier(jnp.mean(inputs, axis=-1, keepdims=True))
    centred = inputs - row_mean
    spread = lax.optimization_barrier(jnp.mean(centred * centred, axis=-1, keepdims=True))
    return centred * lax.rsqrt(spread + EPSILON) * gain_vec + shift_vec

def sequence(inputs, live_count, params):
    w_query, w_key, w_value, w_out, b_query, b_value, b_out, gain_mid, shift_mid, w_up, b_up, w_down, b_down, gain_end, shift_end = params
    seq_rows = inputs.shape[0]
    queries = low(low_back(product(inputs, w_query) + b_query)).reshape(seq_rows, HEADS, HEAD)
    keys_all = low(low_back(product(inputs, w_key))).reshape(seq_rows, HEADS, HEAD)
    values = low(low_back(product(inputs, w_value) + b_value)).reshape(seq_rows, HEADS, HEAD)
    row_live = jnp.arange(seq_rows, dtype=jnp.int32) < live_count
    block_rows = min(512, seq_rows)
    score_scale = 1.0 / math.sqrt(HEAD)

    def attend(first_row):
        query_part = lax.dynamic_slice_in_dim(queries, first_row, block_rows, 0)
        scores = jnp.einsum('qhd,khd->hqk', query_part, keys_all, precision=HIGH) * score_scale
        scores = low_back(scores)
        scores = jnp.where(row_live[None, None, :], scores, NEGATIVE)
        row_max = lax.optimization_barrier(jnp.max(scores, axis=-1, keepdims=True))
        row_total = lax.optimization_barrier(jnp.sum(jnp.exp(scores - row_max), axis=-1, keepdims=True))
        weights = low(jnp.exp(scores - row_max - jnp.log(row_total)))
        return jnp.einsum('hqk,khd->qhd', weights, values, precision=HIGH)
    starts = jnp.arange(0, seq_rows, block_rows, dtype=jnp.int32)
    attended = lax.map(jax.checkpoint(attend), starts).reshape(seq_rows, D)
    attended = low(low_back(attended))
    branch = low_back(product(attended, w_out.T) + b_out)
    middle = layer_norm(inputs + branch, gain_mid, shift_mid)
    hidden = low_back(product(low(middle), w_up) + b_up)
    active = low(jax.nn.gelu(hidden, approximate=True))
    result = low_back(product(active, w_down.T) + b_down)
    normed = layer_norm(middle + result, gain_end, shift_end)
    return jnp.where(row_live[:, None], normed, 0.0)

def reference(tokens, lengths, dealing, w_query, w_key, w_value, w_out, b_query, b_value, b_out, gain_mid, shift_mid, w_up, b_up, w_down, b_down, gain_end, shift_end, cotangent):
    seq_count = dealing.shape[0]
    seq_rows = tokens.shape[0] // seq_count
    by_seq = tokens.astype(jnp.float32).reshape(seq_count, seq_rows, D)
    dealt_rows = by_seq[dealing]
    dealt_live = lengths[dealing]
    params = tuple((weight.astype(jnp.float32) for weight in (w_query, w_key, w_value, w_out, b_query, b_value, b_out, gain_mid, shift_mid, w_up, b_up, w_down, b_down, gain_end, shift_end)))

    def forward(inputs, weight_set):

        def one_seq(carried, seq_pair):
            return (carried, sequence(seq_pair[0], seq_pair[1], weight_set))
        return lax.scan(one_seq, jnp.zeros((), jnp.float32), (inputs, dealt_live))[1]
    normed, pullback = jax.vjp(forward, dealt_rows, params)
    grad_rows, grad_params = pullback(cotangent.astype(jnp.float32).reshape(seq_count, seq_rows, D))
    grad_tokens = jnp.zeros_like(grad_rows).at[dealing].set(grad_rows)
    output = normed.reshape(-1, D).astype(jnp.bfloat16)
    return (output, grad_tokens.reshape(-1, D).astype(jnp.bfloat16), grad_params[0], grad_params[1], grad_params[2], grad_params[3], grad_params[4], grad_params[5], grad_params[6], grad_params[7], grad_params[8], grad_params[9], grad_params[10], grad_params[11], grad_params[12], grad_params[13], grad_params[14])
```

```python
import math

import jax
import jax.numpy as jnp
from jax import lax
from jax.sharding import Mesh
from jax.sharding import PartitionSpec as P

HEAD = 128
EPSILON = 1e-12
NEGATIVE = -1e30
WIDE = jnp.float32
LOWER = jnp.bfloat16

TEAM = ("l", "x")
ROWS = ("h", "l", "y", "x")


def dot(left, right, dims):
    return lax.dot_general(left, right, (dims, ((), ())), preferred_element_type=WIDE)


def mm(left, right):
    return dot(left, right, ((1,), (0,)))


def mm_nt(left, right):
    return dot(left, right, ((1,), (1,)))


def mm_tn(left, right):
    return dot(left, right, ((0,), (0,)))


class Team:
    def __init__(self):
        self.sizes = {name: lax.axis_size(name) for name in ROWS + ("tp",)}
        self.at = {name: lax.axis_index(name) for name in ROWS + ("tp",)}
        ls, xs = self.sizes["l"], self.sizes["x"]
        self.offsets = [(dl, dx) for dl in range(ls) for dx in range(xs)]
        self.members = ls * xs

    def shift(self, value, offset, back=False):
        ls, xs = self.sizes["l"], self.sizes["x"]
        dl, dx = offset
        if back:
            dl, dx = -dl, -dx
        perm = [
            (l * xs + x, ((l + dl) % ls) * xs + (x + dx) % xs) for l in range(ls) for x in range(xs)
        ]
        return lax.ppermute(value, TEAM, perm)

    def ring(self, value, name, step):
        size = self.sizes[name]
        return lax.ppermute(value, name, [(i, (i + step) % size) for i in range(size)])

    def slot(self, offset, back=True):
        ls, xs = self.sizes["l"], self.sizes["x"]
        dl, dx = offset
        if back:
            dl, dx = -dl, -dx
        return lax.rem(self.at["l"] + dl + ls, ls) * xs + lax.rem(self.at["x"] + dx + xs, xs)


def swap_home(value):
    perm = [(l * 2 + y, y * 2 + l) for l in range(2) for y in range(2)]
    return lax.ppermute(value, ("l", "y"), perm)


def gather_rows(team, piece):
    pieces = [piece] + [team.shift(piece, offset) for offset in team.offsets[1:]]
    half = jnp.concatenate(pieces, axis=0)
    halves = [half] + [team.ring(half, "tp", step) for step in range(1, team.sizes["tp"])]
    return jnp.concatenate(halves, axis=0)


def row_blocks(team):
    ts = team.sizes["tp"]
    return [
        team.slot(offset) * ts + lax.rem(team.at["tp"] - step + ts, ts)
        for step in range(ts)
        for offset in team.offsets
    ]


def scatter_rows(team, product, row_count):
    ts, members = team.sizes["tp"], team.members
    half_rows = members * row_count
    total = product(0, half_rows)
    for step in range(1, ts):
        sent = product(step * half_rows, half_rows).astype(LOWER)
        total = total + team.ring(sent, "tp", -step).astype(WIDE)
    own = total[:row_count]
    for j, offset in enumerate(team.offsets):
        if j > 0:
            sent = total[j * row_count : (j + 1) * row_count].astype(LOWER)
            own = own + team.shift(sent, offset, back=True).astype(WIDE)
    return own


def put(buffer, value, starts):
    return lax.dynamic_update_slice(buffer, value, starts)


def gather_weights(team, shards):
    hs, ls, xs = (team.sizes[name] for name in ("h", "l", "x"))
    height = shards[0].shape[0]
    widths = [shard.shape[1] // team.members for shard in shards]
    width = sum(widths)

    def cut(slot):
        return jnp.concatenate(
            [
                lax.dynamic_slice_in_dim(shard, slot * each, each, 1)
                for shard, each in zip(shards, widths)
            ],
            axis=1,
        )

    zero = jnp.int32(0)
    near = jnp.zeros((team.members, height, width), LOWER)
    for j, offset in enumerate(team.offsets):
        piece = cut(team.slot(offset, back=False))
        if j > 0:
            piece = team.shift(piece, offset)
        near = put(near, piece[None], (team.slot(offset), zero, zero))
    near = near.reshape(1, ls, 1, xs * height, width)
    full = jnp.zeros((hs, ls, 2, xs * height, width), LOWER)
    for step in range(hs):
        row = lax.rem(team.at["h"] - step + hs, hs)
        block = team.ring(near, "h", step) if step else near
        full = put(full, block, (row, zero, team.at["y"], zero, zero))
        full = put(full, team.ring(block, "y", 1), (row, zero, 1 - team.at["y"], zero, zero))
    return full.reshape(-1, width)


def scatter_weights(team, grad, widths):
    hs, ls, xs = (team.sizes[name] for name in ("h", "l", "x"))
    width = grad.shape[1]
    height = grad.shape[0] // (hs * ls * 2 * xs)
    grad = grad.reshape(hs, ls, 2, xs * height, width)
    sent = lax.dynamic_slice_in_dim(grad, 1 - team.at["y"], 1, 2).astype(LOWER)
    mine = lax.dynamic_slice_in_dim(grad, team.at["y"], 1, 2)
    mine = mine + team.ring(sent, "y", 1).astype(WIDE)
    total = lax.dynamic_slice_in_dim(mine, team.at["h"], 1, 0)
    for step in range(1, hs):
        row = lax.rem(team.at["h"] + step, hs)
        sent = lax.dynamic_slice_in_dim(mine, row, 1, 0).astype(LOWER)
        total = total + team.ring(sent, "h", step).astype(WIDE)
    total = total.reshape(team.members, height, width)
    outs = [jnp.zeros((height, team.members, each), WIDE) for each in widths]
    for j, offset in enumerate(team.offsets):
        piece = lax.dynamic_slice_in_dim(total, team.slot(offset, back=False), 1, 0)[0]
        if j > 0:
            piece = team.shift(piece.astype(LOWER), offset).astype(WIDE)
        first = 0
        for i, each in enumerate(widths):
            block = piece[:, first : first + each][:, None]
            outs[i] = put(outs[i], block, (0, team.slot(offset), 0))
            first += each
    return [out.reshape(height, -1) for out in outs]


def pick(table, index):
    ids = jnp.arange(table.shape[0], dtype=jnp.int32)
    return jnp.sum(jnp.where(ids == index, table, 0))


def choose(pieces, index):
    out = pieces[0]
    for i in range(1, len(pieces)):
        out = jnp.where(index == i, pieces[i], out)
    return out


def spread_h(team, piece):
    return [piece] + [team.ring(piece, "h", step) for step in range(1, team.sizes["h"])]


def deal_in(team, home, piece):
    hs = team.sizes["h"]
    pieces = spread_h(team, piece)
    got = []
    for flip in range(2):
        target = team.at["l"] if flip == 0 else 1 - team.at["l"]
        group = pick(home, team.at["h"] * 2 + target)
        sent = choose(pieces, lax.rem(team.at["h"] - group // 2 + hs, hs))
        perm = [
            (l * 2 + y, y * 2 + (l if flip == 0 else 1 - l)) for l in range(2) for y in range(2)
        ]
        got.append(lax.ppermute(sent, ("l", "y"), perm))
    group = pick(home, team.at["h"] * 2 + team.at["y"])
    return jnp.where(lax.rem(group, 2) == team.at["y"], got[0], got[1])


def deal_out(team, dealing, piece):
    hs = team.sizes["h"]
    pieces = spread_h(team, piece)
    got = []
    for flip in range(2):
        target = team.at["y"] if flip == 0 else 1 - team.at["y"]
        seq = pick(dealing, team.at["h"] * 2 + target)
        sent = choose(pieces, lax.rem(team.at["h"] - seq // 2 + hs, hs))
        perm = [
            (l * 2 + y, (y if flip == 0 else 1 - y) * 2 + l) for l in range(2) for y in range(2)
        ]
        got.append(lax.ppermute(sent, ("l", "y"), perm))
    seq = pick(dealing, team.at["h"] * 2 + team.at["l"])
    return jnp.where(lax.rem(seq, 2) == team.at["l"], got[0], got[1])


def join_cores(team, piece):
    ts = team.sizes["tp"]
    out = jnp.zeros((ts,) + piece.shape, piece.dtype)
    for step in range(ts):
        other = team.ring(piece, "tp", step) if step else piece
        out = put(out, other[None], (lax.rem(team.at["tp"] - step + ts, ts), 0, 0))
    return out.reshape(-1, piece.shape[-1])


def layer_norm(inputs, gain_vec, shift_vec):
    row_mean = jnp.mean(inputs, axis=-1, keepdims=True)
    centred = inputs - row_mean
    spread = jnp.mean(centred * centred, axis=-1, keepdims=True)
    rate = lax.rsqrt(spread + EPSILON)
    xhat = centred * rate
    return xhat * gain_vec + shift_vec, xhat, rate


def layer_norm_back(grad, gain_vec, xhat, rate):
    scaled = grad * gain_vec
    return rate * (
        scaled
        - jnp.mean(scaled, axis=-1, keepdims=True)
        - xhat * jnp.mean(scaled * xhat, axis=-1, keepdims=True)
    )


def gelu_tanh(inputs):
    return jax.nn.gelu(inputs, approximate=True)


def local(
    tokens,
    lengths,
    dealing,
    w_query,
    w_key,
    w_value,
    w_out,
    b_query,
    b_value,
    b_out,
    gain_mid,
    shift_mid,
    w_up,
    b_up,
    w_down,
    b_down,
    gain_end,
    shift_end,
    cotangent,
):
    team = Team()
    ts, members = team.sizes["tp"], team.members
    row_count = tokens.shape[0] // ts
    key_count = row_count * ts * members
    wide = w_query.shape[1] // members
    heads_here = wide // HEAD
    score_scale = 1.0 / math.sqrt(HEAD)
    my_slot = team.at["l"] * team.sizes["x"] + team.at["x"]
    seq_ids = jnp.arange(dealing.shape[0], dtype=jnp.int32)
    home = jnp.sum(jnp.where(dealing[None, :] == seq_ids[:, None], seq_ids[None, :], 0), axis=1)
    live_count = pick(lengths, team.at["h"] * 2 + team.at["y"])
    position = jnp.concatenate(
        [block * row_count + jnp.arange(row_count, dtype=jnp.int32) for block in row_blocks(team)]
    )
    key_live = position < live_count
    query_live = key_live[:row_count, None]
    half_at = team.at["tp"] * row_count

    own = swap_home(lax.dynamic_slice_in_dim(tokens, half_at, row_count, 0))
    inputs = gather_rows(team, own)
    attn_mat = gather_weights(team, [w_query, w_key, w_value, w_out])
    up_mat = gather_weights(team, [w_up])
    down_mat = gather_weights(team, [w_down])
    bias_q = lax.dynamic_slice_in_dim(b_query, my_slot * wide, wide, 0)
    bias_v = lax.dynamic_slice_in_dim(b_value, my_slot * wide, wide, 0)
    tall = w_up.shape[1] // members
    bias_up = lax.dynamic_slice_in_dim(b_up, my_slot * tall, tall, 0)
    qkv_mat = attn_mat[:, : 3 * wide]
    out_mat = attn_mat[:, 3 * wide :]

    bias_qkv = jnp.concatenate([bias_q, jnp.zeros_like(bias_q), bias_v])
    qkv = (mm(inputs, qkv_mat) + bias_qkv).astype(LOWER)
    heads = []
    attended = []
    for i in range(heads_here):
        query, key, value = (
            qkv[:, part * wide + i * HEAD : part * wide + (i + 1) * HEAD] for part in range(3)
        )
        scores = jnp.where(key_live[None, :], mm_nt(query, key) * score_scale, NEGATIVE)
        row_max = jnp.max(scores, axis=-1, keepdims=True)
        log_sum = jnp.log(jnp.sum(jnp.exp(scores - row_max), axis=-1, keepdims=True)) + row_max
        probs = jnp.exp(scores - log_sum)
        attended.append(mm(probs.astype(LOWER), value))
        heads.append((query, key, value, log_sum))
    attended_b = jnp.concatenate(attended, axis=1).astype(LOWER)

    def out_product(first, count):
        return mm_nt(attended_b[first : first + count], out_mat)

    branch = scatter_rows(team, out_product, row_count) + b_out
    middle, mid_hat, mid_rate = layer_norm(own.astype(WIDE) + branch, gain_mid, shift_mid)
    middle_all = gather_rows(team, middle.astype(LOWER))
    hidden = mm(middle_all, up_mat) + bias_up
    active_b = gelu_tanh(hidden).astype(LOWER)

    def down_product(first, count):
        return mm_nt(active_b[first : first + count], down_mat)

    result = scatter_rows(team, down_product, row_count) + b_down
    normed, end_hat, end_rate = layer_norm(middle + result, gain_end, shift_end)
    output_own = jnp.where(query_live, normed, 0.0).astype(LOWER)
    output = join_cores(team, deal_out(team, dealing, output_own))

    cot_half = lax.dynamic_slice_in_dim(cotangent, half_at, row_count, 0)
    cot = deal_in(team, home, cot_half).astype(WIDE)
    grad_normed = jnp.where(query_live, cot, 0.0)
    grad_gend = jnp.sum(grad_normed * end_hat, axis=0)
    grad_send = jnp.sum(grad_normed, axis=0)
    grad_sum = layer_norm_back(grad_normed, gain_end, end_hat, end_rate)
    grad_result = grad_sum.astype(LOWER)
    grad_bdown = jnp.sum(grad_result.astype(WIDE), axis=0)
    result_all = gather_rows(team, grad_result)
    grad_active = mm(result_all, down_mat)
    gelu_back = jax.vjp(gelu_tanh, hidden)[1]
    grad_hidden = gelu_back(grad_active)[0].astype(LOWER)

    def up_product(first, count):
        return mm_nt(grad_hidden[first : first + count], up_mat)

    grad_middle = grad_sum + scatter_rows(team, up_product, row_count)
    grad_bup = jnp.sum(grad_hidden.astype(WIDE), axis=0)
    grad_down = scatter_weights(team, mm_tn(result_all, active_b), [tall])[0]
    grad_up = scatter_weights(team, mm_tn(middle_all, grad_hidden), [tall])[0]

    grad_gmid = jnp.sum(grad_middle * mid_hat, axis=0)
    grad_smid = jnp.sum(grad_middle, axis=0)
    grad_inner = layer_norm_back(grad_middle, gain_mid, mid_hat, mid_rate)
    grad_branch = grad_inner.astype(LOWER)
    grad_bout = jnp.sum(grad_branch.astype(WIDE), axis=0)
    branch_all = gather_rows(team, grad_branch)
    grad_attended = mm(branch_all, out_mat).astype(LOWER)
    parts = [[], [], []]
    for i in range(heads_here):
        query, key, value, log_sum = heads[i]
        grad_head = grad_attended[:, i * HEAD : (i + 1) * HEAD]
        scores = jnp.where(key_live[None, :], mm_nt(query, key) * score_scale, NEGATIVE)
        probs = jnp.exp(scores - log_sum)
        grad_probs = mm_nt(grad_head, value)
        delta = jnp.sum(probs * grad_probs, axis=-1, keepdims=True)
        grad_scores = (probs * (grad_probs - delta)).astype(LOWER)
        parts[0].append(mm(grad_scores, key) * score_scale)
        parts[1].append(mm_tn(grad_scores, query) * score_scale)
        parts[2].append(mm_tn(probs.astype(LOWER), grad_head))
    grad_qkv = jnp.concatenate(parts[0] + parts[1] + parts[2], axis=1).astype(LOWER)

    def in_product(first, count):
        return mm_nt(grad_qkv[first : first + count], qkv_mat)

    grad_own = (scatter_rows(team, in_product, row_count) + grad_inner).astype(LOWER)
    grad_tokens = join_cores(team, swap_home(grad_own))
    grad_attn = jnp.concatenate([mm_tn(inputs, grad_qkv), mm_tn(branch_all, attended_b)], axis=1)
    grad_query, grad_key, grad_value, grad_out = scatter_weights(team, grad_attn, [wide] * 4)

    qkv_sum = jnp.sum(grad_qkv.astype(WIDE), axis=0)
    zeros = jnp.zeros((members, 1), WIDE)
    by_slot = [
        put(zeros * part[None], part[None], (my_slot, 0)).reshape(-1)
        for part in (qkv_sum[:wide], qkv_sum[2 * wide :], grad_bup)
    ]
    by_row = jnp.concatenate(
        [grad_bout, grad_gmid, grad_smid, grad_bdown, grad_gend, grad_send]
    ).reshape(-1, 128)
    by_row = lax.psum(by_row, "tp").reshape(-1)
    sums = lax.psum(jnp.concatenate(by_slot + [by_row]).reshape(-1, 128), ROWS).reshape(-1)
    smalls = []
    first = 0
    for size in [b_query.shape[0], b_value.shape[0], b_up.shape[0]] + [b_out.shape[0]] * 6:
        smalls.append(sums[first : first + size])
        first += size
    return (
        output,
        grad_tokens,
        grad_query,
        grad_key,
        grad_value,
        grad_out,
        smalls[0],
        smalls[1],
        smalls[3],
        smalls[4],
        smalls[5],
        grad_up,
        smalls[2],
        grad_down,
        smalls[6],
        smalls[7],
        smalls[8],
    )


def solution(mesh):
    fsdp, ctx, tp = (mesh.shape[name] for name in ("fsdp", "ctx", "tp"))
    fine = Mesh(mesh.devices.reshape(fsdp // 2, 2, 2, ctx // 2, tp), ROWS + ("tp",))
    rows, split = P(ROWS, None), P(ROWS, "tp")
    in_specs = (
        (rows, P(), P())
        + (split,) * 4
        + (P("tp"), P("tp"), P(), P(), P(), split, P("tp"), split, P(), P(), P(), rows)
    )
    out_specs = (
        (rows, rows)
        + (split,) * 4
        + (P("tp"), P("tp"), P(), P(), P(), split, P("tp"), split, P(), P(), P())
    )
    return jax.shard_map(local, mesh=fine, in_specs=in_specs, out_specs=out_specs, check_vma=False)
```

```python
import functools
import math

import jax
import jax.numpy as jnp
from jax import lax
from jax.experimental import pallas as pl
from jax.experimental.pallas import tpu as pltpu
from jax.sharding import Mesh
from jax.sharding import PartitionSpec as P

HEAD = 128
EPSILON = 1e-12
NEGATIVE = -1e30
WIDE = jnp.float32
LOWER = jnp.bfloat16

TEAM = ("l", "x")
ROWS = ("h", "l", "y", "x")


def dot(left, right, dims):
    return lax.dot_general(left, right, (dims, ((), ())), preferred_element_type=WIDE)


def mm(left, right):
    return dot(left, right, ((1,), (0,)))


def mm_nt(left, right):
    return dot(left, right, ((1,), (1,)))


def mm_tn(left, right):
    return dot(left, right, ((0,), (0,)))


class Team:
    def __init__(self):
        self.sizes = {name: lax.axis_size(name) for name in ROWS + ("tp",)}
        self.at = {name: lax.axis_index(name) for name in ROWS + ("tp",)}
        ls, xs = self.sizes["l"], self.sizes["x"]
        self.offsets = [(dl, dx) for dl in range(ls) for dx in range(xs)]
        self.members = ls * xs

    def shift(self, value, offset, back=False):
        with jax.named_scope("team%d%d" % offset):
            return self.shift_(value, offset, back)

    def shift_(self, value, offset, back):
        ls, xs = self.sizes["l"], self.sizes["x"]
        dl, dx = offset
        if back:
            dl, dx = -dl, -dx
        perm = [
            (l * xs + x, ((l + dl) % ls) * xs + (x + dx) % xs) for l in range(ls) for x in range(xs)
        ]
        return lax.ppermute(value, TEAM, perm)

    def ring(self, value, name, step):
        size = self.sizes[name]
        with jax.named_scope("ring_" + name):
            return lax.ppermute(value, name, [(i, (i + step) % size) for i in range(size)])

    def slot(self, offset, back=True):
        ls, xs = self.sizes["l"], self.sizes["x"]
        dl, dx = offset
        if back:
            dl, dx = -dl, -dx
        return lax.rem(self.at["l"] + dl + ls, ls) * xs + lax.rem(self.at["x"] + dx + xs, xs)


def fence(*values):
    return lax.optimization_barrier(values)


def swap_home(value):
    perm = [(l * 2 + y, y * 2 + l) for l in range(2) for y in range(2)]
    return lax.ppermute(value, ("l", "y"), perm)


def team_pieces(team, piece):
    return [piece] + [team.shift(piece, offset) for offset in team.offsets[1:]]


def cores(team, value):
    return [team.ring(value, "tp", step) for step in range(1, team.sizes["tp"])]


def row_blocks(team):
    ts = team.sizes["tp"]
    return [
        team.slot(offset) * ts + lax.rem(team.at["tp"] - step + ts, ts)
        for step in range(ts)
        for offset in team.offsets
    ]


def core_send(team, product, half_rows):
    got = []
    for step in range(1, team.sizes["tp"]):
        sent = product(step * half_rows, half_rows).astype(LOWER)
        got.append(team.ring(sent, "tp", -step))
    return got


def core_total(team, product, half_rows, got):
    total = product(0, half_rows)
    for value in got:
        total = total + value.astype(WIDE)
    row_count = half_rows // team.members
    sent = [
        total[j * row_count : (j + 1) * row_count].astype(LOWER) for j in range(1, team.members)
    ]
    return total[:row_count], sent


def team_send(team, sent):
    return [
        team.shift(value, offset, back=True) for value, offset in zip(sent, team.offsets[1:])
    ]


def team_total(own, got):
    for value in got:
        own = own + value.astype(WIDE)
    return own


def put(buffer, value, starts):
    return lax.dynamic_update_slice(buffer, value, starts)


def share_columns(team, shards):
    widths = [shard.shape[1] // team.members for shard in shards]
    pieces = []
    for j, offset in enumerate(team.offsets):
        slot = team.slot(offset, back=False)
        cuts = [
            lax.dynamic_slice_in_dim(shard, slot * each, each, 1)
            for shard, each in zip(shards, widths)
        ]
        piece = jnp.concatenate(cuts, axis=1)
        pieces.append(team.shift(piece, offset) if j > 0 else piece)
    return pieces


def near_rows(team, pieces, first, width):
    near = jnp.zeros((team.members, pieces[0].shape[0], width), LOWER)
    for piece, offset in zip(pieces, team.offsets):
        near = put(near, piece[None, :, first : first + width], (team.slot(offset), 0, 0))
    return near.reshape(-1, width)


def across(team, value):
    return [team.ring(value, "h", -step) for step in range(1, team.sizes["h"])]


def beside(team, values):
    return [team.ring(value, "y", 1) for value in values]


def halves(value):
    middle = value.shape[0] // 2
    return value[:middle], value[middle:]


def pairs(firsts, seconds):
    return [part for pair in zip(firsts, seconds) for part in pair]


class Grads:
    def __init__(self, team, product, rows, name):
        self.team, self.product, self.name = team, product, name
        self.far = rows // 2
        self.near = self.far // team.sizes["h"]

    def send_far(self):
        return self.product(self.far + self.near, self.far - self.near).astype(LOWER)

    def send_near(self):
        return self.product(self.far, self.near).astype(LOWER)

    def cross(self, got):
        mine = self.product(self.near, self.far - self.near) + got.astype(WIDE)
        mine = mine.astype(LOWER)
        return [
            mine[step * self.near : (step + 1) * self.near]
            for step in range(self.team.sizes["h"] - 1)
        ]

    def go(self, sent):
        return [self.team.ring(value, "h", step) for step, value in enumerate(sent, 1)]

    def total(self, got, crossed):
        mine = self.product(0, self.near) + got.astype(WIDE)
        for value in crossed:
            mine = mine + value.astype(WIDE)
        return mine


def home_pieces(team, total):
    height = total.shape[0] // team.members
    total = total.reshape(team.members, height, -1)
    pieces = []
    for j, offset in enumerate(team.offsets):
        piece = lax.dynamic_index_in_dim(total, team.slot(offset, back=False), 0, False)
        pieces.append(team.shift(piece.astype(LOWER), offset) if j > 0 else piece)
    return pieces


def home_join(team, pieces, widths):
    slots = [team.slot(offset) for offset in team.offsets]
    outs = []
    first = 0
    for each in widths:
        blocks = []
        for slot in range(team.members):
            block = pieces[0][:, first : first + each]
            for piece, at in zip(pieces[1:], slots[1:]):
                other = piece[:, first : first + each].astype(WIDE)
                block = jnp.where(at == slot, other, block)
            blocks.append(block)
        outs.append(jnp.concatenate(blocks, axis=1))
        first += each
    return outs


def to_team_order(team, value):
    hs = team.sizes["h"]
    count = value.shape[0]
    value = value.reshape(count, hs, 2, 2, -1).transpose(0, 3, 1, 2, 4)
    value = jnp.roll(value, (-team.at["y"], -team.at["h"]), (1, 2))
    return value.reshape(count, -1)


def from_team_order(team, value):
    hs = team.sizes["h"]
    count = value.shape[0]
    value = value.reshape(count, 2, hs, 2, -1)
    value = jnp.roll(value, (team.at["y"], team.at["h"]), (1, 2))
    return value.transpose(0, 2, 3, 1, 4).reshape(count, -1)


def pick(table, index):
    ids = jnp.arange(table.shape[0], dtype=jnp.int32)
    return jnp.sum(jnp.where(ids == index, table, 0))


def choose(pieces, index):
    out = pieces[0]
    for i in range(1, len(pieces)):
        out = jnp.where(index == i, pieces[i], out)
    return out


def spread_h(team, piece):
    return [piece] + [team.ring(piece, "h", step) for step in range(1, team.sizes["h"])]


def deal(team, table, pieces, inward):
    hs = team.sizes["h"]
    place = team.at["l"] if inward else team.at["y"]
    got = []
    for flip in range(2):
        source = pick(table, team.at["h"] * 2 + (place if flip == 0 else 1 - place))
        sent = choose(pieces, lax.rem(team.at["h"] - source // 2 + hs, hs))
        perm = []
        for l in range(2):
            for y in range(2):
                if inward:
                    perm.append((l * 2 + y, y * 2 + (l if flip == 0 else 1 - l)))
                else:
                    perm.append((l * 2 + y, (y if flip == 0 else 1 - y) * 2 + l))
        with jax.named_scope("flip"):
            got.append(lax.ppermute(sent, ("l", "y"), perm))
    return got


def pick_dealt(team, table, got, inward):
    place = team.at["y"] if inward else team.at["l"]
    source = pick(table, team.at["h"] * 2 + place)
    return jnp.where(lax.rem(source, 2) == place, got[0], got[1])


def join_cores(team, piece):
    ts = team.sizes["tp"]
    out = jnp.zeros((ts,) + piece.shape, piece.dtype)
    for step in range(ts):
        other = team.ring(piece, "tp", step) if step else piece
        out = put(out, other[None], (lax.rem(team.at["tp"] - step + ts, ts), 0, 0))
    return out.reshape(-1, piece.shape[-1])


def layer_norm(inputs, gain_vec, shift_vec):
    row_mean = jnp.mean(inputs, axis=-1, keepdims=True)
    centred = inputs - row_mean
    spread = jnp.mean(centred * centred, axis=-1, keepdims=True)
    rate = lax.rsqrt(spread + EPSILON)
    xhat = centred * rate
    return xhat * gain_vec + shift_vec, xhat, rate


def layer_norm_back(grad, gain_vec, xhat, rate):
    scaled = grad * gain_vec
    return rate * (
        scaled
        - jnp.mean(scaled, axis=-1, keepdims=True)
        - xhat * jnp.mean(scaled * xhat, axis=-1, keepdims=True)
    )


def gelu_tanh(inputs):
    return jax.nn.gelu(inputs, approximate=True)


def masked_scores(key_ref, query, limits_ref, scale):
    count = limits_ref.shape[0]
    height = key_ref.shape[0] // count
    blocks = []
    for j in range(count):
        block = mm_nt(key_ref[j * height : (j + 1) * height, :], query) * scale
        row = lax.broadcasted_iota(jnp.int32, block.shape, 0)
        blocks.append(jnp.where(row < limits_ref[j], block, NEGATIVE))
    return blocks


def attend_kernel(scale, limits_ref, query_ref, key_ref, value_ref, out_ref, log_ref):
    blocks = masked_scores(key_ref, query_ref[...], limits_ref, scale)
    row_max = functools.reduce(jnp.maximum, blocks)
    row_max = jnp.max(row_max, axis=0, keepdims=True)
    blocks = [jnp.exp(block - row_max) for block in blocks]
    total = jnp.sum(functools.reduce(jnp.add, blocks), axis=0, keepdims=True)
    inverse = 1.0 / total
    height = key_ref.shape[0] // len(blocks)
    out = None
    for j, block in enumerate(blocks):
        value = value_ref[j * height : (j + 1) * height, :]
        term = mm_tn(value, (block * inverse).astype(LOWER))
        out = term if out is None else out + term
    out_ref[...] = out.T.astype(LOWER)
    log_ref[0] = row_max + jnp.log(total)


def attend_back_kernel(
    scale, wide, limits_ref, query_ref, key_ref, value_ref, grad_ref, log_ref, out_ref, key_sum, value_sum
):
    head, step = pl.program_id(0), pl.program_id(1)
    query, grad = query_ref[...], grad_ref[...]
    blocks = masked_scores(key_ref, query, limits_ref, scale)
    count = len(blocks)
    height = key_ref.shape[0] // count
    part = [slice(j * height, (j + 1) * height) for j in range(count)]
    log_sum = log_ref[0]
    probs = [jnp.exp(block - log_sum) for block in blocks]
    grad_probs = [mm_nt(value_ref[rows, :], grad) for rows in part]
    delta = functools.reduce(jnp.add, [p * g for p, g in zip(probs, grad_probs)])
    delta = jnp.sum(delta, axis=0, keepdims=True)

    @pl.when(step == 0)
    def _():
        key_sum[...] = jnp.zeros_like(key_sum)
        value_sum[...] = jnp.zeros_like(value_sum)

    grad_query = None
    for j, rows in enumerate(part):
        scores = (probs[j] * (grad_probs[j] - delta)).astype(LOWER)
        term = mm_tn(key_ref[rows, :], scores)
        grad_query = term if grad_query is None else grad_query + term
        key_sum[rows, :] += mm(scores, query)
        value_sum[rows, :] += mm(probs[j].astype(LOWER), grad)
    count = query.shape[0]
    first = pl.multiple_of(step * count, count)
    column = pl.multiple_of(head * HEAD, HEAD)
    out_ref[pl.ds(first, count), pl.ds(column, HEAD)] = (grad_query.T * scale).astype(LOWER)

    @pl.when(step == pl.num_programs(1) - 1)
    def _():
        out_ref[:, pl.ds(wide + column, HEAD)] = (key_sum[...] * scale).astype(LOWER)
        out_ref[:, pl.ds(2 * wide + column, HEAD)] = value_sum[...].astype(LOWER)


LIGHT = pl.CostEstimate(flops=1000000, bytes_accessed=100000, transcendentals=0)
KERNEL = pltpu.CompilerParams(vmem_limit_bytes=24 * 1024 * 1024)


def query_block(rows):
    return min(256, rows)


def attend(qkv, limits, scale):
    rows, wide = qkv.shape[0], qkv.shape[1] // 3
    heads, block = wide // HEAD, query_block(rows)
    return pl.pallas_call(
        functools.partial(attend_kernel, scale),
        grid=(heads, rows // block),
        in_specs=[
            pl.BlockSpec(memory_space=pltpu.SMEM),
            pl.BlockSpec((block, HEAD), lambda h, i: (i, h)),
            pl.BlockSpec((rows, HEAD), lambda h, i: (0, heads + h)),
            pl.BlockSpec((rows, HEAD), lambda h, i: (0, 2 * heads + h)),
        ],
        out_specs=[
            pl.BlockSpec((block, HEAD), lambda h, i: (i, h)),
            pl.BlockSpec((1, 1, block), lambda h, i: (h, 0, i)),
        ],
        out_shape=[
            jax.ShapeDtypeStruct((rows, wide), LOWER),
            jax.ShapeDtypeStruct((heads, 1, rows), WIDE),
        ],
        cost_estimate=LIGHT,
        compiler_params=KERNEL,
    )(limits, qkv, qkv, qkv)


def attend_back(qkv, grad, log_sum, limits, scale):
    rows, wide = grad.shape
    heads, block = wide // HEAD, query_block(rows)
    return pl.pallas_call(
        functools.partial(attend_back_kernel, scale, wide),
        grid=(heads, rows // block),
        in_specs=[
            pl.BlockSpec(memory_space=pltpu.SMEM),
            pl.BlockSpec((block, HEAD), lambda h, i: (i, h)),
            pl.BlockSpec((rows, HEAD), lambda h, i: (0, heads + h)),
            pl.BlockSpec((rows, HEAD), lambda h, i: (0, 2 * heads + h)),
            pl.BlockSpec((block, HEAD), lambda h, i: (i, h)),
            pl.BlockSpec((1, 1, block), lambda h, i: (h, 0, i)),
        ],
        out_specs=pl.BlockSpec((rows, 3 * wide), lambda h, i: (0, 0)),
        out_shape=jax.ShapeDtypeStruct((rows, 3 * wide), LOWER),
        scratch_shapes=[pltpu.VMEM((rows, HEAD), WIDE), pltpu.VMEM((rows, HEAD), WIDE)],
        cost_estimate=LIGHT,
        compiler_params=KERNEL,
    )(limits, qkv, qkv, qkv, grad, log_sum)


def local(
    tokens,
    lengths,
    dealing,
    w_query,
    w_key,
    w_value,
    w_out,
    b_query,
    b_value,
    b_out,
    gain_mid,
    shift_mid,
    w_up,
    b_up,
    w_down,
    b_down,
    gain_end,
    shift_end,
    cotangent,
):
    team = Team()
    ts, members = team.sizes["tp"], team.members
    row_count = tokens.shape[0] // ts
    wide = w_query.shape[1] // members
    tall = w_up.shape[1] // members
    width = tokens.shape[1]
    score_scale = 1.0 / math.sqrt(HEAD)
    my_slot = team.at["l"] * team.sizes["x"] + team.at["x"]
    seq_ids = jnp.arange(dealing.shape[0], dtype=jnp.int32)
    home = jnp.sum(jnp.where(dealing[None, :] == seq_ids[:, None], seq_ids[None, :], 0), axis=1)
    live_count = pick(lengths, team.at["h"] * 2 + team.at["y"])
    limits = live_count - jnp.stack(row_blocks(team)).astype(jnp.int32) * row_count
    query_live = (jnp.arange(row_count, dtype=jnp.int32) < limits[0])[:, None]
    half_at = team.at["tp"] * row_count

    half_rows = members * row_count
    vectors = jnp.stack([b_out, gain_mid, shift_mid, b_down, gain_end, shift_end])
    b_out, gain_mid, shift_mid, b_down, gain_end, shift_end = to_team_order(team, vectors)
    bias_q = lax.dynamic_slice_in_dim(b_query, my_slot * wide, wide, 0)
    bias_v = lax.dynamic_slice_in_dim(b_value, my_slot * wide, wide, 0)
    bias_up = lax.dynamic_slice_in_dim(b_up, my_slot * tall, tall, 0)
    bias_qkv = jnp.concatenate([bias_q, jnp.zeros_like(bias_q), bias_v])
    steps = team.sizes["h"] - 1

    with jax.named_scope("a0"):
        own = swap_home(lax.dynamic_slice_in_dim(tokens, half_at, row_count, 0))
        share = share_columns(team, [w_query, w_key, w_value, w_out])
        own, w_up, w_down, *share = fence(own, w_up, w_down, *share)
    with jax.named_scope("a1"):
        own = to_team_order(team, own)
        near_qkv = near_rows(team, share, 0, 3 * wide)
        near_out = near_rows(team, share, 3 * wide, wide)
        pieces = team_pieces(team, own)
        cross_qkv = across(team, near_qkv)
        side_qkv, side_out = beside(team, [near_qkv, near_out])
        near_out, w_up, w_down, side_qkv, side_out, *rest = fence(
            near_out, w_up, w_down, side_qkv, side_out, *pieces, *cross_qkv
        )
        pieces, cross_qkv = rest[:members], rest[members:]
    with jax.named_scope("a2"):
        half = jnp.concatenate(pieces, axis=0)
        other = cores(team, half)
        far_qkv = beside(team, cross_qkv)
        cross_out = across(team, near_out)
        share = share_columns(team, [w_up, w_down])
        rest = fence(half, *other, *share, *far_qkv, *cross_out)
        inputs = jnp.concatenate(rest[:ts], axis=0)
        share, rest = rest[ts : ts + members], rest[ts + members :]
        far_qkv, cross_out = rest[:steps], rest[steps:]
    with jax.named_scope("c1"):
        near_up = near_rows(team, share, 0, tall)
        near_down = near_rows(team, share, tall, tall)
        up_a, up_b = halves(near_up)
        cross_up_a = across(team, up_a)
        far_out = beside(team, cross_out)
        (side_up,) = beside(team, [near_up])
        qkv_mat = jnp.concatenate([near_qkv, *cross_qkv, side_qkv, *far_qkv], axis=0)
        qkv = (mm(inputs, qkv_mat) + bias_qkv).astype(LOWER)
        attended, log_sum = attend(qkv, limits, score_scale)
        out_mat = jnp.concatenate([near_out, *cross_out, side_out, *far_out], axis=0)

        def out_product(first, count):
            return mm_nt(attended[first : first + count], out_mat)

        got = core_send(team, out_product, half_rows)
        total, sent = core_total(team, out_product, half_rows, got)
        up_b, near_down, side_up, *rest = fence(up_b, near_down, side_up, *cross_up_a, *sent)
        cross_up_a, sent = rest[:steps], rest[steps:]
    with jax.named_scope("s3"):
        got = team_send(team, sent)
        cross_up_b = across(team, up_b)
        far_up_a = beside(team, cross_up_a)
        near_down, *rest = fence(near_down, *got, *cross_up_b, *far_up_a)
        got, rest = rest[: members - 1], rest[members - 1 :]
        cross_up_b, far_up_a = rest[:steps], rest[steps:]
    with jax.named_scope("s4"):
        branch = team_total(total, got) + b_out
        middle, mid_hat, mid_rate = layer_norm(own.astype(WIDE) + branch, gain_mid, shift_mid)
        pieces = team_pieces(team, middle.astype(LOWER))
        down_a, down_b = halves(near_down)
        cross_down_a = across(team, down_a)
        far_up_b = beside(team, cross_up_b)
        near_down, down_b, *rest = fence(near_down, down_b, *pieces, *cross_down_a, *far_up_b)
        pieces, rest = rest[:members], rest[members:]
        cross_down_a, far_up_b = rest[:steps], rest[steps:]
    with jax.named_scope("c2"):
        half = jnp.concatenate(pieces, axis=0)
        other = cores(team, half)
        cross_down_b = across(team, down_b)
        (side_down,) = beside(team, [near_down])
        far_down_a = beside(team, cross_down_a)
        middle_all = jnp.concatenate([half] + other, axis=0)
        up_mat = jnp.concatenate(
            [near_up]
            + pairs(cross_up_a, cross_up_b)
            + [side_up]
            + pairs(far_up_a, far_up_b),
            axis=0,
        )
        hidden = mm(middle_all, up_mat) + bias_up
        active = gelu_tanh(hidden).astype(LOWER)
        active, hidden, side_down, cotangent, *rest = fence(
            active, hidden, side_down, cotangent, *cross_down_b, *far_down_a
        )
        cross_down_b, far_down_a = rest[:steps], rest[steps:]
    with jax.named_scope("s5"):
        cot_pieces = spread_h(team, lax.dynamic_slice_in_dim(cotangent, half_at, row_count, 0))
        far_down_b = beside(team, cross_down_b)
        down_mat = jnp.concatenate(
            [near_down]
            + pairs(cross_down_a, cross_down_b)
            + [side_down]
            + pairs(far_down_a, far_down_b),
            axis=0,
        )

        def down_product(first, count):
            return mm_nt(active[first : first + count], down_mat)

        got = core_send(team, down_product, half_rows)
        total, sent = core_total(team, down_product, half_rows, got)
        rest = fence(*sent, *cot_pieces)
        sent, cot_pieces = rest[: members - 1], rest[members - 1 :]
    with jax.named_scope("s6"):
        got = team_send(team, sent)
        cot_two = deal(team, home, cot_pieces, True)
        rest = fence(*got, *cot_two)
        got, cot_two = rest[: members - 1], rest[members - 1 :]
    with jax.named_scope("s7"):
        result = team_total(total, got) + b_down
        normed, end_hat, end_rate = layer_norm(middle + result, gain_end, shift_end)
        output_own = jnp.where(query_live, normed, 0.0).astype(LOWER)
        cot = to_team_order(team, pick_dealt(team, home, cot_two, True)).astype(WIDE)
        grad_normed = jnp.where(query_live, cot, 0.0)
        grad_sum = layer_norm_back(grad_normed, gain_end, end_hat, end_rate)
        grad_result = grad_sum.astype(LOWER)
        pieces = team_pieces(team, grad_result)
        out_pieces = spread_h(team, from_team_order(team, output_own))
        rest = fence(*pieces, *out_pieces)
        pieces, out_pieces = rest[:members], rest[members:]
        grad_gend = jnp.sum(grad_normed * end_hat, axis=0)
        grad_send = jnp.sum(grad_normed, axis=0)
        grad_bdown = jnp.sum(grad_result.astype(WIDE), axis=0)
    with jax.named_scope("c3"):
        half = jnp.concatenate(pieces, axis=0)
        other = cores(team, half)
        result_all = jnp.concatenate([half] + other, axis=0)
        flow_down = Grads(
            team, lambda f, n: mm_tn(result_all[:, f : f + n], active), width, "down"
        )
        (far_down,) = beside(team, [flow_down.send_far()])
        grad_active = mm(result_all, down_mat)
        gelu_back = jax.vjp(gelu_tanh, hidden)[1]
        grad_hidden = gelu_back(grad_active)[0].astype(LOWER)

        def up_product(first, count):
            return mm_nt(grad_hidden[first : first + count], up_mat)

        got = core_send(team, up_product, half_rows)
        total, sent = core_total(team, up_product, half_rows, got)
        cross_down = flow_down.cross(far_down)
        flow_up = Grads(
            team, lambda f, n: mm_tn(middle_all[:, f : f + n], grad_hidden), width, "up"
        )
        rest = fence(*sent, *cross_down)
        sent, cross_down = rest[: members - 1], rest[members - 1 :]
    with jax.named_scope("s8"):
        got = team_send(team, sent)
        down_halves = [halves(value) for value in cross_down]
        got_down_a = flow_down.go([a for a, b in down_halves])
        (far_up,) = beside(team, [flow_up.send_far()])
        far_up, *rest = fence(far_up, *got, *got_down_a, *[b for a, b in down_halves])
        got, rest = rest[: members - 1], rest[members - 1 :]
        got_down_a, down_b = rest[:steps], rest[steps:]
    with jax.named_scope("s9"):
        grad_middle = team_total(total, got) + grad_sum
        grad_inner = layer_norm_back(grad_middle, gain_mid, mid_hat, mid_rate)
        grad_branch = grad_inner.astype(LOWER)
        pieces = team_pieces(team, grad_branch)
        got_down_b = flow_down.go(down_b)
        (near_down,) = beside(team, [flow_down.send_near()])
        cross_up = flow_up.cross(far_up)
        near_down, *rest = fence(near_down, *pieces, *got_down_b, *cross_up)
        pieces, rest = rest[:members], rest[members:]
        got_down_b, cross_up = rest[:steps], rest[steps:]
        grad_gmid = jnp.sum(grad_middle * mid_hat, axis=0)
        grad_smid = jnp.sum(grad_middle, axis=0)
        grad_bout = jnp.sum(grad_branch.astype(WIDE), axis=0)
    with jax.named_scope("c4"):
        half = jnp.concatenate(pieces, axis=0)
        other = cores(team, half)
        up_halves = [halves(value) for value in cross_up]
        got_up_a = flow_up.go([a for a, b in up_halves])
        (near_up,) = beside(team, [flow_up.send_near()])
        branch_all = jnp.concatenate([half] + other, axis=0)
        flow_out = Grads(
            team, lambda f, n: mm_tn(branch_all[:, f : f + n], attended), width, "out"
        )
        (far_out,) = beside(team, [flow_out.send_far()])
        grad_attended = mm(branch_all, out_mat).astype(LOWER)
        grad_qkv = attend_back(qkv, grad_attended, log_sum, limits, score_scale)

        def in_product(first, count):
            return mm_nt(grad_qkv[first : first + count], qkv_mat)

        got = core_send(team, in_product, half_rows)
        total, sent = core_total(team, in_product, half_rows, got)
        flow_qkv = Grads(
            team, lambda f, n: mm_tn(inputs[:, f : f + n], grad_qkv), width, "qkv"
        )
        cross_out = flow_out.cross(far_out)
        near_up, *rest = fence(
            near_up, *sent, *got_up_a, *[b for a, b in up_halves], *cross_out
        )
        sent, rest = rest[: members - 1], rest[members - 1 :]
        got_up_a, up_b, cross_out = rest[:steps], rest[steps : 2 * steps], rest[2 * steps :]
        total_down = flow_down.total(
            near_down,
            [jnp.concatenate(both, axis=0) for both in zip(got_down_a, got_down_b)],
        )

    qkv_sum = jnp.sum(grad_qkv.astype(WIDE), axis=0)
    grad_bup = jnp.sum(grad_hidden.astype(WIDE), axis=0)
    zeros = jnp.zeros((members, 1), WIDE)
    by_slot = [
        put(zeros * part[None], part[None], (my_slot, 0)).reshape(-1)
        for part in (qkv_sum[:wide], qkv_sum[2 * wide :], grad_bup)
    ]
    by_row = jnp.stack([grad_bout, grad_gmid, grad_smid, grad_bdown, grad_gend, grad_send])
    by_row = from_team_order(team, by_row).reshape(-1)
    sums = jnp.concatenate([by_row] + by_slot).reshape(-1, 128)
    by_row_rows = by_row.shape[0] // 128

    def add_ring(value, name):
        return value + sum(team.ring(value, name, step) for step in range(1, team.sizes[name]))

    with jax.named_scope("s10"):
        got = team_send(team, sent)
        got_up_b = flow_up.go(up_b)
        (far_qkv,) = beside(team, [flow_qkv.send_far()])
        cross_qkv = flow_qkv.cross(far_qkv)
        both = add_ring(sums[:by_row_rows], "tp")
        sums = jnp.concatenate([both, sums[by_row_rows:]], axis=0)
        sums, total_down, near_up, *rest = fence(
            sums, total_down, near_up, *got, *got_up_b, *cross_qkv, *cross_out
        )
        got, rest = rest[: members - 1], rest[members - 1 :]
        got_up_b, cross_qkv, cross_out = rest[:steps], rest[steps : 2 * steps], rest[2 * steps :]
    with jax.named_scope("s11"):
        got_qkv = flow_qkv.go(cross_qkv)
        got_out = flow_out.go(cross_out)
        grad_own = (team_total(total, got) + grad_inner).astype(LOWER)
        swapped = swap_home(from_team_order(team, grad_own))
        sums = add_ring(sums, "y")
        near_qkv, near_out = beside(team, [flow_qkv.send_near(), flow_out.send_near()])
        home_down = home_pieces(team, total_down)
        total_up = flow_up.total(
            near_up, [jnp.concatenate(both, axis=0) for both in zip(got_up_a, got_up_b)]
        )
        rest = fence(sums, swapped, near_qkv, near_out, total_up, *home_down)
        sums, swapped, near_qkv, near_out, total_up = rest[:5]
        home_down = rest[5:]
        (grad_down,) = home_join(team, home_down, [tall])
    with jax.named_scope("s12"):
        home_up = home_pieces(team, total_up)
        out_two = deal(team, dealing, out_pieces, False)
        grad_tokens = join_cores(team, swapped)
        sums = add_ring(sums, "h")
        total_qkv = flow_qkv.total(near_qkv, got_qkv)
        total_out = flow_out.total(near_out, got_out)
        rest = fence(sums, grad_tokens, total_qkv, total_out, *home_up, *out_two)
        sums, grad_tokens, total_qkv, total_out = rest[:4]
        home_up, out_two = rest[4 : 4 + members], rest[4 + members :]
        (grad_up,) = home_join(team, home_up, [tall])
    with jax.named_scope("s13"):
        home_att = home_pieces(team, jnp.concatenate([total_qkv, total_out], axis=1))
        output = join_cores(team, pick_dealt(team, dealing, out_two, False))
        sums = add_ring(add_ring(sums, "l"), "x").reshape(-1)
        grad_query, grad_key, grad_value, grad_out = home_join(team, home_att, [wide] * 4)
    smalls = []
    first = 0
    for size in [width] * 6 + [b_query.shape[0], b_value.shape[0], b_up.shape[0]]:
        smalls.append(sums[first : first + size])
        first += size
    return (
        output,
        grad_tokens,
        grad_query,
        grad_key,
        grad_value,
        grad_out,
        smalls[6],
        smalls[7],
        smalls[0],
        smalls[1],
        smalls[2],
        grad_up,
        smalls[8],
        grad_down,
        smalls[3],
        smalls[4],
        smalls[5],
    )


def solution(mesh):
    fsdp, ctx, tp = (mesh.shape[name] for name in ("fsdp", "ctx", "tp"))
    fine = Mesh(mesh.devices.reshape(fsdp // 2, 2, 2, ctx // 2, tp), ROWS + ("tp",))
    rows, split = P(ROWS, None), P(ROWS, "tp")
    in_specs = (
        (rows, P(), P())
        + (split,) * 4
        + (P("tp"), P("tp"), P(), P(), P(), split, P("tp"), split, P(), P(), P(), rows)
    )
    out_specs = (
        (rows, rows)
        + (split,) * 4
        + (P("tp"), P("tp"), P(), P(), P(), split, P("tp"), split, P(), P(), P())
    )
    return jax.shard_map(local, mesh=fine, in_specs=in_specs, out_specs=out_specs, check_vma=False)
```

```python
import functools
import math

import jax
import jax.numpy as jnp
from jax import lax
from jax.experimental import pallas as pl
from jax.experimental.pallas import tpu as pltpu
from jax.sharding import Mesh
from jax.sharding import PartitionSpec as P

HEAD = 128
EPSILON = 1e-12
NEGATIVE = -1e30
WIDE = jnp.float32
LOWER = jnp.bfloat16

TEAM = ("l", "x")
ROWS = ("h", "l", "y", "x")


def dot(left, right, dims):
    return lax.dot_general(left, right, (dims, ((), ())), preferred_element_type=WIDE)


def mm(left, right):
    return dot(left, right, ((1,), (0,)))


def mm_nt(left, right):
    return dot(left, right, ((1,), (1,)))


def mm_tn(left, right):
    return dot(left, right, ((0,), (0,)))


class Team:
    def __init__(self):
        self.sizes = {name: lax.axis_size(name) for name in ROWS + ("tp",)}
        self.at = {name: lax.axis_index(name) for name in ROWS + ("tp",)}
        ls, xs = self.sizes["l"], self.sizes["x"]
        self.offsets = [(dl, dx) for dl in range(ls) for dx in range(xs)]
        self.members = ls * xs

    def shift(self, value, offset, back=False):
        with jax.named_scope("team%d%d" % offset):
            return self.shift_(value, offset, back)

    def shift_(self, value, offset, back):
        ls, xs = self.sizes["l"], self.sizes["x"]
        dl, dx = offset
        if back:
            dl, dx = -dl, -dx
        perm = [
            (l * xs + x, ((l + dl) % ls) * xs + (x + dx) % xs) for l in range(ls) for x in range(xs)
        ]
        return lax.ppermute(value, TEAM, perm)

    def ring(self, value, name, step):
        size = self.sizes[name]
        with jax.named_scope("ring_" + name):
            return lax.ppermute(value, name, [(i, (i + step) % size) for i in range(size)])

    def slot(self, offset, back=True):
        ls, xs = self.sizes["l"], self.sizes["x"]
        dl, dx = offset
        if back:
            dl, dx = -dl, -dx
        return lax.rem(self.at["l"] + dl + ls, ls) * xs + lax.rem(self.at["x"] + dx + xs, xs)


def fence(*values):
    return lax.optimization_barrier(values)


def swap_home(value):
    perm = [(l * 2 + y, y * 2 + l) for l in range(2) for y in range(2)]
    return lax.ppermute(value, ("l", "y"), perm)


def team_pieces(team, piece):
    far = team.shift(piece, (1, 0))
    across_x = [(0, dx) for dx in range(1, team.sizes["x"])]
    return (
        [piece]
        + [team.shift(piece, offset) for offset in across_x]
        + [far]
        + [team.shift(far, offset) for offset in across_x]
    )


def cores(team, value):
    return [team.ring(value, "tp", step) for step in range(1, team.sizes["tp"])]


def row_blocks(team):
    ts = team.sizes["tp"]
    return [
        team.slot(offset) * ts + lax.rem(team.at["tp"] - step + ts, ts)
        for step in range(ts)
        for offset in team.offsets
    ]


def core_send(team, rows, pieces, half_rows, *others):
    sent = [spread(rows, step, pieces, half_rows) for step in range(1, team.sizes["tp"])]
    sent = fence(*sent, *others)[: len(sent)]
    return [team.ring(value, "tp", -step) for step, value in enumerate(sent, 1)]


def core_total(team, rows, pieces, half_rows, got):
    total, *sent = spread(rows, 0, pieces, half_rows, got, team.members)
    return total, sent


def team_send(team, sent):
    xs = team.sizes["x"]
    across_x = [(0, dx) for dx in range(1, xs)]
    far = sent[xs - 1].astype(WIDE)
    for value, offset in zip(sent[xs:], across_x):
        far = far + team.shift(value, offset, back=True).astype(WIDE)
    got = [team.shift(value, offset, back=True) for value, offset in zip(sent, across_x)]
    return got + [team.shift(far.astype(LOWER), (1, 0), back=True)]


def team_total(own, got):
    for value in got:
        own = own + value.astype(WIDE)
    return own


def put(buffer, value, starts):
    return lax.dynamic_update_slice(buffer, value, starts)


def share_columns(team, shards):
    widths = [shard.shape[1] // team.members for shard in shards]
    pieces = []
    for j, offset in enumerate(team.offsets):
        slot = team.slot(offset, back=False)
        cuts = [
            lax.dynamic_slice_in_dim(shard, slot * each, each, 1)
            for shard, each in zip(shards, widths)
        ]
        piece = jnp.concatenate(cuts, axis=1)
        pieces.append(team.shift(piece, offset) if j > 0 else piece)
    return pieces


def place_rows_kernel(widths, slots_ref, *refs):
    pieces, outs = refs[: len(refs) - len(widths)], refs[len(refs) - len(widths) :]
    for j, piece in enumerate(pieces):
        height = piece.shape[0]
        row = pl.multiple_of(slots_ref[j] * height, height)
        first = 0
        for out, width in zip(outs, widths):
            out[pl.ds(row, height), :] = piece[:, first : first + width]
            first += width


def place_columns_kernel(widths, slots_ref, *refs):
    pieces, outs = refs[: len(refs) - len(widths)], refs[len(refs) - len(widths) :]
    for j, piece in enumerate(pieces):
        first = 0
        for out, width in zip(outs, widths):
            column = pl.multiple_of(slots_ref[j] * width, width)
            block = piece[:, first : first + width].astype(out.dtype)
            out[:, pl.ds(column, width)] = block
            first += width


def place(team, kernel, pieces, widths, shapes):
    slots = jnp.stack([team.slot(offset) for offset in team.offsets]).astype(jnp.int32)
    whole = [pl.BlockSpec(piece.shape, lambda n: (0, 0)) for piece in pieces]
    return pl.pallas_call(
        functools.partial(kernel, widths),
        grid=(1,),
        in_specs=[pl.BlockSpec(memory_space=pltpu.SMEM)] + whole,
        out_specs=[pl.BlockSpec(shape.shape, lambda n: (0, 0)) for shape in shapes],
        out_shape=shapes,
        cost_estimate=LIGHT,
        compiler_params=KERNEL,
    )(slots, *pieces)


def near_rows(team, pieces, widths):
    rows = pieces[0].shape[0] * team.members
    shapes = [jax.ShapeDtypeStruct((rows, width), LOWER) for width in widths]
    return place(team, place_rows_kernel, pieces, widths, shapes)


def across(team, value):
    return [team.ring(value, "h", -step) for step in range(1, team.sizes["h"])]


def beside(team, values):
    return [team.ring(value, "y", 1) for value in values]


def halves(value):
    middle = value.shape[0] // 2
    return value[:middle], value[middle:]


def pairs(firsts, seconds):
    return [part for pair in zip(firsts, seconds) for part in pair]


class Grads:
    def __init__(self, team, lefts, rights):
        self.team, self.lefts, self.rights = team, lefts, rights
        self.far = lefts[0].shape[1] // 2
        self.near = self.far // team.sizes["h"]

    def rows(self, first, count, adds=(), dtype=LOWER):
        return outer(self.lefts, self.rights, first, count, adds, dtype)

    def send_far(self):
        return self.rows(self.far + self.near, self.far - self.near)

    def send_near(self):
        return self.rows(self.far, self.near)

    def cross(self, got):
        mine = self.rows(self.near, self.far - self.near, [got])
        return [
            mine[step * self.near : (step + 1) * self.near]
            for step in range(self.team.sizes["h"] - 1)
        ]

    def go(self, sent):
        return [self.team.ring(value, "h", step) for step, value in enumerate(sent, 1)]

    def total(self, got, crossed):
        return self.rows(0, self.near, [got, *crossed])


def home_pieces(team, total):
    height = total.shape[0] // team.members
    total = total.reshape(team.members, height, -1)
    pieces = []
    for j, offset in enumerate(team.offsets):
        piece = lax.dynamic_index_in_dim(total, team.slot(offset, back=False), 0, False)
        pieces.append(team.shift(piece, offset) if j > 0 else piece)
    return pieces


def home_join(team, pieces, widths):
    height = pieces[0].shape[0]
    shapes = [jax.ShapeDtypeStruct((height, width * team.members), WIDE) for width in widths]
    return place(team, place_columns_kernel, pieces, widths, shapes)


def permute_kernel(count, table_ref, value_ref, out_ref):
    block = value_ref.shape[1] // count
    for i in range(count):
        column = pl.multiple_of(table_ref[i] * block, block)
        out_ref[:, i * block : (i + 1) * block] = value_ref[:, pl.ds(column, block)]


def permute_columns(value, table):
    whole = pl.BlockSpec(value.shape, lambda n: (0, 0))
    return pl.pallas_call(
        functools.partial(permute_kernel, len(table)),
        grid=(1,),
        in_specs=[pl.BlockSpec(memory_space=pltpu.SMEM), whole],
        out_specs=whole,
        out_shape=jax.ShapeDtypeStruct(value.shape, value.dtype),
        cost_estimate=LIGHT,
    )(jnp.stack(table).astype(jnp.int32), value)


def to_team_order(team, value):
    hs = team.sizes["h"]
    table = []
    for dy in range(2):
        for dh in range(hs):
            for l in range(2):
                h, y = lax.rem(team.at["h"] + dh, hs), lax.rem(team.at["y"] + dy, 2)
                table.append((h * 2 + l) * 2 + y)
    return permute_columns(value, table)


def from_team_order(team, value):
    hs = team.sizes["h"]
    table = []
    for h in range(hs):
        for l in range(2):
            for y in range(2):
                dh, dy = lax.rem(h - team.at["h"] + hs, hs), lax.rem(y - team.at["y"] + 2, 2)
                table.append((dy * hs + dh) * 2 + l)
    return permute_columns(value, table)


def pick(table, index):
    ids = jnp.arange(table.shape[0], dtype=jnp.int32)
    return jnp.sum(jnp.where(ids == index, table, 0))


def choose(pieces, index):
    out = pieces[0]
    for i in range(1, len(pieces)):
        out = jnp.where(index == i, pieces[i], out)
    return out


def spread_h(team, piece):
    return [piece] + [team.ring(piece, "h", step) for step in range(1, team.sizes["h"])]


def deal_flips(team, piece):
    got = []
    for flip in range(2):
        perm = []
        for l in range(2):
            for y in range(2):
                perm.append((l * 2 + y, y * 2 + (l if flip == 0 else 1 - l)))
        with jax.named_scope("flip"):
            got.append(lax.ppermute(piece, ("l", "y"), perm))
    return got


def deal_across(team, home, two):
    hs = team.sizes["h"]

    def needed(h):
        group = pick(home, h * 2 + team.at["y"])
        return jnp.where(lax.rem(group, 2) == team.at["y"], two[0], two[1])

    return [needed(team.at["h"])] + [
        team.ring(needed(lax.rem(team.at["h"] + step, hs)), "h", step) for step in range(1, hs)
    ]


def dealt_in(team, home, pieces):
    hs = team.sizes["h"]
    group = pick(home, team.at["h"] * 2 + team.at["y"])
    return choose(pieces, lax.rem(team.at["h"] - group // 2 + hs, hs))


def deal(team, dealing, pieces):
    hs = team.sizes["h"]
    got = []
    for flip in range(2):
        target = team.at["y"] if flip == 0 else 1 - team.at["y"]
        seq = pick(dealing, team.at["h"] * 2 + target)
        sent = choose(pieces, lax.rem(team.at["h"] - seq // 2 + hs, hs))
        perm = []
        for l in range(2):
            for y in range(2):
                perm.append((l * 2 + y, (y if flip == 0 else 1 - y) * 2 + l))
        with jax.named_scope("flip"):
            got.append(lax.ppermute(sent, ("l", "y"), perm))
    return got


def dealt_out(team, dealing, got):
    seq = pick(dealing, team.at["h"] * 2 + team.at["l"])
    return jnp.where(lax.rem(seq, 2) == team.at["l"], got[0], got[1])


def join_cores(team, piece):
    ts = team.sizes["tp"]
    out = jnp.zeros((ts,) + piece.shape, piece.dtype)
    for step in range(ts):
        other = team.ring(piece, "tp", step) if step else piece
        out = put(out, other[None], (lax.rem(team.at["tp"] - step + ts, ts), 0, 0))
    return out.reshape(-1, piece.shape[-1])


def layer_norm(inputs, gain_vec, shift_vec):
    row_mean = jnp.mean(inputs, axis=-1, keepdims=True)
    centred = inputs - row_mean
    spread = jnp.mean(centred * centred, axis=-1, keepdims=True)
    rate = lax.rsqrt(spread + EPSILON)
    xhat = centred * rate
    return xhat * gain_vec + shift_vec, xhat, rate


def layer_norm_back(grad, gain_vec, xhat, rate):
    scaled = grad * gain_vec
    return rate * (
        scaled
        - jnp.mean(scaled, axis=-1, keepdims=True)
        - xhat * jnp.mean(scaled * xhat, axis=-1, keepdims=True)
    )


def gelu_tanh(inputs):
    return jax.nn.gelu(inputs, approximate=True)


def masked_scores(key_ref, query, limits_ref, scale):
    count = limits_ref.shape[0]
    height = key_ref.shape[0] // count
    blocks = []
    for j in range(count):
        block = mm_nt(key_ref[j * height : (j + 1) * height, :], query) * scale
        row = lax.broadcasted_iota(jnp.int32, block.shape, 0)
        blocks.append(jnp.where(row < limits_ref[j], block, NEGATIVE))
    return blocks


def attend_kernel(scale, limits_ref, query_ref, key_ref, value_ref, out_ref, log_ref):
    blocks = masked_scores(key_ref, query_ref[...], limits_ref, scale)
    row_max = functools.reduce(jnp.maximum, blocks)
    row_max = jnp.max(row_max, axis=0, keepdims=True)
    blocks = [jnp.exp(block - row_max) for block in blocks]
    total = jnp.sum(functools.reduce(jnp.add, blocks), axis=0, keepdims=True)
    inverse = 1.0 / total
    height = key_ref.shape[0] // len(blocks)
    out = None
    for j, block in enumerate(blocks):
        value = value_ref[j * height : (j + 1) * height, :]
        term = mm_tn(value, (block * inverse).astype(LOWER))
        out = term if out is None else out + term
    out_ref[...] = out.T.astype(LOWER)
    log_ref[0] = row_max + jnp.log(total)


def attend_back_kernel(
    scale, wide, limits_ref, query_ref, key_ref, value_ref, grad_ref, log_ref, out_ref, key_sum, value_sum
):
    head, step = pl.program_id(0), pl.program_id(1)
    query, grad = query_ref[...], grad_ref[...]
    blocks = masked_scores(key_ref, query, limits_ref, scale)
    count = len(blocks)
    height = key_ref.shape[0] // count
    part = [slice(j * height, (j + 1) * height) for j in range(count)]
    log_sum = log_ref[0]
    probs = [jnp.exp(block - log_sum) for block in blocks]
    grad_probs = [mm_nt(value_ref[rows, :], grad) for rows in part]
    delta = functools.reduce(jnp.add, [p * g for p, g in zip(probs, grad_probs)])
    delta = jnp.sum(delta, axis=0, keepdims=True)

    @pl.when(step == 0)
    def _():
        key_sum[...] = jnp.zeros_like(key_sum)
        value_sum[...] = jnp.zeros_like(value_sum)

    grad_query = None
    for j, rows in enumerate(part):
        scores = (probs[j] * (grad_probs[j] - delta)).astype(LOWER)
        term = mm_tn(key_ref[rows, :], scores)
        grad_query = term if grad_query is None else grad_query + term
        key_sum[rows, :] += mm(scores, query)
        value_sum[rows, :] += mm(probs[j].astype(LOWER), grad)
    count = query.shape[0]
    first = pl.multiple_of(step * count, count)
    column = pl.multiple_of(head * HEAD, HEAD)
    out_ref[pl.ds(first, count), pl.ds(column, HEAD)] = (grad_query.T * scale).astype(LOWER)

    @pl.when(step == pl.num_programs(1) - 1)
    def _():
        out_ref[:, pl.ds(wide + column, HEAD)] = (key_sum[...] * scale).astype(LOWER)
        out_ref[:, pl.ds(2 * wide + column, HEAD)] = value_sum[...].astype(LOWER)


LIGHT = pl.CostEstimate(flops=1000000, bytes_accessed=100000, transcendentals=0)
KERNEL = pltpu.CompilerParams(vmem_limit_bytes=32 * 1024 * 1024)


def gelu_slope(value):
    inner = math.sqrt(2.0 / math.pi)
    square = value * value
    tanh = jnp.tanh(inner * value * (1.0 + 0.044715 * square))
    return 0.5 * (1.0 + tanh) + 0.5 * value * (1.0 - tanh * tanh) * inner * (
        1.0 + 3.0 * 0.044715 * square
    )


def project_kernel(mode, part_count, piece_count, steps, *refs):
    parts, pieces = refs[:part_count], refs[part_count : part_count + piece_count]
    rest = refs[part_count + piece_count :]
    index = pl.program_id(0)

    def run(rows):
        total = None
        first = 0
        for piece in pieces:
            depth = piece.shape[0]
            term = mm(rows[:, first : first + depth], piece[...])
            total = term if total is None else total + term
            first += depth
        if mode == "bias":
            rest[1][...] = (total + rest[0][...]).astype(LOWER)
        elif mode == "gelu":
            total = total + rest[0][...]
            rest[1][...] = total
            rest[2][...] = gelu_tanh(total).astype(LOWER)
        elif mode == "slope":
            rest[1][...] = (total * gelu_slope(rest[0][...])).astype(LOWER)
        else:
            rest[0][...] = total.astype(LOWER)

    for place in range(part_count):

        @pl.when(index // steps == place)
        def _():
            run(parts[place][...])


def project(mode, parts, pieces, width, extra=None):
    half_rows, depth = parts[0].shape
    block = min(256, half_rows)
    steps = half_rows // block
    rows = half_rows * len(parts)

    def part_at(place):
        return lambda i: (jnp.clip(i - place * steps, 0, steps - 1), 0)

    in_specs = [pl.BlockSpec((block, depth), part_at(place)) for place in range(len(parts))]
    for array, column in pieces:
        in_specs.append(
            pl.BlockSpec((array.shape[0], width), functools.partial(lambda c, i: (0, c), column))
        )
    arrays = list(parts) + [array for array, _ in pieces]
    tile = pl.BlockSpec((block, width), lambda i: (i, 0))
    if mode in ("bias", "gelu"):
        in_specs.append(pl.BlockSpec((1, width), lambda i: (0, 0)))
        arrays.append(extra[None])
    elif mode == "slope":
        in_specs.append(tile)
        arrays.append(extra)
    shapes = [jax.ShapeDtypeStruct((rows, width), LOWER)]
    if mode == "gelu":
        shapes = [jax.ShapeDtypeStruct((rows, width), WIDE)] + shapes
    return pl.pallas_call(
        functools.partial(project_kernel, mode, len(parts), len(pieces), steps),
        grid=(len(parts) * steps,),
        in_specs=in_specs,
        out_specs=[tile] * len(shapes),
        out_shape=shapes,
        cost_estimate=LIGHT,
        compiler_params=KERNEL,
    )(*arrays)


def spread_kernel(piece_count, got_count, members, rows_ref, *refs):
    pieces, gots = refs[:piece_count], refs[piece_count : piece_count + got_count]
    outs = refs[piece_count + got_count :]
    rows = rows_ref[...]
    height = rows.shape[0] // members
    first = 0
    for piece in pieces:
        columns = slice(first, first + piece.shape[0])
        total = mm_nt(rows, piece[...])
        for got in gots:
            total = total + got[:, columns].astype(WIDE)
        for j, out in enumerate(outs):
            out[:, columns] = total[j * height : (j + 1) * height].astype(out.dtype)
        first += piece.shape[0]


def spread(rows, place, pieces, half_rows, got=(), members=0):
    if isinstance(rows, (list, tuple)):
        rows, place = rows[place], 0
    depth = rows.shape[1]
    width = sum(array.shape[0] for array, _ in pieces)
    in_specs = [pl.BlockSpec((half_rows, depth), lambda n: (place, 0))]
    for array, column in pieces:
        in_specs.append(
            pl.BlockSpec((array.shape[0], depth), functools.partial(lambda c, n: (0, c), column))
        )
    in_specs += [pl.BlockSpec((half_rows, width), lambda n: (0, 0))] * len(got)
    split = max(members, 1)
    height = half_rows // split
    dtypes = [WIDE] + [LOWER] * (members - 1) if members else [LOWER]
    out = pl.pallas_call(
        functools.partial(spread_kernel, len(pieces), len(got), split),
        grid=(1,),
        in_specs=in_specs,
        out_specs=[pl.BlockSpec((height, width), lambda n: (0, 0))] * split,
        out_shape=[jax.ShapeDtypeStruct((height, width), dtype) for dtype in dtypes],
        cost_estimate=LIGHT,
        compiler_params=KERNEL,
    )(rows, *[array for array, _ in pieces], *got)
    return out if members else out[0]


def outer_kernel(part_count, add_count, *refs):
    lefts, rights = refs[:part_count], refs[part_count : 2 * part_count]
    adds, out = refs[2 * part_count : 2 * part_count + add_count], refs[-1]
    total = None
    for left, right in zip(lefts, rights):
        term = mm_tn(left[...], right[...])
        total = term if total is None else total + term
    for add in adds:
        total = total + add[...].astype(WIDE)
    out[...] = total.astype(out.dtype)


def outer(lefts, rights, first, count, adds=(), dtype=LOWER):
    height, width = rights[0].shape
    block = math.gcd(256, count)
    in_specs = [pl.BlockSpec((height, block), lambda i: (0, first // block + i)) for _ in lefts]
    in_specs += [pl.BlockSpec((height, width), lambda i: (0, 0)) for _ in rights]
    tile = pl.BlockSpec((block, width), lambda i: (i, 0))
    return pl.pallas_call(
        functools.partial(outer_kernel, len(lefts), len(adds)),
        grid=(count // block,),
        in_specs=in_specs + [tile] * len(adds),
        out_specs=tile,
        out_shape=jax.ShapeDtypeStruct((count, width), dtype),
        cost_estimate=LIGHT,
        compiler_params=KERNEL,
    )(*lefts, *rights, *adds)


def query_block(rows):
    return min(256, rows)


def attend(qkv, limits, scale):
    rows, wide = qkv.shape[0], qkv.shape[1] // 3
    heads, block = wide // HEAD, query_block(rows)
    return pl.pallas_call(
        functools.partial(attend_kernel, scale),
        grid=(heads, rows // block),
        in_specs=[
            pl.BlockSpec(memory_space=pltpu.SMEM),
            pl.BlockSpec((block, HEAD), lambda h, i: (i, h)),
            pl.BlockSpec((rows, HEAD), lambda h, i: (0, heads + h)),
            pl.BlockSpec((rows, HEAD), lambda h, i: (0, 2 * heads + h)),
        ],
        out_specs=[
            pl.BlockSpec((block, HEAD), lambda h, i: (i, h)),
            pl.BlockSpec((1, 1, block), lambda h, i: (h, 0, i)),
        ],
        out_shape=[
            jax.ShapeDtypeStruct((rows, wide), LOWER),
            jax.ShapeDtypeStruct((heads, 1, rows), WIDE),
        ],
        cost_estimate=LIGHT,
        compiler_params=KERNEL,
    )(limits, qkv, qkv, qkv)


def attend_back(qkv, grad, log_sum, limits, scale):
    rows, wide = grad.shape
    heads, block = wide // HEAD, query_block(rows)
    return pl.pallas_call(
        functools.partial(attend_back_kernel, scale, wide),
        grid=(heads, rows // block),
        in_specs=[
            pl.BlockSpec(memory_space=pltpu.SMEM),
            pl.BlockSpec((block, HEAD), lambda h, i: (i, h)),
            pl.BlockSpec((rows, HEAD), lambda h, i: (0, heads + h)),
            pl.BlockSpec((rows, HEAD), lambda h, i: (0, 2 * heads + h)),
            pl.BlockSpec((block, HEAD), lambda h, i: (i, h)),
            pl.BlockSpec((1, 1, block), lambda h, i: (h, 0, i)),
        ],
        out_specs=pl.BlockSpec((rows, 3 * wide), lambda h, i: (0, 0)),
        out_shape=jax.ShapeDtypeStruct((rows, 3 * wide), LOWER),
        scratch_shapes=[pltpu.VMEM((rows, HEAD), WIDE), pltpu.VMEM((rows, HEAD), WIDE)],
        cost_estimate=LIGHT,
        compiler_params=KERNEL,
    )(limits, qkv, qkv, qkv, grad, log_sum)


def local(
    tokens,
    lengths,
    dealing,
    w_query,
    w_key,
    w_value,
    w_out,
    b_query,
    b_value,
    b_out,
    gain_mid,
    shift_mid,
    w_up,
    b_up,
    w_down,
    b_down,
    gain_end,
    shift_end,
    cotangent,
):
    team = Team()
    ts, members = team.sizes["tp"], team.members
    row_count = tokens.shape[0] // ts
    wide = w_query.shape[1] // members
    tall = w_up.shape[1] // members
    width = tokens.shape[1]
    score_scale = 1.0 / math.sqrt(HEAD)
    my_slot = team.at["l"] * team.sizes["x"] + team.at["x"]
    seq_ids = jnp.arange(dealing.shape[0], dtype=jnp.int32)
    home = jnp.sum(jnp.where(dealing[None, :] == seq_ids[:, None], seq_ids[None, :], 0), axis=1)
    live_count = pick(lengths, team.at["h"] * 2 + team.at["y"])
    limits = live_count - jnp.stack(row_blocks(team)).astype(jnp.int32) * row_count
    query_live = (jnp.arange(row_count, dtype=jnp.int32) < limits[0])[:, None]
    half_at = team.at["tp"] * row_count

    half_rows = members * row_count
    vectors = jnp.stack([b_out, gain_mid, shift_mid, b_down, gain_end, shift_end])
    b_out, gain_mid, shift_mid, b_down, gain_end, shift_end = to_team_order(team, vectors)
    bias_q = lax.dynamic_slice_in_dim(b_query, my_slot * wide, wide, 0)
    bias_v = lax.dynamic_slice_in_dim(b_value, my_slot * wide, wide, 0)
    bias_up = lax.dynamic_slice_in_dim(b_up, my_slot * tall, tall, 0)
    bias_qkv = jnp.concatenate([bias_q, jnp.zeros_like(bias_q), bias_v])
    steps = team.sizes["h"] - 1
    team_count = team.sizes["x"]


    def first_column(arrays):
        return [(array, 0) for array in arrays]

    with jax.named_scope("a0"):
        own = swap_home(lax.dynamic_slice_in_dim(tokens, half_at, row_count, 0))
        share = share_columns(team, [w_query, w_key, w_value, w_out])
        own, w_up, w_down, *share = fence(own, w_up, w_down, *share)
    with jax.named_scope("a1"):
        own = to_team_order(team, own)
        (near_att,) = near_rows(team, share, [4 * wide])
        pieces = team_pieces(team, own)
        cross_qkv = across(team, near_att[:, : 3 * wide])
        (side_att,) = beside(team, [near_att])
        near_att, w_up, w_down, cotangent, side_att, *rest = fence(
            near_att, w_up, w_down, cotangent, side_att, *pieces, *cross_qkv
        )
        pieces, cross_qkv = rest[:members], rest[members:]
    with jax.named_scope("a2"):
        half = jnp.concatenate(pieces, axis=0)
        other = cores(team, half)
        far_qkv = beside(team, cross_qkv)
        cross_out = across(team, near_att[:, 3 * wide :])
        share = share_columns(team, [w_up, w_down])
        cotangent, *rest = fence(cotangent, half, *other, *share, *far_qkv, *cross_out)
        in_parts = rest[:ts]
        share, rest = rest[ts : ts + members], rest[ts + members :]
        far_qkv, cross_out = rest[:steps], rest[steps:]
    qkv_mat = first_column([near_att, *cross_qkv, side_att, *far_qkv])
    with jax.named_scope("c1"):
        near_up, near_down = near_rows(team, share, [tall, tall])
        up_a, up_b = halves(near_up)
        cross_up_a = across(team, up_a)
        far_out = beside(team, cross_out)
        cot_two = deal_flips(team, lax.dynamic_slice_in_dim(cotangent, half_at, row_count, 0))
        (qkv,) = project("bias", in_parts, qkv_mat, 3 * wide, bias_qkv)
        attended, log_sum = attend(qkv, limits, score_scale)
        out_mat = [(near_att, 3), *first_column(cross_out), (side_att, 3), *first_column(far_out)]
        got = core_send(team, attended, out_mat, half_rows, *cross_up_a, *cot_two)
        total, sent = core_total(team, attended, out_mat, half_rows, got)
        up_b, near_up, near_down, *rest = fence(
            up_b, near_up, near_down, *cross_up_a, *sent, *cot_two
        )
        cross_up_a, rest = rest[:steps], rest[steps:]
        sent, cot_two = rest[: members - 1], rest[members - 1 :]
    with jax.named_scope("s3"):
        got = team_send(team, sent)
        cross_up_b = across(team, up_b)
        side = beside(team, [jnp.concatenate([near_up, *cross_up_a], axis=0)])
        near_down, *rest = fence(near_down, *got, *cross_up_b, *side)
        got, rest = rest[:team_count], rest[team_count:]
        cross_up_b, side_a = rest[:steps], rest[steps]
    with jax.named_scope("s4"):
        branch = team_total(total, got) + b_out
        middle, mid_hat, mid_rate = layer_norm(own.astype(WIDE) + branch, gain_mid, shift_mid)
        pieces = team_pieces(team, middle.astype(LOWER))
        down_a, down_b = halves(near_down)
        cross_down_a = across(team, down_a)
        side = beside(team, [jnp.concatenate([near_down, *cross_up_b], axis=0)])
        near_down, down_b, *rest = fence(near_down, down_b, *pieces, *cross_down_a, *side)
        pieces, rest = rest[:members], rest[members:]
        cross_down_a, side_b = rest[:steps], rest[steps]
    near_count = near_down.shape[0]
    side_up, side_down = side_a[:near_count], side_b[:near_count]
    far_up_a, far_up_b = (
        [
            side[near_count + k * near_count // 2 : near_count + (k + 1) * near_count // 2]
            for k in range(steps)
        ]
        for side in (side_a, side_b)
    )
    up_mat = first_column(
        [near_up]
        + pairs(cross_up_a, cross_up_b)
        + [side_up]
        + pairs(far_up_a, far_up_b)
    )
    with jax.named_scope("c2"):
        half = jnp.concatenate(pieces, axis=0)
        other = cores(team, half)
        cross_down_b = across(team, down_b)
        far_down_a = beside(team, cross_down_a)
        mid_parts = [half] + other
        hidden, active = [], []
        for part in mid_parts:
            hidden_part, active_part = project("gelu", [part], up_mat, tall, bias_up)
            hidden.append(hidden_part)
            active.append(active_part)
        rest = fence(*active, *cross_down_b, *far_down_a, *cot_two)
        active, rest = rest[:ts], rest[ts:]
        cross_down_b, rest = rest[:steps], rest[steps:]
        far_down_a, cot_two = rest[:steps], rest[steps:]
    with jax.named_scope("s5"):
        far_down_b = beside(team, cross_down_b)
        cot_pieces = deal_across(team, home, cot_two)
        down_mat = first_column(
            [near_down]
            + pairs(cross_down_a, cross_down_b)
            + [side_down]
            + pairs(far_down_a, far_down_b)
        )
        got = core_send(team, active, down_mat, half_rows, *cot_pieces)
        total, sent = core_total(team, active, down_mat, half_rows, got)
        rest = fence(*sent, *cot_pieces)
        sent, cot_pieces = rest[: members - 1], rest[members - 1 :]
    with jax.named_scope("s6"):
        cot = to_team_order(team, dealt_in(team, home, cot_pieces))
        cot, *got = fence(cot, *team_send(team, sent))
    with jax.named_scope("s7"):
        result = team_total(total, got) + b_down
        normed, end_hat, end_rate = layer_norm(middle + result, gain_end, shift_end)
        output_own = jnp.where(query_live, normed, 0.0).astype(LOWER)
        grad_normed = jnp.where(query_live, cot.astype(WIDE), 0.0)
        grad_sum = layer_norm_back(grad_normed, gain_end, end_hat, end_rate)
        grad_result = grad_sum.astype(LOWER)
        pieces = team_pieces(team, grad_result)
        out_pieces = spread_h(team, from_team_order(team, output_own))
        rest = fence(*pieces, *out_pieces)
        pieces, out_pieces = rest[:members], rest[members:]
        grad_gend = jnp.sum(grad_normed * end_hat, axis=0)
        grad_send = jnp.sum(grad_normed, axis=0)
        grad_bdown = jnp.sum(grad_result.astype(WIDE), axis=0)
    with jax.named_scope("c3"):
        half = jnp.concatenate(pieces, axis=0)
        other = cores(team, half)
        result_parts = [half] + other
        flow_down = Grads(team, result_parts, active)
        (far_down,) = beside(team, [flow_down.send_far()])
        out_two = deal(team, dealing, out_pieces)
        grad_hidden = []
        for part, hidden_part in zip(result_parts, hidden):
            grad_hidden += project("slope", [part], down_mat, tall, hidden_part)
        got = core_send(team, grad_hidden, up_mat, half_rows, far_down, *grad_hidden, *out_two)
        total, sent = core_total(team, grad_hidden, up_mat, half_rows, got)
        cross_down = flow_down.cross(far_down)
        flow_up = Grads(team, mid_parts, grad_hidden)
        rest = fence(*sent, *cross_down, *out_two)
        sent, rest = rest[: members - 1], rest[members - 1 :]
        cross_down, out_two = rest[:steps], rest[steps:]
    with jax.named_scope("s8"):
        got = team_send(team, sent)
        down_halves = [halves(value) for value in cross_down]
        got_down_a = flow_down.go([a for a, b in down_halves])
        (far_up,) = beside(team, [flow_up.send_far()])
        far_up, *rest = fence(far_up, *got, *got_down_a, *[b for a, b in down_halves])
        got, rest = rest[:team_count], rest[team_count:]
        got_down_a, down_b = rest[:steps], rest[steps:]
    with jax.named_scope("s9"):
        grad_middle = team_total(total, got) + grad_sum
        grad_inner = layer_norm_back(grad_middle, gain_mid, mid_hat, mid_rate)
        grad_branch = grad_inner.astype(LOWER)
        pieces = team_pieces(team, grad_branch)
        got_down_b = flow_down.go(down_b)
        (near_down,) = beside(team, [flow_down.send_near()])
        cross_up = flow_up.cross(far_up)
        near_down, *rest = fence(near_down, *pieces, *got_down_b, *cross_up)
        pieces, rest = rest[:members], rest[members:]
        got_down_b, cross_up = rest[:steps], rest[steps:]
        grad_gmid = jnp.sum(grad_middle * mid_hat, axis=0)
        grad_smid = jnp.sum(grad_middle, axis=0)
        grad_bout = jnp.sum(grad_branch.astype(WIDE), axis=0)
    with jax.named_scope("c4"):
        half = jnp.concatenate(pieces, axis=0)
        other = cores(team, half)
        up_halves = [halves(value) for value in cross_up]
        got_up_a = flow_up.go([a for a, b in up_halves])
        (near_up,) = beside(team, [flow_up.send_near()])
        branch_parts = [half] + other
        attended_parts = [attended[k * half_rows : (k + 1) * half_rows] for k in range(ts)]
        flow_out = Grads(team, branch_parts, attended_parts)
        (far_out,) = beside(team, [flow_out.send_far()])
        (grad_attended,) = project("plain", branch_parts, out_mat, wide)
        grad_qkv = attend_back(qkv, grad_attended, log_sum, limits, score_scale)
        got = core_send(team, grad_qkv, qkv_mat, half_rows, near_up, *got_up_a)
        total, sent = core_total(team, grad_qkv, qkv_mat, half_rows, got)
        grad_parts = [grad_qkv[k * half_rows : (k + 1) * half_rows] for k in range(ts)]
        flow_qkv = Grads(team, in_parts, grad_parts)
        near_up, far_out, near_down, *rest = fence(
            near_up, far_out, near_down, *sent, *got_up_a, *[b for a, b in up_halves]
        )
        sent, rest = rest[: members - 1], rest[members - 1 :]
        got_up_a, up_b = rest[:steps], rest[steps:]

    qkv_sum = jnp.sum(grad_qkv.astype(WIDE), axis=0)
    grad_bup = sum(jnp.sum(part.astype(WIDE), axis=0) for part in grad_hidden)
    zeros = jnp.zeros((members, 1), WIDE)
    by_slot = [
        put(zeros * part[None], part[None], (my_slot, 0)).reshape(-1)
        for part in (qkv_sum[:wide], qkv_sum[2 * wide :], grad_bup)
    ]
    by_row = jnp.stack([grad_bout, grad_gmid, grad_smid, grad_bdown, grad_gend, grad_send])
    by_row = from_team_order(team, by_row).reshape(-1)
    sums = jnp.concatenate([by_row] + by_slot).reshape(-1, 128)
    by_row_rows = by_row.shape[0] // 128

    def add_ring(value, name):
        return value + sum(team.ring(value, name, step) for step in range(1, team.sizes[name]))

    with jax.named_scope("s10"):
        got = team_send(team, sent)
        total_down = flow_down.total(
            near_down,
            [jnp.concatenate(both, axis=0) for both in zip(got_down_a, got_down_b)],
        )
        got_up_b = flow_up.go(up_b)
        (far_qkv,) = beside(team, [flow_qkv.send_far()])
        cross_qkv, cross_out = flow_qkv.cross(far_qkv), flow_out.cross(far_out)
        both = add_ring(sums[:by_row_rows], "tp")
        sums = jnp.concatenate([both, sums[by_row_rows:]], axis=0)
        cross_att = [
            jnp.concatenate(blocks, axis=1) for blocks in zip(cross_qkv, cross_out)
        ]
        sums, total_down, near_up, *rest = fence(
            sums, total_down, near_up, *got, *got_up_b, *cross_att
        )
        got, rest = rest[:team_count], rest[team_count:]
        got_up_b, cross_att = rest[:steps], rest[steps:]
    with jax.named_scope("s11"):
        att_halves = [halves(value) for value in cross_att]
        got_att_a = flow_qkv.go([a for a, b in att_halves])
        grad_own = (team_total(total, got) + grad_inner).astype(LOWER)
        swapped = swap_home(from_team_order(team, grad_own))
        home_down = home_pieces(team, total_down)
        total_up = flow_up.total(
            near_up, [jnp.concatenate(both, axis=0) for both in zip(got_up_a, got_up_b)]
        )
        near_att = jnp.concatenate([flow_qkv.send_near(), flow_out.send_near()], axis=1)
        (near_att,) = beside(team, [near_att])
        sums, swapped, near_att, total_up, *rest = fence(
            sums, swapped, near_att, total_up, *out_two,
            *home_down, *got_att_a, *[b for a, b in att_halves]
        )
        out_two, rest = rest[:2], rest[2:]
        home_down, rest = rest[:members], rest[members:]
        got_att_a, att_b = rest[:steps], rest[steps:]
        (grad_down,) = home_join(team, home_down, [tall])
    with jax.named_scope("s12"):
        got_att_b = flow_qkv.go(att_b)
        home_up = home_pieces(team, total_up)
        sums = add_ring(sums, "y")
        grad_tokens = join_cores(team, swapped)
        output = join_cores(team, dealt_out(team, dealing, out_two))
        got_att = [jnp.concatenate(both, axis=0) for both in zip(got_att_a, got_att_b)]
        total_qkv = flow_qkv.total(
            near_att[:, : 3 * wide], [value[:, : 3 * wide] for value in got_att]
        )
        total_out = flow_out.total(
            near_att[:, 3 * wide :], [value[:, 3 * wide :] for value in got_att]
        )
        total_att = jnp.concatenate([total_qkv, total_out], axis=1)
        sums, grad_tokens, output, total_att, *home_up = fence(
            sums, grad_tokens, output, total_att, *home_up
        )
        (grad_up,) = home_join(team, home_up, [tall])
    with jax.named_scope("s13"):
        home_att = home_pieces(team, total_att)
        sums = add_ring(add_ring(add_ring(sums, "h"), "l"), "x").reshape(-1)
        grad_query, grad_key, grad_value, grad_out = home_join(team, home_att, [wide] * 4)
    smalls = []
    first = 0
    for size in [width] * 6 + [b_query.shape[0], b_value.shape[0], b_up.shape[0]]:
        smalls.append(sums[first : first + size])
        first += size
    return (
        output,
        grad_tokens,
        grad_query,
        grad_key,
        grad_value,
        grad_out,
        smalls[6],
        smalls[7],
        smalls[0],
        smalls[1],
        smalls[2],
        grad_up,
        smalls[8],
        grad_down,
        smalls[3],
        smalls[4],
        smalls[5],
    )


def solution(mesh):
    fsdp, ctx, tp = (mesh.shape[name] for name in ("fsdp", "ctx", "tp"))
    fine = Mesh(mesh.devices.reshape(fsdp // 2, 2, 2, ctx // 2, tp), ROWS + ("tp",))
    rows, split = P(ROWS, None), P(ROWS, "tp")
    in_specs = (
        (rows, P(), P())
        + (split,) * 4
        + (P("tp"), P("tp"), P(), P(), P(), split, P("tp"), split, P(), P(), P(), rows)
    )
    out_specs = (
        (rows, rows)
        + (split,) * 4
        + (P("tp"), P("tp"), P(), P(), P(), split, P("tp"), split, P(), P(), P())
    )
    return jax.shard_map(local, mesh=fine, in_specs=in_specs, out_specs=out_specs, check_vma=False)
```

```python
import functools
import math

import jax
import jax.numpy as jnp
from jax import lax
from jax.experimental import pallas as pl
from jax.experimental.pallas import tpu as pltpu
from jax.sharding import Mesh
from jax.sharding import PartitionSpec as P

HEAD = 128
EPSILON = 1e-12
NEGATIVE = -1e30
WIDE = jnp.float32
LOWER = jnp.bfloat16

TEAM = ("l", "x")
ROWS = ("h", "l", "y", "x")


def dot(left, right, dims):
    return lax.dot_general(left, right, (dims, ((), ())), preferred_element_type=WIDE)


def mm(left, right):
    return dot(left, right, ((1,), (0,)))


def mm_nt(left, right):
    return dot(left, right, ((1,), (1,)))


def mm_tn(left, right):
    return dot(left, right, ((0,), (0,)))


class Team:
    def __init__(self):
        self.sizes = {name: lax.axis_size(name) for name in ROWS + ("tp",)}
        self.at = {name: lax.axis_index(name) for name in ROWS + ("tp",)}
        ls, xs = self.sizes["l"], self.sizes["x"]
        self.offsets = [(dl, dx) for dl in range(ls) for dx in range(xs)]
        self.members = ls * xs

    def shift(self, value, offset, back=False):
        with jax.named_scope("team%d%d" % offset):
            return self.shift_(value, offset, back)

    def shift_(self, value, offset, back):
        ls, xs = self.sizes["l"], self.sizes["x"]
        dl, dx = offset
        if back:
            dl, dx = -dl, -dx
        perm = [
            (l * xs + x, ((l + dl) % ls) * xs + (x + dx) % xs) for l in range(ls) for x in range(xs)
        ]
        return lax.ppermute(value, TEAM, perm)

    def ring(self, value, name, step):
        size = self.sizes[name]
        with jax.named_scope("ring_" + name):
            return lax.ppermute(value, name, [(i, (i + step) % size) for i in range(size)])

    def slot(self, offset, back=True):
        ls, xs = self.sizes["l"], self.sizes["x"]
        dl, dx = offset
        if back:
            dl, dx = -dl, -dx
        return lax.rem(self.at["l"] + dl + ls, ls) * xs + lax.rem(self.at["x"] + dx + xs, xs)


def fence(*values):
    return lax.optimization_barrier(values)


def swap_home(value):
    perm = [(l * 2 + y, y * 2 + l) for l in range(2) for y in range(2)]
    return lax.ppermute(value, ("l", "y"), perm)


def team_pieces(team, piece):
    far = team.shift(piece, (1, 0))
    across_x = [(0, dx) for dx in range(1, team.sizes["x"])]
    return (
        [piece]
        + [team.shift(piece, offset) for offset in across_x]
        + [far]
        + [team.shift(far, offset) for offset in across_x]
    )


def cores(team, value):
    return [team.ring(value, "tp", step) for step in range(1, team.sizes["tp"])]


def row_blocks(team):
    ts = team.sizes["tp"]
    return [
        team.slot(offset) * ts + lax.rem(team.at["tp"] - step + ts, ts)
        for step in range(ts)
        for offset in team.offsets
    ]


def core_send(team, rows, pieces, half_rows, *others):
    sent = [spread(rows, step, pieces, half_rows) for step in range(1, team.sizes["tp"])]
    sent = fence(*sent, *others)[: len(sent)]
    return [team.ring(value, "tp", -step) for step, value in enumerate(sent, 1)]


def core_total(team, rows, pieces, half_rows, got):
    total, *sent = spread(rows, 0, pieces, half_rows, got, team.members)
    return total, sent


def team_send(team, sent):
    xs = team.sizes["x"]
    across_x = [(0, dx) for dx in range(1, xs)]
    far = sent[xs - 1].astype(WIDE)
    for value, offset in zip(sent[xs:], across_x):
        far = far + team.shift(value, offset, back=True).astype(WIDE)
    got = [team.shift(value, offset, back=True) for value, offset in zip(sent, across_x)]
    return got + [team.shift(far.astype(LOWER), (1, 0), back=True)]


def team_total(own, got):
    for value in got:
        own = own + value.astype(WIDE)
    return own


def put(buffer, value, starts):
    return lax.dynamic_update_slice(buffer, value, starts)


def share_columns(team, shards):
    widths = [shard.shape[1] // team.members for shard in shards]
    pieces = []
    for j, offset in enumerate(team.offsets):
        slot = team.slot(offset, back=False)
        cuts = [
            lax.dynamic_slice_in_dim(shard, slot * each, each, 1)
            for shard, each in zip(shards, widths)
        ]
        piece = jnp.concatenate(cuts, axis=1)
        pieces.append(team.shift(piece, offset) if j > 0 else piece)
    return pieces


def place_rows_kernel(widths, slots_ref, *refs):
    pieces, outs = refs[: len(refs) - len(widths)], refs[len(refs) - len(widths) :]
    for j, piece in enumerate(pieces):
        height = piece.shape[0]
        row = pl.multiple_of(slots_ref[j] * height, height)
        first = 0
        for out, width in zip(outs, widths):
            out[pl.ds(row, height), :] = piece[:, first : first + width]
            first += width


def place_columns_kernel(widths, slots_ref, *refs):
    pieces, outs = refs[: len(refs) - len(widths)], refs[len(refs) - len(widths) :]
    for j, piece in enumerate(pieces):
        first = 0
        for out, width in zip(outs, widths):
            column = pl.multiple_of(slots_ref[j] * width, width)
            block = piece[:, first : first + width].astype(out.dtype)
            out[:, pl.ds(column, width)] = block
            first += width


def place(team, kernel, pieces, widths, shapes):
    slots = jnp.stack([team.slot(offset) for offset in team.offsets]).astype(jnp.int32)
    whole = [pl.BlockSpec(piece.shape, lambda n: (0, 0)) for piece in pieces]
    return pl.pallas_call(
        functools.partial(kernel, widths),
        grid=(1,),
        in_specs=[pl.BlockSpec(memory_space=pltpu.SMEM)] + whole,
        out_specs=[pl.BlockSpec(shape.shape, lambda n: (0, 0)) for shape in shapes],
        out_shape=shapes,
        cost_estimate=LIGHT,
        compiler_params=KERNEL,
    )(slots, *pieces)


def stack_rows_kernel(*refs):
    height = refs[0].shape[0]
    for j, piece in enumerate(refs[:-1]):
        refs[-1][j * height : (j + 1) * height, :] = piece[...]


def stack_rows(pieces):
    height, width = pieces[0].shape
    rows = height * len(pieces)
    return pl.pallas_call(
        stack_rows_kernel,
        grid=(1,),
        in_specs=[pl.BlockSpec((height, width), lambda n: (0, 0)) for _ in pieces],
        out_specs=pl.BlockSpec((rows, width), lambda n: (0, 0)),
        out_shape=jax.ShapeDtypeStruct((rows, width), pieces[0].dtype),
        cost_estimate=LIGHT,
        compiler_params=KERNEL,
    )(*pieces)


def near_rows(team, pieces, widths):
    rows = pieces[0].shape[0] * team.members
    shapes = [jax.ShapeDtypeStruct((rows, width), LOWER) for width in widths]
    return place(team, place_rows_kernel, pieces, widths, shapes)


def across(team, value):
    return [team.ring(value, "h", -step) for step in range(1, team.sizes["h"])]


def beside(team, values):
    return [team.ring(value, "y", 1) for value in values]


def halves(value):
    middle = value.shape[0] // 2
    return value[:middle], value[middle:]


def pairs(firsts, seconds):
    return [part for pair in zip(firsts, seconds) for part in pair]


def add_ring(team, value, name):
    return value + sum(team.ring(value, name, step) for step in range(1, team.sizes[name]))


class Grads:
    def __init__(self, team, lefts, rights):
        self.team, self.lefts, self.rights = team, lefts, rights
        self.far = lefts[0].shape[1] // 2
        self.near = self.far // team.sizes["h"]

        self.half = self.near // 2
        self.steps = range(1, team.sizes["h"])

    def rows(self, first, count, adds=(), offset=0, column=0):
        return outer(self.lefts, self.rights, first, count, adds, offset, column)

    def send_far(self):
        return self.rows(self.far + self.near, self.far - self.near)

    def send_half(self, part):
        start = self.far + part * self.half
        return [self.rows(start + step * self.near, self.half) for step in self.steps]

    def send_near(self):
        return self.rows(self.far, self.near)

    def cross(self, got):
        offsets = [(step - 1) * self.near for step in self.steps]
        return [self.rows(self.near + first, self.near, [got], first) for first in offsets]

    def cross_half(self, part, got):
        offsets = [(step - 1) * self.near + part * self.half for step in self.steps]
        return [self.rows(self.near + first, self.half, [got], first) for first in offsets]

    def cross_halves(self, part, gots):
        start = part * self.half
        return [
            self.rows(start + step * self.near, self.half, [got])
            for step, got in zip(self.steps, gots)
        ]

    def go(self, sent):
        return [self.team.ring(value, "h", step) for step, value in zip(self.steps, sent)]

    def total(self, got, crossed, column=0):
        return self.rows(0, self.near, [got, *crossed], column=column)


def home_pieces(team, total):
    height = total.shape[0] // team.members
    total = total.reshape(team.members, height, -1)
    pieces = []
    for j, offset in enumerate(team.offsets):
        piece = lax.dynamic_index_in_dim(total, team.slot(offset, back=False), 0, False)
        pieces.append(team.shift(piece, offset) if j > 0 else piece)
    return pieces


def home_join(team, pieces, widths):
    height = pieces[0].shape[0]
    shapes = [jax.ShapeDtypeStruct((height, width * team.members), WIDE) for width in widths]
    return place(team, place_columns_kernel, pieces, widths, shapes)


def permute_kernel(count, table_ref, value_ref, out_ref):
    block = value_ref.shape[1] // count
    for i in range(count):
        column = pl.multiple_of(table_ref[i] * block, block)
        out_ref[:, i * block : (i + 1) * block] = value_ref[:, pl.ds(column, block)]


def permute_columns(value, table):
    whole = pl.BlockSpec(value.shape, lambda n: (0, 0))
    return pl.pallas_call(
        functools.partial(permute_kernel, len(table)),
        grid=(1,),
        in_specs=[pl.BlockSpec(memory_space=pltpu.SMEM), whole],
        out_specs=whole,
        out_shape=jax.ShapeDtypeStruct(value.shape, value.dtype),
        cost_estimate=LIGHT,
    )(jnp.stack(table).astype(jnp.int32), value)


def to_team_order(team, value):
    hs = team.sizes["h"]
    table = []
    for dy in range(2):
        for dh in range(hs):
            for l in range(2):
                h, y = lax.rem(team.at["h"] + dh, hs), lax.rem(team.at["y"] + dy, 2)
                table.append((h * 2 + l) * 2 + y)
    return permute_columns(value, table)


def from_team_order(team, value):
    hs = team.sizes["h"]
    table = []
    for h in range(hs):
        for l in range(2):
            for y in range(2):
                dh, dy = lax.rem(h - team.at["h"] + hs, hs), lax.rem(y - team.at["y"] + 2, 2)
                table.append((dy * hs + dh) * 2 + l)
    return permute_columns(value, table)


def pick(table, index):
    ids = jnp.arange(table.shape[0], dtype=jnp.int32)
    return jnp.sum(jnp.where(ids == index, table, 0))


def choose(pieces, index):
    out = pieces[0]
    for i in range(1, len(pieces)):
        out = jnp.where(index == i, pieces[i], out)
    return out


def spread_h(team, piece):
    return [piece] + [team.ring(piece, "h", step) for step in range(1, team.sizes["h"])]


def deal_flip(team, piece, flip):
    perm = []
    for l in range(2):
        for y in range(2):
            perm.append((l * 2 + y, y * 2 + (l if flip == 0 else 1 - l)))
    with jax.named_scope("flip"):
        return lax.ppermute(piece, ("l", "y"), perm)


def deal_across(team, home, two):
    hs = team.sizes["h"]

    def needed(h):
        group = pick(home, h * 2 + team.at["y"])
        return jnp.where(lax.rem(group, 2) == team.at["y"], two[0], two[1])

    return [needed(team.at["h"])] + [
        team.ring(needed(lax.rem(team.at["h"] + step, hs)), "h", step) for step in range(1, hs)
    ]


def dealt_in(team, home, pieces):
    hs = team.sizes["h"]
    group = pick(home, team.at["h"] * 2 + team.at["y"])
    return choose(pieces, lax.rem(team.at["h"] - group // 2 + hs, hs))


def deal(team, dealing, pieces):
    hs = team.sizes["h"]
    got = []
    for flip in range(2):
        target = team.at["y"] if flip == 0 else 1 - team.at["y"]
        seq = pick(dealing, team.at["h"] * 2 + target)
        sent = choose(pieces, lax.rem(team.at["h"] - seq // 2 + hs, hs))
        perm = []
        for l in range(2):
            for y in range(2):
                perm.append((l * 2 + y, (y if flip == 0 else 1 - y) * 2 + l))
        with jax.named_scope("flip"):
            got.append(lax.ppermute(sent, ("l", "y"), perm))
    return got


def dealt_out(team, dealing, got):
    seq = pick(dealing, team.at["h"] * 2 + team.at["l"])
    return jnp.where(lax.rem(seq, 2) == team.at["l"], got[0], got[1])


def join_cores(team, piece):
    ts = team.sizes["tp"]
    out = jnp.zeros((ts,) + piece.shape, piece.dtype)
    for step in range(ts):
        other = team.ring(piece, "tp", step) if step else piece
        out = put(out, other[None], (lax.rem(team.at["tp"] - step + ts, ts), 0, 0))
    return out.reshape(-1, piece.shape[-1])


def layer_norm(inputs, gain_vec, shift_vec):
    row_mean = jnp.mean(inputs, axis=-1, keepdims=True)
    centred = inputs - row_mean
    spread = jnp.mean(centred * centred, axis=-1, keepdims=True)
    rate = lax.rsqrt(spread + EPSILON)
    xhat = centred * rate
    return xhat * gain_vec + shift_vec, xhat, rate


def layer_norm_back(grad, gain_vec, xhat, rate):
    scaled = grad * gain_vec
    return rate * (
        scaled
        - jnp.mean(scaled, axis=-1, keepdims=True)
        - xhat * jnp.mean(scaled * xhat, axis=-1, keepdims=True)
    )


def gelu_tanh(inputs):
    return jax.nn.gelu(inputs, approximate=True)


def masked_scores(key_ref, query, limits_ref, scale):
    count = limits_ref.shape[0]
    height = key_ref.shape[0] // count
    blocks = []
    for j in range(count):
        block = mm_nt(key_ref[j * height : (j + 1) * height, :], query) * scale
        row = lax.broadcasted_iota(jnp.int32, block.shape, 0)
        blocks.append(jnp.where(row < limits_ref[j], block, NEGATIVE))
    return blocks


def attend_kernel(scale, limits_ref, query_ref, key_ref, value_ref, out_ref, log_ref):
    blocks = masked_scores(key_ref, query_ref[...], limits_ref, scale)
    row_max = functools.reduce(jnp.maximum, blocks)
    row_max = jnp.max(row_max, axis=0, keepdims=True)
    blocks = [jnp.exp(block - row_max) for block in blocks]
    total = jnp.sum(functools.reduce(jnp.add, blocks), axis=0, keepdims=True)
    inverse = 1.0 / total
    height = key_ref.shape[0] // len(blocks)
    out = None
    for j, block in enumerate(blocks):
        value = value_ref[j * height : (j + 1) * height, :]
        term = mm_tn(value, (block * inverse).astype(LOWER))
        out = term if out is None else out + term
    out_ref[...] = out.T.astype(LOWER)
    log_ref[0] = row_max + jnp.log(total)


def attend_back_kernel(
    scale, wide, limits_ref, query_ref, key_ref, value_ref, grad_ref, log_ref, out_ref, key_sum, value_sum
):
    head, step = pl.program_id(0), pl.program_id(1)
    query, grad = query_ref[...], grad_ref[...]
    blocks = masked_scores(key_ref, query, limits_ref, scale)
    count = len(blocks)
    height = key_ref.shape[0] // count
    part = [slice(j * height, (j + 1) * height) for j in range(count)]
    log_sum = log_ref[0]
    probs = [jnp.exp(block - log_sum) for block in blocks]
    grad_probs = [mm_nt(value_ref[rows, :], grad) for rows in part]
    delta = functools.reduce(jnp.add, [p * g for p, g in zip(probs, grad_probs)])
    delta = jnp.sum(delta, axis=0, keepdims=True)

    @pl.when(step == 0)
    def _():
        key_sum[...] = jnp.zeros_like(key_sum)
        value_sum[...] = jnp.zeros_like(value_sum)

    grad_query = None
    for j, rows in enumerate(part):
        scores = (probs[j] * (grad_probs[j] - delta)).astype(LOWER)
        term = mm_tn(key_ref[rows, :], scores)
        grad_query = term if grad_query is None else grad_query + term
        key_sum[rows, :] += mm(scores, query)
        value_sum[rows, :] += mm(probs[j].astype(LOWER), grad)
    count = query.shape[0]
    first = pl.multiple_of(step * count, count)
    column = pl.multiple_of(head * HEAD, HEAD)
    out_ref[pl.ds(first, count), pl.ds(column, HEAD)] = (grad_query.T * scale).astype(LOWER)

    @pl.when(step == pl.num_programs(1) - 1)
    def _():
        out_ref[:, pl.ds(wide + column, HEAD)] = (key_sum[...] * scale).astype(LOWER)
        out_ref[:, pl.ds(2 * wide + column, HEAD)] = value_sum[...].astype(LOWER)


LIGHT = pl.CostEstimate(flops=1000000, bytes_accessed=100000, transcendentals=0)
KERNEL = pltpu.CompilerParams(vmem_limit_bytes=24 * 1024 * 1024)


def gelu_slope(value):
    inner = math.sqrt(2.0 / math.pi)
    square = value * value
    tanh = jnp.tanh(inner * value * (1.0 + 0.044715 * square))
    return 0.5 * (1.0 + tanh) + 0.5 * value * (1.0 - tanh * tanh) * inner * (
        1.0 + 3.0 * 0.044715 * square
    )


def project_kernel(mode, part_count, piece_count, steps, *refs):
    parts, pieces = refs[:part_count], refs[part_count : part_count + piece_count]
    rest = refs[part_count + piece_count :]
    index = pl.program_id(0)

    def run(rows):
        total = None
        first = 0
        for piece in pieces:
            depth = piece.shape[0]
            term = mm(rows[:, first : first + depth], piece[...])
            total = term if total is None else total + term
            first += depth
        if mode == "bias":
            rest[1][...] = (total + rest[0][...]).astype(LOWER)
        elif mode == "gelu":
            total = total + rest[0][...]
            rest[1][...] = total
            rest[2][...] = gelu_tanh(total).astype(LOWER)
        elif mode == "slope":
            rest[1][...] = (total * gelu_slope(rest[0][...])).astype(LOWER)
        else:
            rest[0][...] = total.astype(LOWER)

    for place in range(part_count):

        @pl.when(index // steps == place)
        def _():
            run(parts[place][...])


def project(mode, parts, pieces, width, extra=None):
    half_rows, depth = parts[0].shape
    block = min(256, half_rows)
    steps = half_rows // block
    rows = half_rows * len(parts)

    def part_at(place):
        return lambda i: (jnp.clip(i - place * steps, 0, steps - 1), 0)

    in_specs = [pl.BlockSpec((block, depth), part_at(place)) for place in range(len(parts))]
    for array, column in pieces:
        in_specs.append(
            pl.BlockSpec((array.shape[0], width), functools.partial(lambda c, i: (0, c), column))
        )
    arrays = list(parts) + [array for array, _ in pieces]
    tile = pl.BlockSpec((block, width), lambda i: (i, 0))
    if mode in ("bias", "gelu"):
        in_specs.append(pl.BlockSpec((1, width), lambda i: (0, 0)))
        arrays.append(extra[None])
    elif mode == "slope":
        in_specs.append(tile)
        arrays.append(extra)
    shapes = [jax.ShapeDtypeStruct((rows, width), LOWER)]
    if mode == "gelu":
        shapes = [jax.ShapeDtypeStruct((rows, width), WIDE)] + shapes
    return pl.pallas_call(
        functools.partial(project_kernel, mode, len(parts), len(pieces), steps),
        grid=(len(parts) * steps,),
        in_specs=in_specs,
        out_specs=[tile] * len(shapes),
        out_shape=shapes,
        cost_estimate=LIGHT,
        compiler_params=KERNEL,
    )(*arrays)


def spread_kernel(piece_count, got_count, members, rows_ref, *refs):
    pieces, gots = refs[:piece_count], refs[piece_count : piece_count + got_count]
    outs = refs[piece_count + got_count :]
    rows = rows_ref[...]
    height = rows.shape[0] // members
    first = 0
    for piece in pieces:
        columns = slice(first, first + piece.shape[0])
        total = mm_nt(rows, piece[...])
        for got in gots:
            total = total + got[:, columns].astype(WIDE)
        for j, out in enumerate(outs):
            out[:, columns] = total[j * height : (j + 1) * height].astype(out.dtype)
        first += piece.shape[0]


def spread(rows, place, pieces, half_rows, got=(), members=0):
    if isinstance(rows, (list, tuple)):
        rows, place = rows[place], 0
    depth = rows.shape[1]
    width = sum(array.shape[0] for array, _ in pieces)
    in_specs = [pl.BlockSpec((half_rows, depth), lambda n: (place, 0))]
    for array, column in pieces:
        in_specs.append(
            pl.BlockSpec((array.shape[0], depth), functools.partial(lambda c, n: (0, c), column))
        )
    in_specs += [pl.BlockSpec((half_rows, width), lambda n: (0, 0))] * len(got)
    split = max(members, 1)
    height = half_rows // split
    dtypes = [WIDE] + [LOWER] * (members - 1) if members else [LOWER]
    out = pl.pallas_call(
        functools.partial(spread_kernel, len(pieces), len(got), split),
        grid=(1,),
        in_specs=in_specs,
        out_specs=[pl.BlockSpec((height, width), lambda n: (0, 0))] * split,
        out_shape=[jax.ShapeDtypeStruct((height, width), dtype) for dtype in dtypes],
        cost_estimate=LIGHT,
        compiler_params=KERNEL,
    )(rows, *[array for array, _ in pieces], *got)
    return out if members else out[0]


def outer_kernel(part_count, add_count, *refs):
    lefts, rights = refs[:part_count], refs[part_count : 2 * part_count]
    adds, out = refs[2 * part_count : 2 * part_count + add_count], refs[-1]
    total = None
    for left, right in zip(lefts, rights):
        term = mm_tn(left[...], right[...])
        total = term if total is None else total + term
    for add in adds:
        total = total + add[...].astype(WIDE)
    out[...] = total.astype(out.dtype)


def outer(lefts, rights, first, count, adds, offset, column):
    height, width = rights[0].shape
    block = math.gcd(256, count)
    in_specs = [pl.BlockSpec((height, block), lambda i: (0, first // block + i)) for _ in lefts]
    in_specs += [pl.BlockSpec((height, width), lambda i: (0, 0)) for _ in rights]
    tile = pl.BlockSpec((block, width), lambda i: (i, 0))
    add_tile = pl.BlockSpec((block, width), lambda i: (offset // block + i, 0))
    first_tile = pl.BlockSpec((block, width), lambda i: (offset // block + i, column))
    return pl.pallas_call(
        functools.partial(outer_kernel, len(lefts), len(adds)),
        grid=(count // block,),
        in_specs=in_specs + [first_tile] * len(adds[:1]) + [add_tile] * len(adds[1:]),
        out_specs=tile,
        out_shape=jax.ShapeDtypeStruct((count, width), LOWER),
        cost_estimate=LIGHT,
        compiler_params=KERNEL,
    )(*lefts, *rights, *adds)


def query_block(rows):
    return min(256, rows)


def attend(qkv, limits, scale):
    rows, wide = qkv.shape[0], qkv.shape[1] // 3
    heads, block = wide // HEAD, query_block(rows)
    return pl.pallas_call(
        functools.partial(attend_kernel, scale),
        grid=(heads, rows // block),
        in_specs=[
            pl.BlockSpec(memory_space=pltpu.SMEM),
            pl.BlockSpec((block, HEAD), lambda h, i: (i, h)),
            pl.BlockSpec((rows, HEAD), lambda h, i: (0, heads + h)),
            pl.BlockSpec((rows, HEAD), lambda h, i: (0, 2 * heads + h)),
        ],
        out_specs=[
            pl.BlockSpec((block, HEAD), lambda h, i: (i, h)),
            pl.BlockSpec((1, 1, block), lambda h, i: (h, 0, i)),
        ],
        out_shape=[
            jax.ShapeDtypeStruct((rows, wide), LOWER),
            jax.ShapeDtypeStruct((heads, 1, rows), WIDE),
        ],
        cost_estimate=LIGHT,
        compiler_params=KERNEL,
    )(limits, qkv, qkv, qkv)


def attend_back(qkv, grad, log_sum, limits, scale):
    rows, wide = grad.shape
    heads, block = wide // HEAD, query_block(rows)
    return pl.pallas_call(
        functools.partial(attend_back_kernel, scale, wide),
        grid=(heads, rows // block),
        in_specs=[
            pl.BlockSpec(memory_space=pltpu.SMEM),
            pl.BlockSpec((block, HEAD), lambda h, i: (i, h)),
            pl.BlockSpec((rows, HEAD), lambda h, i: (0, heads + h)),
            pl.BlockSpec((rows, HEAD), lambda h, i: (0, 2 * heads + h)),
            pl.BlockSpec((block, HEAD), lambda h, i: (i, h)),
            pl.BlockSpec((1, 1, block), lambda h, i: (h, 0, i)),
        ],
        out_specs=pl.BlockSpec((rows, 3 * wide), lambda h, i: (0, 0)),
        out_shape=jax.ShapeDtypeStruct((rows, 3 * wide), LOWER),
        scratch_shapes=[pltpu.VMEM((rows, HEAD), WIDE), pltpu.VMEM((rows, HEAD), WIDE)],
        cost_estimate=LIGHT,
        compiler_params=KERNEL,
    )(limits, qkv, qkv, qkv, grad, log_sum)


def local(
    tokens,
    lengths,
    dealing,
    w_query,
    w_key,
    w_value,
    w_out,
    b_query,
    b_value,
    b_out,
    gain_mid,
    shift_mid,
    w_up,
    b_up,
    w_down,
    b_down,
    gain_end,
    shift_end,
    cotangent,
):
    team = Team()
    ts, members = team.sizes["tp"], team.members
    row_count = tokens.shape[0] // ts
    wide = w_query.shape[1] // members
    tall = w_up.shape[1] // members
    width = tokens.shape[1]
    score_scale = 1.0 / math.sqrt(HEAD)
    my_slot = team.at["l"] * team.sizes["x"] + team.at["x"]
    seq_ids = jnp.arange(dealing.shape[0], dtype=jnp.int32)
    home = jnp.sum(jnp.where(dealing[None, :] == seq_ids[:, None], seq_ids[None, :], 0), axis=1)
    live_count = pick(lengths, team.at["h"] * 2 + team.at["y"])
    limits = live_count - jnp.stack(row_blocks(team)).astype(jnp.int32) * row_count
    query_live = (jnp.arange(row_count, dtype=jnp.int32) < limits[0])[:, None]
    half_at = team.at["tp"] * row_count

    half_rows = members * row_count
    vectors = jnp.stack([b_out, gain_mid, shift_mid, b_down, gain_end, shift_end])
    b_out, gain_mid, shift_mid, b_down, gain_end, shift_end = to_team_order(team, vectors)
    bias_q = lax.dynamic_slice_in_dim(b_query, my_slot * wide, wide, 0)
    bias_v = lax.dynamic_slice_in_dim(b_value, my_slot * wide, wide, 0)
    bias_up = lax.dynamic_slice_in_dim(b_up, my_slot * tall, tall, 0)
    bias_qkv = jnp.concatenate([bias_q, jnp.zeros_like(bias_q), bias_v])
    steps = team.sizes["h"] - 1
    team_count = team.sizes["x"]


    def first_column(arrays):
        return [(array, 0) for array in arrays]

    with jax.named_scope("a0"):
        own = swap_home(lax.dynamic_slice_in_dim(tokens, half_at, row_count, 0))
        share = share_columns(team, [w_query, w_key, w_value, w_out])
        own, w_up, w_down, bias_qkv, bias_up, *share = fence(
            own, w_up, w_down, bias_qkv, bias_up, *share
        )
    with jax.named_scope("a1"):
        own = to_team_order(team, own)
        (near_att,) = near_rows(team, share, [4 * wide])
        pieces = team_pieces(team, own)
        cross_qkv = across(team, near_att[:, : 3 * wide])
        (side_att,) = beside(team, [near_att])
        near_att, w_up, w_down, cotangent, side_att, *rest = fence(
            near_att, w_up, w_down, cotangent, side_att, *pieces, *cross_qkv
        )
        pieces, cross_qkv = rest[:members], rest[members:]
    with jax.named_scope("a2"):
        half = stack_rows(pieces)
        other = cores(team, half)
        far_qkv = beside(team, cross_qkv)
        cross_out = across(team, near_att[:, 3 * wide :])
        share = share_columns(team, [w_up])
        cotangent, w_down, *rest = fence(
            cotangent, w_down, half, *other, *share, *far_qkv, *cross_out
        )
        in_parts = rest[:ts]
        share, rest = rest[ts : ts + members], rest[ts + members :]
        far_qkv, cross_out = rest[:steps], rest[steps:]
    qkv_mat = first_column([near_att, *cross_qkv, side_att, *far_qkv])
    with jax.named_scope("c1"):
        (near_up,) = near_rows(team, share, [tall])
        up_a, up_b = halves(near_up)
        cross_up_a = across(team, up_a)
        far_out = beside(team, cross_out)
        cot_half = lax.dynamic_slice_in_dim(cotangent, half_at, row_count, 0)
        cot_one = deal_flip(team, cot_half, 0)
        share = share_columns(team, [w_down])
        (qkv,) = project("bias", in_parts, qkv_mat, 3 * wide, bias_qkv)
        attended, log_sum = attend(qkv, limits, score_scale)
        out_mat = [(near_att, 3), *first_column(cross_out), (side_att, 3), *first_column(far_out)]
        got = core_send(team, attended, out_mat, half_rows, cot_one, *cross_up_a, *share)
        total, sent = core_total(team, attended, out_mat, half_rows, got)
        up_b, near_up, cot_half, cot_one, *rest = fence(
            up_b, near_up, cot_half, cot_one, *cross_up_a, *share, *sent
        )
        cross_up_a, rest = rest[:steps], rest[steps:]
        share, sent = rest[:members], rest[members:]
    with jax.named_scope("s3"):
        got = team_send(team, sent)
        cross_up_b = across(team, up_b)
        (near_down,) = near_rows(team, share, [tall])
        side = beside(team, [jnp.concatenate([near_up, *cross_up_a], axis=0)])
        near_down, *rest = fence(near_down, *got, *cross_up_b, *side)
        got, rest = rest[:team_count], rest[team_count:]
        cross_up_b, side_a = rest[:steps], rest[steps]
    with jax.named_scope("s4"):
        branch = team_total(total, got) + b_out
        middle, mid_hat, mid_rate = layer_norm(own.astype(WIDE) + branch, gain_mid, shift_mid)
        pieces = team_pieces(team, middle.astype(LOWER))
        down_a, down_b = halves(near_down)
        cross_down_a = across(team, down_a)
        side = beside(team, [jnp.concatenate([near_down, *cross_up_b], axis=0)])
        near_down, down_b, *rest = fence(near_down, down_b, *pieces, *cross_down_a, *side)
        pieces, rest = rest[:members], rest[members:]
        cross_down_a, side_b = rest[:steps], rest[steps]
    whole, part = near_down.shape[0], down_a.shape[0]
    side_up, side_down = side_a[:whole], side_b[:whole]
    far_up_a, far_up_b = (
        [side[whole + k * part : whole + (k + 1) * part] for k in range(steps)]
        for side in (side_a, side_b)
    )
    up_mat = first_column(
        [near_up]
        + pairs(cross_up_a, cross_up_b)
        + [side_up]
        + pairs(far_up_a, far_up_b)
    )
    with jax.named_scope("c2"):
        half = stack_rows(pieces)
        other = cores(team, half)
        cross_down_b = across(team, down_b)
        far_down_a = beside(team, cross_down_a)
        mid_parts = [half] + other
        hidden, active = [], []
        for part in mid_parts:
            hidden_part, active_part = project("gelu", [part], up_mat, tall, bias_up)
            hidden.append(hidden_part)
            active.append(active_part)
        cot_two = [cot_one, deal_flip(team, cot_half, 1)]
        rest = fence(*active, *cross_down_b, *far_down_a, *cot_two)
        active, rest = rest[:ts], rest[ts:]
        cross_down_b, rest = rest[:steps], rest[steps:]
        far_down_a, cot_two = rest[:steps], rest[steps:]
    with jax.named_scope("s5"):
        far_down_b = beside(team, cross_down_b)
        cot_pieces = deal_across(team, home, cot_two)
        down_mat = first_column(
            [near_down]
            + pairs(cross_down_a, cross_down_b)
            + [side_down]
            + pairs(far_down_a, far_down_b)
        )
        got = core_send(team, active, down_mat, half_rows, *cot_pieces)
        total, sent = core_total(team, active, down_mat, half_rows, got)
        rest = fence(*sent, *cot_pieces)
        sent, cot_pieces = rest[: members - 1], rest[members - 1 :]
    with jax.named_scope("s6"):
        cot = to_team_order(team, dealt_in(team, home, cot_pieces))
        cot, *got = fence(cot, *team_send(team, sent))
    with jax.named_scope("s7"):
        result = team_total(total, got) + b_down
        normed, end_hat, end_rate = layer_norm(middle + result, gain_end, shift_end)
        output_own = jnp.where(query_live, normed, 0.0).astype(LOWER)
        grad_normed = jnp.where(query_live, cot.astype(WIDE), 0.0)
        grad_sum = layer_norm_back(grad_normed, gain_end, end_hat, end_rate)
        grad_result = grad_sum.astype(LOWER)
        pieces = team_pieces(team, grad_result)
        out_pieces = spread_h(team, from_team_order(team, output_own))
        rest = fence(*pieces, *out_pieces)
        pieces, out_pieces = rest[:members], rest[members:]
        grad_gend = jnp.sum(grad_normed * end_hat, axis=0)
        grad_send = jnp.sum(grad_normed, axis=0)
        grad_bdown = jnp.sum(grad_result.astype(WIDE), axis=0)
    with jax.named_scope("c3"):
        half = stack_rows(pieces)
        other = cores(team, half)
        result_parts = [half] + other
        flow_down = Grads(team, result_parts, active)
        far_down_a = beside(team, flow_down.send_half(0))
        grad_hidden = []
        for part, hidden_part in zip(result_parts, hidden):
            grad_hidden += project("slope", [part], down_mat, tall, hidden_part)
        got = core_send(team, grad_hidden, up_mat, half_rows, *far_down_a, *grad_hidden)
        total, sent = core_total(team, grad_hidden, up_mat, half_rows, got)
        cross_down = flow_down.cross_halves(0, far_down_a)
        flow_up = Grads(team, mid_parts, grad_hidden)
        rest = fence(*sent, *cross_down)
        sent, cross_down = rest[: members - 1], rest[members - 1 :]
    with jax.named_scope("s8"):
        got = team_send(team, sent)
        got_down_a = flow_down.go(cross_down)
        far_down_b = beside(team, flow_down.send_half(1))
        far_up, *far_down_b = fence(flow_up.send_far(), *far_down_b)
        (far_up,) = beside(team, [far_up])
        cross_down = flow_down.cross_halves(1, far_down_b)
        far_up, *rest = fence(far_up, *got, *got_down_a, *cross_down)
        got, rest = rest[:team_count], rest[team_count:]
        got_down_a, cross_down = rest[:steps], rest[steps:]
    with jax.named_scope("s9"):
        grad_middle = team_total(total, got) + grad_sum
        grad_inner = layer_norm_back(grad_middle, gain_mid, mid_hat, mid_rate)
        grad_branch = grad_inner.astype(LOWER)
        pieces = team_pieces(team, grad_branch)
        got_down_b = flow_down.go(cross_down)
        (near_down,) = beside(team, [flow_down.send_near()])
        grad_gmid = jnp.sum(grad_middle * mid_hat, axis=0)
        grad_smid = jnp.sum(grad_middle, axis=0)
        grad_bout = jnp.sum(grad_branch.astype(WIDE), axis=0)
        by_row = jnp.stack([grad_bout, grad_gmid, grad_smid, grad_bdown, grad_gend, grad_send])
        by_row = add_ring(team, from_team_order(team, by_row), "tp")
        cross_up_a, cross_up_b = flow_up.cross_half(0, far_up), flow_up.cross_half(1, far_up)
        by_row, near_down, *rest = fence(by_row, near_down, *pieces, *got_down_b, *cross_up_a, *cross_up_b)
        pieces, rest = rest[:members], rest[members:]
        got_down_b, rest = rest[:steps], rest[steps:]
        cross_up_a, cross_up_b = rest[:steps], rest[steps:]
    with jax.named_scope("c4"):
        half = stack_rows(pieces)
        other = cores(team, half)
        got_up_a, got_up_b = flow_up.go(cross_up_a), flow_up.go(cross_up_b)
        out_two = deal(team, dealing, out_pieces)
        branch_parts = [half] + other
        attended_parts = [attended[k * half_rows : (k + 1) * half_rows] for k in range(ts)]
        flow_out = Grads(team, branch_parts, attended_parts)
        (far_out,) = beside(team, [flow_out.send_far()])
        (grad_attended,) = project("plain", branch_parts, out_mat, wide)
        grad_qkv = attend_back(qkv, grad_attended, log_sum, limits, score_scale)
        got = core_send(team, grad_qkv, qkv_mat, half_rows, far_out, *got_up_a, *out_two)
        total, sent = core_total(team, grad_qkv, qkv_mat, half_rows, got)
        grad_parts = [grad_qkv[k * half_rows : (k + 1) * half_rows] for k in range(ts)]
        flow_qkv = Grads(team, in_parts, grad_parts)
        qkv_sum = jnp.sum(grad_qkv.astype(WIDE), axis=0)
        grad_bup = sum(jnp.sum(part.astype(WIDE), axis=0) for part in grad_hidden)
        zeros = jnp.zeros((members, 1), WIDE)
        by_slot = [
            put(zeros * part[None], part[None], (my_slot, 0)).reshape(-1)
            for part in (qkv_sum[:wide], qkv_sum[2 * wide :], grad_bup)
        ]
        sums = jnp.concatenate([by_row.reshape(-1)] + by_slot).reshape(-1, 128)
        sums = add_ring(team, sums, "l")
        (far_qkv,) = beside(team, [flow_qkv.send_far()])
        cross_out, cross_qkv = flow_out.cross(far_out), flow_qkv.cross(far_qkv)
        sums, near_down, *rest = fence(
            sums, near_down, *cross_out, *cross_qkv, *sent, *got_up_a, *got_up_b, *out_two
        )
        cross_out, cross_qkv, rest = rest[:steps], rest[steps : 2 * steps], rest[2 * steps :]
        sent, rest = rest[: members - 1], rest[members - 1 :]
        got_up_a, got_up_b, out_two = rest[:steps], rest[steps : 2 * steps], rest[2 * steps :]

    with jax.named_scope("s10"):
        got = team_send(team, sent)
        total_down = flow_down.total(
            near_down,
            [jnp.concatenate(both, axis=0) for both in zip(got_down_a, got_down_b)],
        )
        got_qkv = flow_qkv.go(cross_qkv)
        (near_up,) = beside(team, [flow_up.send_near()])
        sums = add_ring(team, sums, "x")
        sums, total_down, near_up, *rest = fence(
            sums, total_down, near_up, *out_two, *got, *got_qkv, *cross_out
        )
        out_two, rest = rest[:2], rest[2:]
        got, rest = rest[:team_count], rest[team_count:]
        got_qkv, cross_out = rest[:steps], rest[steps:]
    with jax.named_scope("s11"):
        got_out = flow_out.go(cross_out)
        home_down = home_pieces(team, total_down)
        grad_own = (team_total(total, got) + grad_inner).astype(LOWER)
        swapped = swap_home(from_team_order(team, grad_own))
        near_att = jnp.concatenate([flow_qkv.send_near(), flow_out.send_near()], axis=1)
        (near_att,) = beside(team, [near_att])
        total_up = flow_up.total(
            near_up, [jnp.concatenate(both, axis=0) for both in zip(got_up_a, got_up_b)]
        )
        total_out = flow_out.total(near_att, got_out, 3)
        sums = add_ring(team, sums, "y")
        total_qkv = flow_qkv.total(near_att, got_qkv, 0)
        sums, swapped, total_up, total_out, total_qkv, *rest = fence(
            sums, swapped, total_up, total_out, total_qkv, *home_down, *out_two
        )
        home_down, out_two = rest[:members], rest[members:]
        (grad_down,) = home_join(team, home_down, [tall])
    with jax.named_scope("s12"):
        grad_tokens = join_cores(team, swapped)
        home_all = home_pieces(team, jnp.concatenate([total_up, total_qkv, total_out], axis=1))
        output = join_cores(team, dealt_out(team, dealing, out_two))
        sums = add_ring(team, sums, "h").reshape(-1)
        grad_up, grad_query, grad_key, grad_value, grad_out = home_join(
            team, home_all, [tall] + [wide] * 4
        )
    smalls = []
    first = 0
    for size in [width] * 6 + [b_query.shape[0], b_value.shape[0], b_up.shape[0]]:
        smalls.append(sums[first : first + size])
        first += size
    return (
        output,
        grad_tokens,
        grad_query,
        grad_key,
        grad_value,
        grad_out,
        smalls[6],
        smalls[7],
        smalls[0],
        smalls[1],
        smalls[2],
        grad_up,
        smalls[8],
        grad_down,
        smalls[3],
        smalls[4],
        smalls[5],
    )


def solution(mesh):
    fsdp, ctx, tp = (mesh.shape[name] for name in ("fsdp", "ctx", "tp"))
    fine = Mesh(mesh.devices.reshape(fsdp // 2, 2, 2, ctx // 2, tp), ROWS + ("tp",))
    rows, split = P(ROWS, None), P(ROWS, "tp")
    in_specs = (
        (rows, P(), P())
        + (split,) * 4
        + (P("tp"), P("tp"), P(), P(), P(), split, P("tp"), split, P(), P(), P(), rows)
    )
    out_specs = (
        (rows, rows)
        + (split,) * 4
        + (P("tp"), P("tp"), P(), P(), P(), split, P("tp"), split, P(), P(), P())
    )
    return jax.shard_map(local, mesh=fine, in_specs=in_specs, out_specs=out_specs, check_vma=False)
```

```python
import functools
import math

import jax
import jax.numpy as jnp
from jax import lax
from jax.experimental import pallas as pl
from jax.experimental.pallas import tpu as pltpu
from jax.sharding import Mesh
from jax.sharding import PartitionSpec as P

HEAD = 128
EPSILON = 1e-12
NEGATIVE = -1e30
WIDE = jnp.float32
LOWER = jnp.bfloat16

TEAM = ("l", "x")
ROWS = ("h", "l", "y", "x")


def dot(left, right, dims):
    return lax.dot_general(left, right, (dims, ((), ())), preferred_element_type=WIDE)


def mm(left, right):
    return dot(left, right, ((1,), (0,)))


def mm_nt(left, right):
    return dot(left, right, ((1,), (1,)))


def mm_tn(left, right):
    return dot(left, right, ((0,), (0,)))


def modulo(value, size):
    if isinstance(size, int) and size & (size - 1) == 0:
        return jnp.bitwise_and(value, size - 1)
    return lax.rem(value, size)


class Team:
    def __init__(self):
        self.sizes = {name: lax.axis_size(name) for name in ROWS + ("tp",)}
        self.at = {name: lax.axis_index(name) for name in ROWS + ("tp",)}
        ls, xs = self.sizes["l"], self.sizes["x"]
        self.offsets = [(dl, dx) for dl in range(ls) for dx in range(xs)]
        self.members = ls * xs

    def shift(self, value, offset, back=False):
        with jax.named_scope("team%d%d" % offset):
            return self.shift_(value, offset, back)

    def shift_(self, value, offset, back):
        ls, xs = self.sizes["l"], self.sizes["x"]
        dl, dx = offset
        if back:
            dl, dx = -dl, -dx
        perm = [
            (l * xs + x, ((l + dl) % ls) * xs + (x + dx) % xs) for l in range(ls) for x in range(xs)
        ]
        return lax.ppermute(value, TEAM, perm)

    def ring(self, value, name, step):
        size = self.sizes[name]
        with jax.named_scope("ring_" + name):
            return lax.ppermute(value, name, [(i, (i + step) % size) for i in range(size)])

    def slot(self, offset, back=True):
        return self.slots[back][self.offsets.index(offset)]

    def plan(self, dealing, home):
        hs, h, l, y = self.sizes["h"], self.at["h"], self.at["l"], self.at["y"]
        own = pick(home, h * 2 + y)
        needs = [
            modulo(pick(home, modulo(h + step, hs) * 2 + y), 2) == y for step in range(hs)
        ]
        sources = [pick(dealing, h * 2 + target) for target in (y, 1 - y)]
        steps = [modulo(h - lax.shift_right_logical(source, 1) + hs, hs) for source in sources]
        here = pick(dealing, h * 2 + l)
        return (
            [self.slot_(offset, back) for back in (False, True) for offset in self.offsets]
            + [l == y, modulo(h - lax.shift_right_logical(own, 1) + hs, hs), modulo(here, 2) == l]
            + steps
            + needs
        )

    def set_plan(self, plan):
        self.slots = {False: plan[: self.members], True: plan[self.members : 2 * self.members]}
        rest = plan[2 * self.members :]
        self.same, self.in_step, self.out_first = rest[:3]
        self.out_steps, self.needs = rest[3:5], rest[5:]

    def slot_(self, offset, back):
        ls, xs = self.sizes["l"], self.sizes["x"]
        dl, dx = offset
        if back:
            dl, dx = -dl, -dx
        return modulo(self.at["l"] + dl + ls, ls) * xs + modulo(self.at["x"] + dx + xs, xs)


def fence(*values):
    return lax.optimization_barrier(values)


def swap_home(value):
    return lax.ppermute(value, ("l", "y"), [(1, 2), (2, 1)])


def swapped_home(team, value, moved):
    return jnp.where(team.same, value, moved)


def team_pieces(team, piece):
    far = team.shift(piece, (1, 0))
    across_x = [(0, dx) for dx in range(1, team.sizes["x"])]
    return (
        [piece]
        + [team.shift(piece, offset) for offset in across_x]
        + [far]
        + [team.shift(far, offset) for offset in across_x]
    )


def cores(team, value):
    return [team.ring(value, "tp", step) for step in range(1, team.sizes["tp"])]


def row_blocks(team):
    ts = team.sizes["tp"]
    return [
        team.slot(offset) * ts + modulo(team.at["tp"] - step + ts, ts)
        for step in range(ts)
        for offset in team.offsets
    ]


def core_send(team, rows, pieces, half_rows, *others):
    sent = [spread(rows, step, pieces, half_rows) for step in range(1, team.sizes["tp"])]
    sent = fence(*sent, *others)[: len(sent)]
    return [team.ring(value, "tp", -step) for step, value in enumerate(sent, 1)]


def core_total(team, rows, pieces, half_rows, got):
    total, *sent = spread(rows, 0, pieces, half_rows, got, team.members)
    return total, sent


def team_send_direct(team, sent):
    return [
        team.shift(value, offset, back=True) for value, offset in zip(sent, team.offsets[1:])
    ]


def team_send(team, sent):
    xs = team.sizes["x"]
    across_x = [(0, dx) for dx in range(1, xs)]
    far = sent[xs - 1].astype(WIDE)
    for value, offset in zip(sent[xs:], across_x):
        far = far + team.shift(value, offset, back=True).astype(WIDE)
    got = [team.shift(value, offset, back=True) for value, offset in zip(sent, across_x)]
    return got + [team.shift(far.astype(LOWER), (1, 0), back=True)]


def team_total(own, got):
    for value in got:
        own = own + value.astype(WIDE)
    return own


def put(buffer, value, starts):
    return lax.dynamic_update_slice(buffer, value, starts)


def share_columns(team, shards):
    widths = [shard.shape[1] // team.members for shard in shards]
    pieces = []
    for j, offset in enumerate(team.offsets):
        slot = team.slot(offset, back=False)
        cuts = [
            lax.dynamic_slice_in_dim(shard, slot * each, each, 1)
            for shard, each in zip(shards, widths)
        ]
        piece = jnp.concatenate(cuts, axis=1)
        pieces.append(team.shift(piece, offset) if j > 0 else piece)
    return pieces


def place_rows_kernel(widths, slots_ref, *refs):
    pieces, outs = refs[: len(refs) - len(widths)], refs[len(refs) - len(widths) :]
    for j, piece in enumerate(pieces):
        height = piece.shape[0]
        row = pl.multiple_of(slots_ref[j] * height, height)
        first = 0
        for out, width in zip(outs, widths):
            out[pl.ds(row, height), :] = piece[:, first : first + width]
            first += width


def place_columns_kernel(widths, slots_ref, *refs):
    pieces, outs = refs[: len(refs) - len(widths)], refs[len(refs) - len(widths) :]
    for j, piece in enumerate(pieces):
        first = 0
        for out, width in zip(outs, widths):
            column = pl.multiple_of(slots_ref[j] * width, width)
            block = piece[:, first : first + width].astype(out.dtype)
            out[:, pl.ds(column, width)] = block
            first += width


def place(team, kernel, pieces, widths, shapes):
    slots = jnp.stack([team.slot(offset) for offset in team.offsets]).astype(jnp.int32)
    whole = [pl.BlockSpec(piece.shape, lambda n: (0, 0)) for piece in pieces]
    return pl.pallas_call(
        kernel if widths is None else functools.partial(kernel, widths),
        grid=(1,),
        in_specs=[pl.BlockSpec(memory_space=pltpu.SMEM)] + whole,
        out_specs=[pl.BlockSpec(shape.shape, lambda n: (0, 0)) for shape in shapes],
        out_shape=shapes,
        cost_estimate=LIGHT,
        compiler_params=KERNEL,
    )(slots, *pieces)


def stack_rows_kernel(*refs):
    height = refs[0].shape[0]
    for j, piece in enumerate(refs[:-1]):
        refs[-1][j * height : (j + 1) * height, :] = piece[...]


def stack_rows(pieces):
    height, width = pieces[0].shape
    rows = height * len(pieces)
    return pl.pallas_call(
        stack_rows_kernel,
        grid=(1,),
        in_specs=[pl.BlockSpec((height, width), lambda n: (0, 0)) for _ in pieces],
        out_specs=pl.BlockSpec((rows, width), lambda n: (0, 0)),
        out_shape=jax.ShapeDtypeStruct((rows, width), pieces[0].dtype),
        cost_estimate=LIGHT,
        compiler_params=KERNEL,
    )(*pieces)


def place_halves_kernel(slots_ref, *refs):
    pieces, outs = refs[:-2], refs[-2:]
    split = len(pieces) // 2
    for j, piece in enumerate(pieces):
        height = piece.shape[0]
        for part, out in enumerate(outs):

            @pl.when(lax.div(slots_ref[j], split) == part)
            def _():
                row = pl.multiple_of(lax.rem(slots_ref[j], split) * height, height)
                out[pl.ds(row, height), :] = piece[...]


def near_rows(team, pieces, parts=1):
    height, width = pieces[0].shape
    shape = jax.ShapeDtypeStruct((height * team.members // parts, width), LOWER)
    if parts == 1:
        return place(team, place_rows_kernel, pieces, [width], [shape])
    return place(team, place_halves_kernel, pieces, None, [shape] * 2)


def across(team, value):
    return [team.ring(value, "h", -step) for step in range(1, team.sizes["h"])]


def beside(team, values):
    return [team.ring(value, "y", 1) for value in values]


def halves(value):
    middle = value.shape[0] // 2
    return value[:middle], value[middle:]


def pairs(firsts, seconds):
    return [part for pair in zip(firsts, seconds) for part in pair]


def add_ring(team, value, name):
    return value + sum(team.ring(value, name, step) for step in range(1, team.sizes[name]))


class Grads:
    def __init__(self, team, lefts, rights):
        self.team, self.lefts, self.rights = team, lefts, rights
        self.far = lefts[0].shape[1] // 2
        self.near = self.far // team.sizes["h"]

        self.half = self.near // 2
        self.steps = range(1, team.sizes["h"])

    def rows(self, first, count, adds=(), offset=0, column=0):
        return outer(self.lefts, self.rights, first, count, adds, offset, column)

    def send_far(self):
        return self.rows(self.far + self.near, self.far - self.near)

    def send_half(self, part):
        start = self.far + part * self.half
        return [self.rows(start + step * self.near, self.half) for step in self.steps]

    def send_near(self):
        return self.rows(self.far, self.near)

    def cross(self, got):
        offsets = [(step - 1) * self.near for step in self.steps]
        return [self.rows(self.near + first, self.near, [got], first) for first in offsets]

    def cross_half(self, part, got):
        offsets = [(step - 1) * self.near + part * self.half for step in self.steps]
        return [self.rows(self.near + first, self.half, [got], first) for first in offsets]

    def cross_halves(self, part, gots):
        start = part * self.half
        return [
            self.rows(start + step * self.near, self.half, [got])
            for step, got in zip(self.steps, gots)
        ]

    def go(self, sent):
        return [self.team.ring(value, "h", step) for step, value in zip(self.steps, sent)]

    def total(self, got, crossed, column=0):
        return self.rows(0, self.near, [got, *crossed], column=column)


def home_pieces(team, total):
    height = total.shape[0] // team.members
    total = total.reshape(team.members, height, -1)
    pieces = []
    for j, offset in enumerate(team.offsets):
        piece = lax.dynamic_index_in_dim(total, team.slot(offset, back=False), 0, False)
        pieces.append(team.shift(piece, offset) if j > 0 else piece)
    return pieces


def home_join(team, pieces, widths):
    height = pieces[0].shape[0]
    shapes = [jax.ShapeDtypeStruct((height, width * team.members), WIDE) for width in widths]
    return place(team, place_columns_kernel, pieces, widths, shapes)


def permute_kernel(count, table_ref, value_ref, out_ref):
    block = value_ref.shape[1] // count
    for i in range(count):
        column = pl.multiple_of(table_ref[i] * block, block)
        out_ref[:, i * block : (i + 1) * block] = value_ref[:, pl.ds(column, block)]


def permute_columns(value, table):
    whole = pl.BlockSpec(value.shape, lambda n: (0, 0))
    return pl.pallas_call(
        functools.partial(permute_kernel, len(table)),
        grid=(1,),
        in_specs=[pl.BlockSpec(memory_space=pltpu.SMEM), whole],
        out_specs=whole,
        out_shape=jax.ShapeDtypeStruct(value.shape, value.dtype),
        cost_estimate=LIGHT,
    )(jnp.stack(table).astype(jnp.int32), value)


def to_team_order(team, value):
    hs = team.sizes["h"]
    table = []
    for dy in range(2):
        for dh in range(hs):
            for l in range(2):
                h, y = modulo(team.at["h"] + dh, hs), modulo(team.at["y"] + dy, 2)
                table.append((h * 2 + l) * 2 + y)
    return permute_columns(value, table)


def from_team_order(team, value):
    hs = team.sizes["h"]
    table = []
    for h in range(hs):
        for l in range(2):
            for y in range(2):
                dh, dy = modulo(h - team.at["h"] + hs, hs), modulo(y - team.at["y"] + 2, 2)
                table.append((dy * hs + dh) * 2 + l)
    return permute_columns(value, table)


def pick(table, index):
    ids = jnp.arange(table.shape[0], dtype=jnp.int32)
    return jnp.sum(jnp.where(ids == index, table, 0))


def choose(pieces, index):
    out = pieces[0]
    for i in range(1, len(pieces)):
        out = jnp.where(index == i, pieces[i], out)
    return out


def spread_h(team, piece):
    return [piece] + [team.ring(piece, "h", step) for step in range(1, team.sizes["h"])]


def deal_flip(team, piece, flip):
    if flip == 0:
        return swap_home(piece)
    perm = [(l * 2 + y, y * 2 + 1 - l) for l in range(2) for y in range(2)]
    with jax.named_scope("flip"):
        return lax.ppermute(piece, ("l", "y"), perm)


def deal_across(team, two):
    first = swapped_home(team, two[0], two[1])
    chosen = [jnp.where(need, first, two[2]) for need in team.needs]
    return chosen[:1] + [team.ring(value, "h", step) for step, value in enumerate(chosen) if step]


def dealt_in(team, pieces):
    return choose(pieces, team.in_step)


def deal(team, pieces):
    first, second = (choose(pieces, step) for step in team.out_steps)
    perm = [(l * 2 + y, (1 - y) * 2 + l) for l in range(2) for y in range(2)]
    return [first, swap_home(first), lax.ppermute(second, ("l", "y"), perm)]


def dealt_out(team, got):
    return jnp.where(team.out_first, swapped_home(team, got[0], got[1]), got[2])


def join_cores(team, piece):
    ts = team.sizes["tp"]
    out = jnp.zeros((ts,) + piece.shape, piece.dtype)
    for step in range(ts):
        other = team.ring(piece, "tp", step) if step else piece
        out = put(out, other[None], (modulo(team.at["tp"] - step + ts, ts), 0, 0))
    return out.reshape(-1, piece.shape[-1])


def layer_norm(inputs, gain_vec, shift_vec):
    row_mean = jnp.mean(inputs, axis=-1, keepdims=True)
    centred = inputs - row_mean
    spread = jnp.mean(centred * centred, axis=-1, keepdims=True)
    rate = lax.rsqrt(spread + EPSILON)
    xhat = centred * rate
    return xhat * gain_vec + shift_vec, xhat, rate


def layer_norm_back(grad, gain_vec, xhat, rate):
    scaled = grad * gain_vec
    return rate * (
        scaled
        - jnp.mean(scaled, axis=-1, keepdims=True)
        - xhat * jnp.mean(scaled * xhat, axis=-1, keepdims=True)
    )


def gelu_tanh(inputs):
    return jax.nn.gelu(inputs, approximate=True)


def masked_scores(key_ref, query, limits_ref, scale):
    count = limits_ref.shape[0]
    height = key_ref.shape[0] // count
    blocks = []
    for j in range(count):
        block = mm_nt(key_ref[j * height : (j + 1) * height, :], query) * scale
        row = lax.broadcasted_iota(jnp.int32, block.shape, 0)
        blocks.append(jnp.where(row < limits_ref[j], block, NEGATIVE))
    return blocks


def attend_kernel(scale, limits_ref, query_ref, key_ref, value_ref, out_ref, log_ref):
    blocks = masked_scores(key_ref, query_ref[...], limits_ref, scale)
    row_max = functools.reduce(jnp.maximum, blocks)
    row_max = jnp.max(row_max, axis=0, keepdims=True)
    blocks = [jnp.exp(block - row_max) for block in blocks]
    total = jnp.sum(functools.reduce(jnp.add, blocks), axis=0, keepdims=True)
    inverse = 1.0 / total
    height = key_ref.shape[0] // len(blocks)
    out = None
    for j, block in enumerate(blocks):
        value = value_ref[j * height : (j + 1) * height, :]
        term = mm_tn(value, (block * inverse).astype(LOWER))
        out = term if out is None else out + term
    out_ref[...] = out.T.astype(LOWER)
    log_ref[0] = row_max + jnp.log(total)


def attend_back_kernel(
    scale, wide, limits_ref, query_ref, key_ref, value_ref, grad_ref, log_ref, out_ref, key_sum, value_sum
):
    head, step = pl.program_id(0), pl.program_id(1)
    query, grad = query_ref[...], grad_ref[...]
    blocks = masked_scores(key_ref, query, limits_ref, scale)
    count = len(blocks)
    height = key_ref.shape[0] // count
    part = [slice(j * height, (j + 1) * height) for j in range(count)]
    log_sum = log_ref[0]
    probs = [jnp.exp(block - log_sum) for block in blocks]
    grad_probs = [mm_nt(value_ref[rows, :], grad) for rows in part]
    delta = functools.reduce(jnp.add, [p * g for p, g in zip(probs, grad_probs)])
    delta = jnp.sum(delta, axis=0, keepdims=True)

    @pl.when(step == 0)
    def _():
        key_sum[...] = jnp.zeros_like(key_sum)
        value_sum[...] = jnp.zeros_like(value_sum)

    grad_query = None
    for j, rows in enumerate(part):
        scores = (probs[j] * (grad_probs[j] - delta)).astype(LOWER)
        term = mm_tn(key_ref[rows, :], scores)
        grad_query = term if grad_query is None else grad_query + term
        key_sum[rows, :] += mm(scores, query)
        value_sum[rows, :] += mm(probs[j].astype(LOWER), grad)
    count = query.shape[0]
    first = pl.multiple_of(step * count, count)
    column = pl.multiple_of(head * HEAD, HEAD)
    out_ref[pl.ds(first, count), pl.ds(column, HEAD)] = (grad_query.T * scale).astype(LOWER)

    @pl.when(step == pl.num_programs(1) - 1)
    def _():
        out_ref[:, pl.ds(wide + column, HEAD)] = (key_sum[...] * scale).astype(LOWER)
        out_ref[:, pl.ds(2 * wide + column, HEAD)] = value_sum[...].astype(LOWER)


LIGHT = pl.CostEstimate(flops=1000000, bytes_accessed=100000, transcendentals=0)
KERNEL = pltpu.CompilerParams(vmem_limit_bytes=24 * 1024 * 1024)


def gelu_slope(value):
    inner = math.sqrt(2.0 / math.pi)
    square = value * value
    tanh = jnp.tanh(inner * value * (1.0 + 0.044715 * square))
    return 0.5 * (1.0 + tanh) + 0.5 * value * (1.0 - tanh * tanh) * inner * (
        1.0 + 3.0 * 0.044715 * square
    )


def project_kernel(mode, part_count, piece_count, steps, *refs):
    parts, pieces = refs[:part_count], refs[part_count : part_count + piece_count]
    rest = refs[part_count + piece_count :]
    index = pl.program_id(0)

    def run(rows):
        total = None
        first = 0
        for piece in pieces:
            depth = piece.shape[0]
            term = mm(rows[:, first : first + depth], piece[...])
            total = term if total is None else total + term
            first += depth
        if mode == "bias":
            rest[1][...] = (total + rest[0][...]).astype(LOWER)
        elif mode == "gelu":
            total = total + rest[0][...]
            rest[1][...] = total
            rest[2][...] = gelu_tanh(total).astype(LOWER)
        elif mode == "slope":
            rest[1][...] = (total * gelu_slope(rest[0][...])).astype(LOWER)
        else:
            rest[0][...] = total.astype(LOWER)

    for place in range(part_count):

        @pl.when(index // steps == place)
        def _():
            run(parts[place][...])


def project(mode, parts, pieces, width, extra=None):
    half_rows, depth = parts[0].shape
    block = min(256, half_rows)
    steps = half_rows // block
    rows = half_rows * len(parts)

    def part_at(place):
        return lambda i: (jnp.clip(i - place * steps, 0, steps - 1), 0)

    in_specs = [pl.BlockSpec((block, depth), part_at(place)) for place in range(len(parts))]
    for array, column in pieces:
        in_specs.append(
            pl.BlockSpec((array.shape[0], width), functools.partial(lambda c, i: (0, c), column))
        )
    arrays = list(parts) + [array for array, _ in pieces]
    tile = pl.BlockSpec((block, width), lambda i: (i, 0))
    if mode in ("bias", "gelu"):
        in_specs.append(pl.BlockSpec((1, width), lambda i: (0, 0)))
        arrays.append(extra[None])
    elif mode == "slope":
        in_specs.append(tile)
        arrays.append(extra)
    shapes = [jax.ShapeDtypeStruct((rows, width), LOWER)]
    if mode == "gelu":
        shapes = [jax.ShapeDtypeStruct((rows, width), WIDE)] + shapes
    return pl.pallas_call(
        functools.partial(project_kernel, mode, len(parts), len(pieces), steps),
        grid=(len(parts) * steps,),
        in_specs=in_specs,
        out_specs=[tile] * len(shapes),
        out_shape=shapes,
        cost_estimate=LIGHT,
        compiler_params=KERNEL,
    )(*arrays)


def spread_kernel(piece_count, got_count, members, rows_ref, *refs):
    pieces, gots = refs[:piece_count], refs[piece_count : piece_count + got_count]
    outs = refs[piece_count + got_count :]
    rows = rows_ref[...]
    height = rows.shape[0] // members
    first = 0
    for piece in pieces:
        columns = slice(first, first + piece.shape[0])
        total = mm_nt(rows, piece[...])
        for got in gots:
            total = total + got[:, columns].astype(WIDE)
        for j, out in enumerate(outs):
            out[:, columns] = total[j * height : (j + 1) * height].astype(out.dtype)
        first += piece.shape[0]


def spread(rows, place, pieces, half_rows, got=(), members=0):
    if isinstance(rows, (list, tuple)):
        rows, place = rows[place], 0
    depth = rows.shape[1]
    width = sum(array.shape[0] for array, _ in pieces)
    in_specs = [pl.BlockSpec((half_rows, depth), lambda n: (place, 0))]
    for array, column in pieces:
        in_specs.append(
            pl.BlockSpec((array.shape[0], depth), functools.partial(lambda c, n: (0, c), column))
        )
    in_specs += [pl.BlockSpec((half_rows, width), lambda n: (0, 0))] * len(got)
    split = max(members, 1)
    height = half_rows // split
    dtypes = [WIDE] + [LOWER] * (members - 1) if members else [LOWER]
    out = pl.pallas_call(
        functools.partial(spread_kernel, len(pieces), len(got), split),
        grid=(1,),
        in_specs=in_specs,
        out_specs=[pl.BlockSpec((height, width), lambda n: (0, 0))] * split,
        out_shape=[jax.ShapeDtypeStruct((height, width), dtype) for dtype in dtypes],
        cost_estimate=LIGHT,
        compiler_params=KERNEL,
    )(rows, *[array for array, _ in pieces], *got)
    return out if members else out[0]


def outer_kernel(part_count, add_count, *refs):
    lefts, rights = refs[:part_count], refs[part_count : 2 * part_count]
    adds, out = refs[2 * part_count : 2 * part_count + add_count], refs[-1]
    total = None
    for left, right in zip(lefts, rights):
        term = mm_tn(left[...], right[...])
        total = term if total is None else total + term
    for add in adds:
        total = total + add[...].astype(WIDE)
    out[...] = total.astype(out.dtype)


def outer(lefts, rights, first, count, adds, offset, column):
    height = lefts[0].shape[0]
    rights = [right if isinstance(right, tuple) else (right, 0) for right in rights]
    width = rights[0][0].shape[1]
    block = math.gcd(256, count)
    in_specs = [pl.BlockSpec((height, block), lambda i: (0, first // block + i)) for _ in lefts]
    for _, row in rights:
        in_specs.append(
            pl.BlockSpec((height, width), functools.partial(lambda r, i: (r, 0), row))
        )
    tile = pl.BlockSpec((block, width), lambda i: (i, 0))
    add_tile = pl.BlockSpec((block, width), lambda i: (offset // block + i, 0))
    first_tile = pl.BlockSpec((block, width), lambda i: (offset // block + i, column))
    return pl.pallas_call(
        functools.partial(outer_kernel, len(lefts), len(adds)),
        grid=(count // block,),
        in_specs=in_specs + [first_tile] * len(adds[:1]) + [add_tile] * len(adds[1:]),
        out_specs=tile,
        out_shape=jax.ShapeDtypeStruct((count, width), LOWER),
        cost_estimate=LIGHT,
        compiler_params=KERNEL,
    )(*lefts, *[right for right, _ in rights], *adds)


def query_block(rows):
    return min(256, rows)


def attend(qkv, limits, scale):
    rows, wide = qkv.shape[0], qkv.shape[1] // 3
    heads, block = wide // HEAD, query_block(rows)
    return pl.pallas_call(
        functools.partial(attend_kernel, scale),
        grid=(heads, rows // block),
        in_specs=[
            pl.BlockSpec(memory_space=pltpu.SMEM),
            pl.BlockSpec((block, HEAD), lambda h, i: (i, h)),
            pl.BlockSpec((rows, HEAD), lambda h, i: (0, heads + h)),
            pl.BlockSpec((rows, HEAD), lambda h, i: (0, 2 * heads + h)),
        ],
        out_specs=[
            pl.BlockSpec((block, HEAD), lambda h, i: (i, h)),
            pl.BlockSpec((1, 1, block), lambda h, i: (h, 0, i)),
        ],
        out_shape=[
            jax.ShapeDtypeStruct((rows, wide), LOWER),
            jax.ShapeDtypeStruct((heads, 1, rows), WIDE),
        ],
        cost_estimate=LIGHT,
        compiler_params=KERNEL,
    )(limits, qkv, qkv, qkv)


def attend_back(qkv, grad, log_sum, limits, scale):
    rows, wide = grad.shape
    heads, block = wide // HEAD, query_block(rows)
    return pl.pallas_call(
        functools.partial(attend_back_kernel, scale, wide),
        grid=(heads, rows // block),
        in_specs=[
            pl.BlockSpec(memory_space=pltpu.SMEM),
            pl.BlockSpec((block, HEAD), lambda h, i: (i, h)),
            pl.BlockSpec((rows, HEAD), lambda h, i: (0, heads + h)),
            pl.BlockSpec((rows, HEAD), lambda h, i: (0, 2 * heads + h)),
            pl.BlockSpec((block, HEAD), lambda h, i: (i, h)),
            pl.BlockSpec((1, 1, block), lambda h, i: (h, 0, i)),
        ],
        out_specs=pl.BlockSpec((rows, 3 * wide), lambda h, i: (0, 0)),
        out_shape=jax.ShapeDtypeStruct((rows, 3 * wide), LOWER),
        scratch_shapes=[pltpu.VMEM((rows, HEAD), WIDE), pltpu.VMEM((rows, HEAD), WIDE)],
        cost_estimate=LIGHT,
        compiler_params=KERNEL,
    )(limits, qkv, qkv, qkv, grad, log_sum)


def local(
    tokens,
    lengths,
    dealing,
    w_query,
    w_key,
    w_value,
    w_out,
    b_query,
    b_value,
    b_out,
    gain_mid,
    shift_mid,
    w_up,
    b_up,
    w_down,
    b_down,
    gain_end,
    shift_end,
    cotangent,
):
    team = Team()
    ts, members = team.sizes["tp"], team.members
    row_count = tokens.shape[0] // ts
    wide = w_query.shape[1] // members
    tall = w_up.shape[1] // members
    width = tokens.shape[1]
    score_scale = 1.0 / math.sqrt(HEAD)
    my_slot = team.at["l"] * team.sizes["x"] + team.at["x"]
    seq_ids = jnp.arange(dealing.shape[0], dtype=jnp.int32)
    home = jnp.sum(jnp.where(dealing[None, :] == seq_ids[:, None], seq_ids[None, :], 0), axis=1)
    plan = team.plan(dealing, home)
    team.set_plan(plan)
    live_count = pick(lengths, team.at["h"] * 2 + team.at["y"])
    limits = live_count - jnp.stack(row_blocks(team)).astype(jnp.int32) * row_count
    query_live = (jnp.arange(row_count, dtype=jnp.int32) < limits[0])[:, None]
    half_at = team.at["tp"] * row_count

    half_rows = members * row_count
    vectors = jnp.stack([b_out, gain_mid, shift_mid, b_down, gain_end, shift_end])
    b_out, gain_mid, shift_mid, b_down, gain_end, shift_end = to_team_order(team, vectors)
    bias_q = lax.dynamic_slice_in_dim(b_query, my_slot * wide, wide, 0)
    bias_v = lax.dynamic_slice_in_dim(b_value, my_slot * wide, wide, 0)
    bias_up = lax.dynamic_slice_in_dim(b_up, my_slot * tall, tall, 0)
    bias_qkv = jnp.concatenate([bias_q, jnp.zeros_like(bias_q), bias_v])
    steps = team.sizes["h"] - 1
    team_count = team.sizes["x"]


    def first_column(arrays):
        return [(array, 0) for array in arrays]

    with jax.named_scope("a0"):
        mine = lax.dynamic_slice_in_dim(tokens, half_at, row_count, 0)
        own = swap_home(mine)
        share = share_columns(team, [w_query, w_key, w_value, w_out])
        own, w_up, w_down, bias_qkv, bias_up, limits, query_live, *rest = fence(
            own, w_up, w_down, bias_qkv, bias_up, limits, query_live, *share, *plan
        )
        share, plan = rest[:members], rest[members:]
        team.set_plan(plan)
    with jax.named_scope("a1"):
        own = to_team_order(team, swapped_home(team, mine, own))
        (near_att,) = near_rows(team, share)
        pieces = team_pieces(team, own)
        cross_qkv = across(team, near_att[:, : 3 * wide])
        (side_att,) = beside(team, [near_att])
        near_att, w_up, w_down, cotangent, side_att, *rest = fence(
            near_att, w_up, w_down, cotangent, side_att, *pieces, *cross_qkv
        )
        pieces, cross_qkv = rest[:members], rest[members:]
    with jax.named_scope("a2"):
        half = stack_rows(pieces)
        other = cores(team, half)
        far_qkv = beside(team, cross_qkv)
        cross_out = across(team, near_att[:, 3 * wide :])
        share = share_columns(team, [w_up])
        cotangent, w_down, *rest = fence(
            cotangent, w_down, half, *other, *share, *far_qkv, *cross_out
        )
        in_parts = rest[:ts]
        share, rest = rest[ts : ts + members], rest[ts + members :]
        far_qkv, cross_out = rest[:steps], rest[steps:]
    qkv_mat = first_column([near_att, *cross_qkv, side_att, *far_qkv])
    with jax.named_scope("c1"):
        up_a, up_b = near_rows(team, share, 2)
        cross_up_a = across(team, up_a)
        far_out = beside(team, cross_out)
        cot_half = lax.dynamic_slice_in_dim(cotangent, half_at, row_count, 0)
        share = share_columns(team, [w_down])
        (qkv,) = project("bias", in_parts, qkv_mat, 3 * wide, bias_qkv)
        attended, log_sum = attend(qkv, limits, score_scale)
        out_mat = [(near_att, 3), *first_column(cross_out), (side_att, 3), *first_column(far_out)]
        got = core_send(team, attended, out_mat, half_rows, *cross_up_a, *share)
        total, sent = core_total(team, attended, out_mat, half_rows, got)
        up_a, up_b, cot_half, *rest = fence(
            up_a, up_b, cot_half, *cross_up_a, *share, *sent
        )
        cross_up_a, rest = rest[:steps], rest[steps:]
        share, sent = rest[:members], rest[members:]
    with jax.named_scope("s3"):
        got = team_send(team, sent)
        cross_up_b = across(team, up_b)
        down_a, down_b = near_rows(team, share, 2)
        side = beside(team, [jnp.concatenate([up_a, *cross_up_a], axis=0)])
        cot_one = deal_flip(team, cot_half, 0)
        cot_half, cot_one, up_b, down_a, down_b, *rest = fence(
            cot_half, cot_one, up_b, down_a, down_b, *got, *cross_up_b, *side
        )
        got, rest = rest[:team_count], rest[team_count:]
        cross_up_b, side_a = rest[:steps], rest[steps]
    with jax.named_scope("s4"):
        branch = team_total(total, got) + b_out
        middle, mid_hat, mid_rate = layer_norm(own.astype(WIDE) + branch, gain_mid, shift_mid)
        pieces = team_pieces(team, middle.astype(LOWER))
        cross_down_a = across(team, down_a)
        side = beside(team, [jnp.concatenate([up_b, *cross_up_b], axis=0)])
        cot_two = [cot_half, cot_one, deal_flip(team, cot_half, 1)]
        down_a, down_b, *rest = fence(
            down_a, down_b, *cot_two, *pieces, *cross_down_a, *side
        )
        cot_two, rest = rest[:3], rest[3:]
        pieces, rest = rest[:members], rest[members:]
        cross_down_a, side_b = rest[:steps], rest[steps]
    part_rows = down_a.shape[0]

    def split_side(side):
        blocks = [side[k * part_rows : (k + 1) * part_rows] for k in range(steps + 1)]
        return blocks[0], blocks[1:]

    side_up_a, far_up_a = split_side(side_a)
    side_up_b, far_up_b = split_side(side_b)
    up_mat = first_column(
        [up_a, up_b]
        + pairs(cross_up_a, cross_up_b)
        + [side_up_a, side_up_b]
        + pairs(far_up_a, far_up_b)
    )
    with jax.named_scope("c2"):
        half = stack_rows(pieces)
        other = cores(team, half)
        cross_down_b = across(team, down_b)
        side = beside(team, [jnp.concatenate([down_a, *cross_down_a], axis=0)])
        mid_parts = [half] + other
        hidden, active = [], []
        for part in mid_parts:
            hidden_part, active_part = project("gelu", [part], up_mat, tall, bias_up)
            hidden.append(hidden_part)
            active.append(active_part)
        down_b, *rest = fence(down_b, *active, *cross_down_b, *side, *cot_two)
        active, rest = rest[:ts], rest[ts:]
        cross_down_b, side, cot_two = rest[:steps], rest[steps], rest[steps + 1 :]
        side_down_a, far_down_a = split_side(side)
    with jax.named_scope("s5"):
        (side,) = beside(team, [jnp.concatenate([down_b, *cross_down_b], axis=0)])
        side_down_b, far_down_b = split_side(side)
        cot_pieces = deal_across(team, cot_two)
        down_mat = first_column(
            [down_a, down_b]
            + pairs(cross_down_a, cross_down_b)
            + [side_down_a, side_down_b]
            + pairs(far_down_a, far_down_b)
        )
        got = core_send(team, active, down_mat, half_rows, *cot_pieces)
        total, sent = core_total(team, active, down_mat, half_rows, got)
        rest = fence(*sent, *cot_pieces)
        sent, cot_pieces = rest[: members - 1], rest[members - 1 :]
    with jax.named_scope("s6"):
        cot = to_team_order(team, dealt_in(team, cot_pieces))
        cot, *got = fence(cot, *team_send_direct(team, sent))
    with jax.named_scope("s7"):
        result = team_total(total, got) + b_down
        normed, end_hat, end_rate = layer_norm(middle + result, gain_end, shift_end)
        output_own = jnp.where(query_live, normed, 0.0).astype(LOWER)
        grad_normed = jnp.where(query_live, cot.astype(WIDE), 0.0)
        grad_sum = layer_norm_back(grad_normed, gain_end, end_hat, end_rate)
        grad_result = grad_sum.astype(LOWER)
        pieces = team_pieces(team, grad_result)
        out_pieces = spread_h(team, from_team_order(team, output_own))
        rest = fence(*pieces, *out_pieces)
        pieces, out_pieces = rest[:members], rest[members:]
        grad_gend = jnp.sum(grad_normed * end_hat, axis=0)
        grad_send = jnp.sum(grad_normed, axis=0)
        grad_bdown = jnp.sum(grad_result.astype(WIDE), axis=0)
    with jax.named_scope("c3"):
        half = stack_rows(pieces)
        other = cores(team, half)
        result_parts = [half] + other
        flow_down = Grads(team, result_parts, active)
        far_down_a = beside(team, flow_down.send_half(0))
        grad_hidden = []
        for part, hidden_part in zip(result_parts, hidden):
            grad_hidden += project("slope", [part], down_mat, tall, hidden_part)
        got = core_send(team, grad_hidden, up_mat, half_rows, *far_down_a, *grad_hidden)
        total, sent = core_total(team, grad_hidden, up_mat, half_rows, got)
        cross_down = flow_down.cross_halves(0, far_down_a)
        flow_up = Grads(team, mid_parts, grad_hidden)
        rest = fence(*sent, *cross_down)
        sent, cross_down = rest[: members - 1], rest[members - 1 :]
    with jax.named_scope("s8"):
        got = team_send(team, sent)
        got_down_a = flow_down.go(cross_down)
        far_down_b = beside(team, flow_down.send_half(1))
        far_up, *far_down_b = fence(flow_up.send_far(), *far_down_b)
        (far_up,) = beside(team, [far_up])
        cross_down = flow_down.cross_halves(1, far_down_b)
        far_up, *rest = fence(far_up, *got, *got_down_a, *cross_down)
        got, rest = rest[:team_count], rest[team_count:]
        got_down_a, cross_down = rest[:steps], rest[steps:]
    with jax.named_scope("s9"):
        grad_middle = team_total(total, got) + grad_sum
        grad_inner = layer_norm_back(grad_middle, gain_mid, mid_hat, mid_rate)
        grad_branch = grad_inner.astype(LOWER)
        pieces = team_pieces(team, grad_branch)
        got_down_b = flow_down.go(cross_down)
        (near_down,) = beside(team, [flow_down.send_near()])
        grad_gmid = jnp.sum(grad_middle * mid_hat, axis=0)
        grad_smid = jnp.sum(grad_middle, axis=0)
        grad_bout = jnp.sum(grad_branch.astype(WIDE), axis=0)
        by_row = jnp.stack([grad_bout, grad_gmid, grad_smid, grad_bdown, grad_gend, grad_send])
        by_row = add_ring(team, from_team_order(team, by_row), "tp")
        cross_up_a, cross_up_b = flow_up.cross_half(0, far_up), flow_up.cross_half(1, far_up)
        by_row, near_down, *rest = fence(by_row, near_down, *pieces, *got_down_b, *cross_up_a, *cross_up_b)
        pieces, rest = rest[:members], rest[members:]
        got_down_b, rest = rest[:steps], rest[steps:]
        cross_up_a, cross_up_b = rest[:steps], rest[steps:]
    with jax.named_scope("c4"):
        half = stack_rows(pieces)
        other = cores(team, half)
        got_up_a, got_up_b = flow_up.go(cross_up_a), flow_up.go(cross_up_b)
        out_two = deal(team, out_pieces)
        branch_parts = [half] + other
        attended_parts = [(attended, k) for k in range(ts)]
        flow_out = Grads(team, branch_parts, attended_parts)
        (far_out,) = beside(team, [flow_out.send_far()])
        (grad_attended,) = project("plain", branch_parts, out_mat, wide)
        grad_qkv = attend_back(qkv, grad_attended, log_sum, limits, score_scale)
        got = core_send(team, grad_qkv, qkv_mat, half_rows, far_out, *got_up_a, *out_two)
        total, sent = core_total(team, grad_qkv, qkv_mat, half_rows, got)
        grad_parts = [(grad_qkv, k) for k in range(ts)]
        flow_qkv = Grads(team, in_parts, grad_parts)
        qkv_sum = jnp.sum(grad_qkv.astype(WIDE), axis=0)
        grad_bup = sum(jnp.sum(part.astype(WIDE), axis=0) for part in grad_hidden)
        zeros = jnp.zeros((members, 1), WIDE)
        by_slot = [
            put(zeros * part[None], part[None], (my_slot, 0)).reshape(-1)
            for part in (qkv_sum[:wide], qkv_sum[2 * wide :], grad_bup)
        ]
        sums = jnp.concatenate([by_row.reshape(-1)] + by_slot).reshape(-1, 128)
        sums = add_ring(team, sums, "x")
        (far_qkv,) = beside(team, [flow_qkv.send_far()])
        cross_out = flow_out.cross(far_out)
        sums, near_down, far_qkv, *rest = fence(
            sums, near_down, far_qkv, *cross_out, *sent, *got_up_a, *got_up_b, *out_two
        )
        cross_out, rest = rest[:steps], rest[steps:]
        sent, rest = rest[: members - 1], rest[members - 1 :]
        got_up_a, got_up_b, out_two = rest[:steps], rest[steps : 2 * steps], rest[2 * steps :]
    with jax.named_scope("s10"):
        got = team_send(team, sent)
        total_down = flow_down.total(
            near_down,
            [jnp.concatenate(both, axis=0) for both in zip(got_down_a, got_down_b)],
        )
        got_qkv = flow_qkv.go(flow_qkv.cross(far_qkv))
        (near_up,) = beside(team, [flow_up.send_near()])
        sums = add_ring(team, sums, "l")
        sums, total_down, near_up, *rest = fence(
            sums, total_down, near_up, *out_two, *got, *got_qkv, *cross_out
        )
        out_two, rest = rest[:3], rest[3:]
        got, rest = rest[:team_count], rest[team_count:]
        got_qkv, cross_out = rest[:steps], rest[steps:]
    with jax.named_scope("s11"):
        got_out = flow_out.go(cross_out)
        home_down = home_pieces(team, total_down)
        grad_own = (team_total(total, got) + grad_inner).astype(LOWER)
        grad_own = from_team_order(team, grad_own)
        swapped = swap_home(grad_own)
        near_att = jnp.concatenate([flow_qkv.send_near(), flow_out.send_near()], axis=1)
        (near_att,) = beside(team, [near_att])
        total_up = flow_up.total(
            near_up, [jnp.concatenate(both, axis=0) for both in zip(got_up_a, got_up_b)]
        )
        total_out = flow_out.total(near_att, got_out, 3)
        total_qkv = flow_qkv.total(near_att, got_qkv, 0)
        sums, swapped, total_up, total_out, total_qkv, *rest = fence(
            sums, swapped, total_up, total_out, total_qkv, *home_down, *out_two
        )
        home_down, out_two = rest[:members], rest[members:]
        (grad_down,) = home_join(team, home_down, [tall])
    with jax.named_scope("s12"):
        grad_tokens = join_cores(team, swapped_home(team, grad_own, swapped))
        home_all = home_pieces(team, jnp.concatenate([total_up, total_qkv, total_out], axis=1))
        output = join_cores(team, dealt_out(team, out_two))
        sums = add_ring(team, add_ring(team, sums, "h"), "y").reshape(-1)
        grad_up, grad_query, grad_key, grad_value, grad_out = home_join(
            team, home_all, [tall] + [wide] * 4
        )
    smalls = []
    first = 0
    for size in [width] * 6 + [b_query.shape[0], b_value.shape[0], b_up.shape[0]]:
        smalls.append(sums[first : first + size])
        first += size
    return (
        output,
        grad_tokens,
        grad_query,
        grad_key,
        grad_value,
        grad_out,
        smalls[6],
        smalls[7],
        smalls[0],
        smalls[1],
        smalls[2],
        grad_up,
        smalls[8],
        grad_down,
        smalls[3],
        smalls[4],
        smalls[5],
    )


def solution(mesh):
    fsdp, ctx, tp = (mesh.shape[name] for name in ("fsdp", "ctx", "tp"))
    fine = Mesh(mesh.devices.reshape(fsdp // 2, 2, 2, ctx // 2, tp), ROWS + ("tp",))
    rows, split = P(ROWS, None), P(ROWS, "tp")
    in_specs = (
        (rows, P(), P())
        + (split,) * 4
        + (P("tp"), P("tp"), P(), P(), P(), split, P("tp"), split, P(), P(), P(), rows)
    )
    out_specs = (
        (rows, rows)
        + (split,) * 4
        + (P("tp"), P("tp"), P(), P(), P(), split, P("tp"), split, P(), P(), P())
    )
    return jax.shard_map(local, mesh=fine, in_specs=in_specs, out_specs=out_specs, check_vma=False)
```

```python
import functools
import math

import jax
import jax.numpy as jnp
from jax import lax
from jax.experimental import pallas as pl
from jax.experimental.pallas import tpu as pltpu
from jax.sharding import Mesh
from jax.sharding import PartitionSpec as P

HEAD = 128
EPSILON = 1e-12
NEGATIVE = -1e30
WIDE = jnp.float32
LOWER = jnp.bfloat16

TEAM = ("l", "x")
ROWS = ("h", "l", "y", "x")


def dot(left, right, dims):
    return lax.dot_general(left, right, (dims, ((), ())), preferred_element_type=WIDE)


def mm(left, right):
    return dot(left, right, ((1,), (0,)))


def mm_nt(left, right):
    return dot(left, right, ((1,), (1,)))


def mm_tn(left, right):
    return dot(left, right, ((0,), (0,)))


def modulo(value, size):
    if isinstance(size, int) and size & (size - 1) == 0:
        return jnp.bitwise_and(value, size - 1)
    return lax.rem(value, size)


class Team:
    def __init__(self):
        self.sizes = {name: lax.axis_size(name) for name in ROWS + ("tp",)}
        self.at = {name: lax.axis_index(name) for name in ROWS + ("tp",)}
        ls, xs = self.sizes["l"], self.sizes["x"]
        self.offsets = [(dl, dx) for dl in range(ls) for dx in range(xs)]
        self.members = ls * xs

    def shift(self, value, offset, back=False):
        with jax.named_scope("team%d%d" % offset):
            return self.shift_(value, offset, back)

    def shift_(self, value, offset, back):
        ls, xs = self.sizes["l"], self.sizes["x"]
        dl, dx = offset
        if back:
            dl, dx = -dl, -dx
        perm = [
            (l * xs + x, ((l + dl) % ls) * xs + (x + dx) % xs) for l in range(ls) for x in range(xs)
        ]
        return lax.ppermute(value, TEAM, perm)

    def ring(self, value, name, step):
        size = self.sizes[name]
        with jax.named_scope("ring_" + name):
            return lax.ppermute(value, name, [(i, (i + step) % size) for i in range(size)])

    def slot(self, offset, back=True):
        return self.slots[back][self.offsets.index(offset)]

    def plan(self, dealing, home):
        hs, h, l, y = self.sizes["h"], self.at["h"], self.at["l"], self.at["y"]
        own = pick(home, h * 2 + y)
        needs = [
            modulo(pick(home, modulo(h + step, hs) * 2 + y), 2) == y for step in range(hs)
        ]
        sources = [pick(dealing, h * 2 + target) for target in (y, 1 - y)]
        steps = [modulo(h - lax.shift_right_logical(source, 1) + hs, hs) for source in sources]
        here = pick(dealing, h * 2 + l)
        return (
            [self.slot_(offset, back) for back in (False, True) for offset in self.offsets]
            + [l == y, modulo(h - lax.shift_right_logical(own, 1) + hs, hs), modulo(here, 2) == l]
            + steps
            + needs
        )

    def set_plan(self, plan):
        self.slots = {False: plan[: self.members], True: plan[self.members : 2 * self.members]}
        rest = plan[2 * self.members :]
        self.same, self.in_step, self.out_first = rest[:3]
        self.out_steps, self.needs = rest[3:5], rest[5:]

    def slot_(self, offset, back):
        ls, xs = self.sizes["l"], self.sizes["x"]
        dl, dx = offset
        if back:
            dl, dx = -dl, -dx
        return modulo(self.at["l"] + dl + ls, ls) * xs + modulo(self.at["x"] + dx + xs, xs)


def fence(*values):
    return lax.optimization_barrier(values)


def swap_home(value):
    return lax.ppermute(value, ("l", "y"), [(1, 2), (2, 1)])


def swapped_home(team, value, moved):
    return jnp.where(team.same, value, moved)


def team_pieces(team, piece):
    far = team.shift(piece, (1, 0))
    across_x = [(0, dx) for dx in range(1, team.sizes["x"])]
    return (
        [piece]
        + [team.shift(piece, offset) for offset in across_x]
        + [far]
        + [team.shift(far, offset) for offset in across_x]
    )


def cores(team, value):
    return [team.ring(value, "tp", step) for step in range(1, team.sizes["tp"])]


def row_blocks(team):
    ts = team.sizes["tp"]
    return [
        team.slot(offset) * ts + modulo(team.at["tp"] - step + ts, ts)
        for step in range(ts)
        for offset in team.offsets
    ]


def core_send(team, rows, pieces, half_rows, *others):
    sent = [spread(rows, step, pieces, half_rows) for step in range(1, team.sizes["tp"])]
    sent = fence(*sent, *others)[: len(sent)]
    return [team.ring(value, "tp", -step) for step, value in enumerate(sent, 1)]


def core_total(team, rows, pieces, half_rows, got):
    total, *sent = spread(rows, 0, pieces, half_rows, got, team.members)
    return total, sent


def team_send_direct(team, sent):
    return [
        team.shift(value, offset, back=True) for value, offset in zip(sent, team.offsets[1:])
    ]


def team_send(team, sent):
    xs = team.sizes["x"]
    across_x = [(0, dx) for dx in range(1, xs)]
    far = sent[xs - 1].astype(WIDE)
    for value, offset in zip(sent[xs:], across_x):
        far = far + team.shift(value, offset, back=True).astype(WIDE)
    got = [team.shift(value, offset, back=True) for value, offset in zip(sent, across_x)]
    return got + [team.shift(far.astype(LOWER), (1, 0), back=True)]


def team_total(own, got):
    for value in got:
        own = own + value.astype(WIDE)
    return own


def put(buffer, value, starts):
    return lax.dynamic_update_slice(buffer, value, starts)


def share_columns(team, shards):
    widths = [shard.shape[1] // team.members for shard in shards]
    pieces = []
    for j, offset in enumerate(team.offsets):
        slot = team.slot(offset, back=False)
        cuts = [
            lax.dynamic_slice_in_dim(shard, slot * each, each, 1)
            for shard, each in zip(shards, widths)
        ]
        piece = jnp.concatenate(cuts, axis=1)
        pieces.append(team.shift(piece, offset) if j > 0 else piece)
    return pieces


def place_rows_kernel(widths, slots_ref, *refs):
    pieces, outs = refs[: len(refs) - len(widths)], refs[len(refs) - len(widths) :]
    for j, piece in enumerate(pieces):
        height = piece.shape[0]
        row = pl.multiple_of(slots_ref[j] * height, height)
        first = 0
        for out, width in zip(outs, widths):
            out[pl.ds(row, height), :] = piece[:, first : first + width]
            first += width


def place_columns_kernel(widths, slots_ref, *refs):
    pieces, outs = refs[: len(refs) - len(widths)], refs[len(refs) - len(widths) :]
    for j, piece in enumerate(pieces):
        first = 0
        for out, width in zip(outs, widths):
            column = pl.multiple_of(slots_ref[j] * width, width)
            block = piece[:, first : first + width].astype(out.dtype)
            out[:, pl.ds(column, width)] = block
            first += width


def place(team, kernel, pieces, widths, shapes):
    slots = jnp.stack([team.slot(offset) for offset in team.offsets]).astype(jnp.int32)
    whole = [pl.BlockSpec(piece.shape, lambda n: (0, 0)) for piece in pieces]
    return pl.pallas_call(
        kernel if widths is None else functools.partial(kernel, widths),
        grid=(1,),
        in_specs=[pl.BlockSpec(memory_space=pltpu.SMEM)] + whole,
        out_specs=[pl.BlockSpec(shape.shape, lambda n: (0, 0)) for shape in shapes],
        out_shape=shapes,
        cost_estimate=LIGHT,
        compiler_params=KERNEL,
    )(slots, *pieces)


def stack_rows_kernel(*refs):
    height = refs[0].shape[0]
    for j, piece in enumerate(refs[:-1]):
        refs[-1][j * height : (j + 1) * height, :] = piece[...]


def stack_rows(pieces):
    height, width = pieces[0].shape
    rows = height * len(pieces)
    return pl.pallas_call(
        stack_rows_kernel,
        grid=(1,),
        in_specs=[pl.BlockSpec((height, width), lambda n: (0, 0)) for _ in pieces],
        out_specs=pl.BlockSpec((rows, width), lambda n: (0, 0)),
        out_shape=jax.ShapeDtypeStruct((rows, width), pieces[0].dtype),
        cost_estimate=LIGHT,
        compiler_params=KERNEL,
    )(*pieces)


def place_halves_kernel(slots_ref, *refs):
    pieces, outs = refs[:-2], refs[-2:]
    split = len(pieces) // 2
    for j, piece in enumerate(pieces):
        height = piece.shape[0]
        for part, out in enumerate(outs):

            @pl.when(lax.div(slots_ref[j], split) == part)
            def _():
                row = pl.multiple_of(lax.rem(slots_ref[j], split) * height, height)
                out[pl.ds(row, height), :] = piece[...]


def near_rows(team, pieces, parts=1):
    height, width = pieces[0].shape
    shape = jax.ShapeDtypeStruct((height * team.members // parts, width), LOWER)
    if parts == 1:
        return place(team, place_rows_kernel, pieces, [width], [shape])
    return place(team, place_halves_kernel, pieces, None, [shape] * 2)


def across(team, value):
    return [team.ring(value, "h", -step) for step in range(1, team.sizes["h"])]


def beside(team, values):
    return [team.ring(value, "y", 1) for value in values]


def halves(value):
    middle = value.shape[0] // 2
    return value[:middle], value[middle:]


def pairs(firsts, seconds):
    return [part for pair in zip(firsts, seconds) for part in pair]


def add_ring(team, value, name):
    return value + sum(team.ring(value, name, step) for step in range(1, team.sizes[name]))


class Grads:
    def __init__(self, team, lefts, rights):
        self.team, self.lefts, self.rights = team, lefts, rights
        self.far = lefts[0].shape[1] // 2
        self.near = self.far // team.sizes["h"]

        self.half = self.near // 2
        self.steps = range(1, team.sizes["h"])

    def rows(self, first, count, adds=(), offset=0, column=0):
        return outer(self.lefts, self.rights, first, count, adds, offset, column)

    def send_far(self):
        return self.rows(self.far + self.near, self.far - self.near)

    def send_half(self, part):
        start = self.far + part * self.half
        return [self.rows(start + step * self.near, self.half) for step in self.steps]

    def send_near(self):
        return self.rows(self.far, self.near)

    def cross(self, got):
        offsets = [(step - 1) * self.near for step in self.steps]
        return [self.rows(self.near + first, self.near, [got], first) for first in offsets]

    def cross_half(self, part, got):
        offsets = [(step - 1) * self.near + part * self.half for step in self.steps]
        return [self.rows(self.near + first, self.half, [got], first) for first in offsets]

    def cross_halves(self, part, gots):
        start = part * self.half
        return [
            self.rows(start + step * self.near, self.half, [got])
            for step, got in zip(self.steps, gots)
        ]

    def go(self, sent):
        return [self.team.ring(value, "h", step) for step, value in zip(self.steps, sent)]

    def total(self, got, crossed, column=0):
        return self.rows(0, self.near, [got, *crossed], column=column)


def home_pieces(team, total):
    height = total.shape[0] // team.members
    total = total.reshape(team.members, height, -1)
    pieces = []
    for j, offset in enumerate(team.offsets):
        piece = lax.dynamic_index_in_dim(total, team.slot(offset, back=False), 0, False)
        pieces.append(team.shift(piece, offset) if j > 0 else piece)
    return pieces


def home_join(team, pieces, widths):
    height = pieces[0].shape[0]
    shapes = [jax.ShapeDtypeStruct((height, width * team.members), WIDE) for width in widths]
    return place(team, place_columns_kernel, pieces, widths, shapes)


def permute_kernel(count, table_ref, value_ref, out_ref):
    block = value_ref.shape[1] // count
    for i in range(count):
        column = pl.multiple_of(table_ref[i] * block, block)
        out_ref[:, i * block : (i + 1) * block] = value_ref[:, pl.ds(column, block)]


def permute_columns(value, table):
    whole = pl.BlockSpec(value.shape, lambda n: (0, 0))
    return pl.pallas_call(
        functools.partial(permute_kernel, len(table)),
        grid=(1,),
        in_specs=[pl.BlockSpec(memory_space=pltpu.SMEM), whole],
        out_specs=whole,
        out_shape=jax.ShapeDtypeStruct(value.shape, value.dtype),
        cost_estimate=LIGHT,
    )(jnp.stack(table).astype(jnp.int32), value)


def to_team_order(team, value):
    hs = team.sizes["h"]
    table = []
    for dy in range(2):
        for dh in range(hs):
            for l in range(2):
                h, y = modulo(team.at["h"] + dh, hs), modulo(team.at["y"] + dy, 2)
                table.append((h * 2 + l) * 2 + y)
    return permute_columns(value, table)


def from_team_order(team, value):
    hs = team.sizes["h"]
    table = []
    for h in range(hs):
        for l in range(2):
            for y in range(2):
                dh, dy = modulo(h - team.at["h"] + hs, hs), modulo(y - team.at["y"] + 2, 2)
                table.append((dy * hs + dh) * 2 + l)
    return permute_columns(value, table)


def pick(table, index):
    ids = jnp.arange(table.shape[0], dtype=jnp.int32)
    return jnp.sum(jnp.where(ids == index, table, 0))


def choose(pieces, index):
    out = pieces[0]
    for i in range(1, len(pieces)):
        out = jnp.where(index == i, pieces[i], out)
    return out


def spread_h(team, piece):
    return [piece] + [team.ring(piece, "h", step) for step in range(1, team.sizes["h"])]


def deal_flip(team, piece, flip):
    if flip == 0:
        return swap_home(piece)
    perm = [(l * 2 + y, y * 2 + 1 - l) for l in range(2) for y in range(2)]
    with jax.named_scope("flip"):
        return lax.ppermute(piece, ("l", "y"), perm)


def deal_across(team, two):
    first = swapped_home(team, two[0], two[1])
    chosen = [jnp.where(need, first, two[2]) for need in team.needs]
    return chosen[:1] + [team.ring(value, "h", step) for step, value in enumerate(chosen) if step]


def dealt_in(team, pieces):
    return choose(pieces, team.in_step)


def deal(team, pieces):
    first, second = (choose(pieces, step) for step in team.out_steps)
    return first, swap_home(first), second


def deal_second(value):
    perm = [(l * 2 + y, (1 - y) * 2 + l) for l in range(2) for y in range(2)]
    return lax.ppermute(value, ("l", "y"), perm)


def dealt_out(team, got):
    return jnp.where(team.out_first, swapped_home(team, got[0], got[1]), got[2])


def join_cores(team, piece):
    ts = team.sizes["tp"]
    out = jnp.zeros((ts,) + piece.shape, piece.dtype)
    for step in range(ts):
        other = team.ring(piece, "tp", step) if step else piece
        out = put(out, other[None], (modulo(team.at["tp"] - step + ts, ts), 0, 0))
    return out.reshape(-1, piece.shape[-1])


def layer_norm(inputs, gain_vec, shift_vec):
    row_mean = jnp.mean(inputs, axis=-1, keepdims=True)
    centred = inputs - row_mean
    spread = jnp.mean(centred * centred, axis=-1, keepdims=True)
    rate = lax.rsqrt(spread + EPSILON)
    xhat = centred * rate
    return xhat * gain_vec + shift_vec, xhat, rate


def layer_norm_back(grad, gain_vec, xhat, rate):
    scaled = grad * gain_vec
    return rate * (
        scaled
        - jnp.mean(scaled, axis=-1, keepdims=True)
        - xhat * jnp.mean(scaled * xhat, axis=-1, keepdims=True)
    )


def gelu_tanh(inputs):
    return jax.nn.gelu(inputs, approximate=True)


def masked_scores(key_ref, query, limits_ref, scale):
    count = limits_ref.shape[0]
    height = key_ref.shape[0] // count
    blocks = []
    for j in range(count):
        block = mm_nt(key_ref[j * height : (j + 1) * height, :], query) * scale
        row = lax.broadcasted_iota(jnp.int32, block.shape, 0)
        blocks.append(jnp.where(row < limits_ref[j], block, NEGATIVE))
    return blocks


def attend_kernel(scale, limits_ref, query_ref, key_ref, value_ref, out_ref, log_ref):
    blocks = masked_scores(key_ref, query_ref[...], limits_ref, scale)
    row_max = functools.reduce(jnp.maximum, blocks)
    row_max = jnp.max(row_max, axis=0, keepdims=True)
    blocks = [jnp.exp(block - row_max) for block in blocks]
    total = jnp.sum(functools.reduce(jnp.add, blocks), axis=0, keepdims=True)
    inverse = 1.0 / total
    height = key_ref.shape[0] // len(blocks)
    out = None
    for j, block in enumerate(blocks):
        value = value_ref[j * height : (j + 1) * height, :]
        term = mm_tn(value, (block * inverse).astype(LOWER))
        out = term if out is None else out + term
    out_ref[...] = out.T.astype(LOWER)
    log_ref[0] = row_max + jnp.log(total)


def attend_back_kernel(
    scale, wide, limits_ref, query_ref, key_ref, value_ref, grad_ref, log_ref, out_ref, key_sum, value_sum
):
    head, step = pl.program_id(0), pl.program_id(1)
    query, grad = query_ref[...], grad_ref[...]
    blocks = masked_scores(key_ref, query, limits_ref, scale)
    count = len(blocks)
    height = key_ref.shape[0] // count
    part = [slice(j * height, (j + 1) * height) for j in range(count)]
    log_sum = log_ref[0]
    probs = [jnp.exp(block - log_sum) for block in blocks]
    grad_probs = [mm_nt(value_ref[rows, :], grad) for rows in part]
    delta = functools.reduce(jnp.add, [p * g for p, g in zip(probs, grad_probs)])
    delta = jnp.sum(delta, axis=0, keepdims=True)

    @pl.when(step == 0)
    def _():
        key_sum[...] = jnp.zeros_like(key_sum)
        value_sum[...] = jnp.zeros_like(value_sum)

    grad_query = None
    for j, rows in enumerate(part):
        scores = (probs[j] * (grad_probs[j] - delta)).astype(LOWER)
        term = mm_tn(key_ref[rows, :], scores)
        grad_query = term if grad_query is None else grad_query + term
        key_sum[rows, :] += mm(scores, query)
        value_sum[rows, :] += mm(probs[j].astype(LOWER), grad)
    count = query.shape[0]
    first = pl.multiple_of(step * count, count)
    column = pl.multiple_of(head * HEAD, HEAD)
    out_ref[pl.ds(first, count), pl.ds(column, HEAD)] = (grad_query.T * scale).astype(LOWER)

    @pl.when(step == pl.num_programs(1) - 1)
    def _():
        out_ref[:, pl.ds(wide + column, HEAD)] = (key_sum[...] * scale).astype(LOWER)
        out_ref[:, pl.ds(2 * wide + column, HEAD)] = value_sum[...].astype(LOWER)


LIGHT = pl.CostEstimate(flops=1000000, bytes_accessed=100000, transcendentals=0)
KERNEL = pltpu.CompilerParams(vmem_limit_bytes=24 * 1024 * 1024)


def gelu_slope(value):
    inner = math.sqrt(2.0 / math.pi)
    square = value * value
    tanh = jnp.tanh(inner * value * (1.0 + 0.044715 * square))
    return 0.5 * (1.0 + tanh) + 0.5 * value * (1.0 - tanh * tanh) * inner * (
        1.0 + 3.0 * 0.044715 * square
    )


def project_kernel(mode, part_count, piece_count, steps, *refs):
    parts, pieces = refs[:part_count], refs[part_count : part_count + piece_count]
    rest = refs[part_count + piece_count :]
    index = pl.program_id(0)

    def run(rows):
        total = None
        first = 0
        for piece in pieces:
            depth = piece.shape[0]
            term = mm(rows[:, first : first + depth], piece[...])
            total = term if total is None else total + term
            first += depth
        if mode == "bias":
            rest[1][...] = (total + rest[0][...]).astype(LOWER)
        elif mode == "gelu":
            total = total + rest[0][...]
            rest[1][...] = total
            rest[2][...] = gelu_tanh(total).astype(LOWER)
        elif mode == "slope":
            rest[1][...] = (total * gelu_slope(rest[0][...])).astype(LOWER)
        else:
            rest[0][...] = total.astype(LOWER)

    for place in range(part_count):

        @pl.when(index // steps == place)
        def _():
            run(parts[place][...])


def project(mode, parts, pieces, width, extra=None):
    half_rows, depth = parts[0].shape
    block = min(256, half_rows)
    steps = half_rows // block
    rows = half_rows * len(parts)

    def part_at(place):
        return lambda i: (jnp.clip(i - place * steps, 0, steps - 1), 0)

    in_specs = [pl.BlockSpec((block, depth), part_at(place)) for place in range(len(parts))]
    for array, column in pieces:
        in_specs.append(
            pl.BlockSpec((array.shape[0], width), functools.partial(lambda c, i: (0, c), column))
        )
    arrays = list(parts) + [array for array, _ in pieces]
    tile = pl.BlockSpec((block, width), lambda i: (i, 0))
    if mode in ("bias", "gelu"):
        in_specs.append(pl.BlockSpec((1, width), lambda i: (0, 0)))
        arrays.append(extra[None])
    elif mode == "slope":
        in_specs.append(tile)
        arrays.append(extra)
    shapes = [jax.ShapeDtypeStruct((rows, width), LOWER)]
    if mode == "gelu":
        shapes = [jax.ShapeDtypeStruct((rows, width), WIDE)] + shapes
    return pl.pallas_call(
        functools.partial(project_kernel, mode, len(parts), len(pieces), steps),
        grid=(len(parts) * steps,),
        in_specs=in_specs,
        out_specs=[tile] * len(shapes),
        out_shape=shapes,
        cost_estimate=LIGHT,
        compiler_params=KERNEL,
    )(*arrays)


def spread_kernel(piece_count, got_count, members, rows_ref, *refs):
    pieces, gots = refs[:piece_count], refs[piece_count : piece_count + got_count]
    outs = refs[piece_count + got_count :]
    rows = rows_ref[...]
    height = rows.shape[0] // members
    first = 0
    for piece in pieces:
        columns = slice(first, first + piece.shape[0])
        total = mm_nt(rows, piece[...])
        for got in gots:
            total = total + got[:, columns].astype(WIDE)
        for j, out in enumerate(outs):
            out[:, columns] = total[j * height : (j + 1) * height].astype(out.dtype)
        first += piece.shape[0]


def spread(rows, place, pieces, half_rows, got=(), members=0):
    if isinstance(rows, (list, tuple)):
        rows, place = rows[place], 0
    depth = rows.shape[1]
    width = sum(array.shape[0] for array, _ in pieces)
    in_specs = [pl.BlockSpec((half_rows, depth), lambda n: (place, 0))]
    for array, column in pieces:
        in_specs.append(
            pl.BlockSpec((array.shape[0], depth), functools.partial(lambda c, n: (0, c), column))
        )
    in_specs += [pl.BlockSpec((half_rows, width), lambda n: (0, 0))] * len(got)
    split = max(members, 1)
    height = half_rows // split
    dtypes = [WIDE] + [LOWER] * (members - 1) if members else [LOWER]
    out = pl.pallas_call(
        functools.partial(spread_kernel, len(pieces), len(got), split),
        grid=(1,),
        in_specs=in_specs,
        out_specs=[pl.BlockSpec((height, width), lambda n: (0, 0))] * split,
        out_shape=[jax.ShapeDtypeStruct((height, width), dtype) for dtype in dtypes],
        cost_estimate=LIGHT,
        compiler_params=KERNEL,
    )(rows, *[array for array, _ in pieces], *got)
    return out if members else out[0]


def outer_kernel(part_count, add_count, *refs):
    lefts, rights = refs[:part_count], refs[part_count : 2 * part_count]
    adds, out = refs[2 * part_count : 2 * part_count + add_count], refs[-1]
    total = None
    for left, right in zip(lefts, rights):
        term = mm_tn(left[...], right[...])
        total = term if total is None else total + term
    for add in adds:
        total = total + add[...].astype(WIDE)
    out[...] = total.astype(out.dtype)


def outer(lefts, rights, first, count, adds, offset, column):
    height = lefts[0].shape[0]
    rights = [right if isinstance(right, tuple) else (right, 0) for right in rights]
    width = rights[0][0].shape[1]
    block = math.gcd(256, count)
    in_specs = [pl.BlockSpec((height, block), lambda i: (0, first // block + i)) for _ in lefts]
    for _, row in rights:
        in_specs.append(
            pl.BlockSpec((height, width), functools.partial(lambda r, i: (r, 0), row))
        )
    tile = pl.BlockSpec((block, width), lambda i: (i, 0))
    add_tile = pl.BlockSpec((block, width), lambda i: (offset // block + i, 0))
    first_tile = pl.BlockSpec((block, width), lambda i: (offset // block + i, column))
    return pl.pallas_call(
        functools.partial(outer_kernel, len(lefts), len(adds)),
        grid=(count // block,),
        in_specs=in_specs + [first_tile] * len(adds[:1]) + [add_tile] * len(adds[1:]),
        out_specs=tile,
        out_shape=jax.ShapeDtypeStruct((count, width), LOWER),
        cost_estimate=LIGHT,
        compiler_params=KERNEL,
    )(*lefts, *[right for right, _ in rights], *adds)


def query_block(rows):
    return min(512, rows)


def attend(qkv, limits, scale):
    rows, wide = qkv.shape[0], qkv.shape[1] // 3
    heads, block = wide // HEAD, query_block(rows)
    return pl.pallas_call(
        functools.partial(attend_kernel, scale),
        grid=(heads, rows // block),
        in_specs=[
            pl.BlockSpec(memory_space=pltpu.SMEM),
            pl.BlockSpec((block, HEAD), lambda h, i: (i, h)),
            pl.BlockSpec((rows, HEAD), lambda h, i: (0, heads + h)),
            pl.BlockSpec((rows, HEAD), lambda h, i: (0, 2 * heads + h)),
        ],
        out_specs=[
            pl.BlockSpec((block, HEAD), lambda h, i: (i, h)),
            pl.BlockSpec((1, 1, block), lambda h, i: (h, 0, i)),
        ],
        out_shape=[
            jax.ShapeDtypeStruct((rows, wide), LOWER),
            jax.ShapeDtypeStruct((heads, 1, rows), WIDE),
        ],
        cost_estimate=LIGHT,
        compiler_params=KERNEL,
    )(limits, qkv, qkv, qkv)


def attend_back(qkv, grad, log_sum, limits, scale):
    rows, wide = grad.shape
    heads, block = wide // HEAD, query_block(rows)
    return pl.pallas_call(
        functools.partial(attend_back_kernel, scale, wide),
        grid=(heads, rows // block),
        in_specs=[
            pl.BlockSpec(memory_space=pltpu.SMEM),
            pl.BlockSpec((block, HEAD), lambda h, i: (i, h)),
            pl.BlockSpec((rows, HEAD), lambda h, i: (0, heads + h)),
            pl.BlockSpec((rows, HEAD), lambda h, i: (0, 2 * heads + h)),
            pl.BlockSpec((block, HEAD), lambda h, i: (i, h)),
            pl.BlockSpec((1, 1, block), lambda h, i: (h, 0, i)),
        ],
        out_specs=pl.BlockSpec((rows, 3 * wide), lambda h, i: (0, 0)),
        out_shape=jax.ShapeDtypeStruct((rows, 3 * wide), LOWER),
        scratch_shapes=[pltpu.VMEM((rows, HEAD), WIDE), pltpu.VMEM((rows, HEAD), WIDE)],
        cost_estimate=LIGHT,
        compiler_params=KERNEL,
    )(limits, qkv, qkv, qkv, grad, log_sum)


def local(
    tokens,
    lengths,
    dealing,
    w_query,
    w_key,
    w_value,
    w_out,
    b_query,
    b_value,
    b_out,
    gain_mid,
    shift_mid,
    w_up,
    b_up,
    w_down,
    b_down,
    gain_end,
    shift_end,
    cotangent,
):
    team = Team()
    ts, members = team.sizes["tp"], team.members
    row_count = tokens.shape[0] // ts
    wide = w_query.shape[1] // members
    tall = w_up.shape[1] // members
    width = tokens.shape[1]
    score_scale = 1.0 / math.sqrt(HEAD)
    my_slot = team.at["l"] * team.sizes["x"] + team.at["x"]
    seq_ids = jnp.arange(dealing.shape[0], dtype=jnp.int32)
    home = jnp.sum(jnp.where(dealing[None, :] == seq_ids[:, None], seq_ids[None, :], 0), axis=1)
    plan = team.plan(dealing, home)
    team.set_plan(plan)
    live_count = pick(lengths, team.at["h"] * 2 + team.at["y"])
    limits = live_count - jnp.stack(row_blocks(team)).astype(jnp.int32) * row_count
    query_live = (jnp.arange(row_count, dtype=jnp.int32) < limits[0])[:, None]
    half_at = team.at["tp"] * row_count

    half_rows = members * row_count
    vectors = jnp.stack([b_out, gain_mid, shift_mid, b_down, gain_end, shift_end])
    b_out, gain_mid, shift_mid, b_down, gain_end, shift_end = to_team_order(team, vectors)
    bias_q = lax.dynamic_slice_in_dim(b_query, my_slot * wide, wide, 0)
    bias_v = lax.dynamic_slice_in_dim(b_value, my_slot * wide, wide, 0)
    bias_up = lax.dynamic_slice_in_dim(b_up, my_slot * tall, tall, 0)
    bias_qkv = jnp.concatenate([bias_q, jnp.zeros_like(bias_q), bias_v])
    steps = team.sizes["h"] - 1
    team_count = team.sizes["x"]


    def first_column(arrays):
        return [(array, 0) for array in arrays]

    with jax.named_scope("a0"):
        mine = lax.dynamic_slice_in_dim(tokens, half_at, row_count, 0)
        own = swap_home(mine)
        share = share_columns(team, [w_query, w_key, w_value, w_out])
        own, w_up, w_down, bias_qkv, bias_up, limits, query_live, *rest = fence(
            own, w_up, w_down, bias_qkv, bias_up, limits, query_live, *share, *plan
        )
        share, plan = rest[:members], rest[members:]
        team.set_plan(plan)
    with jax.named_scope("a1"):
        own = to_team_order(team, swapped_home(team, mine, own))
        (near_att,) = near_rows(team, share)
        pieces = team_pieces(team, own)
        cross_qkv = across(team, near_att[:, : 3 * wide])
        (side_att,) = beside(team, [near_att])
        near_att, w_up, w_down, cotangent, side_att, *rest = fence(
            near_att, w_up, w_down, cotangent, side_att, *pieces, *cross_qkv
        )
        pieces, cross_qkv = rest[:members], rest[members:]
    with jax.named_scope("a2"):
        half = stack_rows(pieces)
        other = cores(team, half)
        far_qkv = beside(team, cross_qkv)
        cross_out = across(team, near_att[:, 3 * wide :])
        share = share_columns(team, [w_up])
        cotangent, w_down, *rest = fence(
            cotangent, w_down, half, *other, *share, *far_qkv, *cross_out
        )
        in_parts = rest[:ts]
        share, rest = rest[ts : ts + members], rest[ts + members :]
        far_qkv, cross_out = rest[:steps], rest[steps:]
    qkv_mat = first_column([near_att, *cross_qkv, side_att, *far_qkv])
    with jax.named_scope("c1"):
        up_a, up_b = near_rows(team, share, 2)
        cross_up_a = across(team, up_a)
        far_out = beside(team, cross_out)
        cot_half = lax.dynamic_slice_in_dim(cotangent, half_at, row_count, 0)
        share = share_columns(team, [w_down])
        (qkv,) = project("bias", in_parts, qkv_mat, 3 * wide, bias_qkv)
        attended, log_sum = attend(qkv, limits, score_scale)
        out_mat = [(near_att, 3), *first_column(cross_out), (side_att, 3), *first_column(far_out)]
        got = core_send(team, attended, out_mat, half_rows, *cross_up_a, *share)
        total, sent = core_total(team, attended, out_mat, half_rows, got)
        up_a, up_b, cot_half, *rest = fence(
            up_a, up_b, cot_half, *cross_up_a, *share, *sent
        )
        cross_up_a, rest = rest[:steps], rest[steps:]
        share, sent = rest[:members], rest[members:]
    with jax.named_scope("s3"):
        got = team_send(team, sent)
        cross_up_b = across(team, up_b)
        down_a, down_b = near_rows(team, share, 2)
        side = beside(team, [jnp.concatenate([up_a, *cross_up_a], axis=0)])
        cot_one = deal_flip(team, cot_half, 0)
        cot_half, cot_one, up_b, down_a, down_b, *rest = fence(
            cot_half, cot_one, up_b, down_a, down_b, *got, *cross_up_b, *side
        )
        got, rest = rest[:team_count], rest[team_count:]
        cross_up_b, side_a = rest[:steps], rest[steps]
    with jax.named_scope("s4"):
        branch = team_total(total, got) + b_out
        middle, mid_hat, mid_rate = layer_norm(own.astype(WIDE) + branch, gain_mid, shift_mid)
        pieces = team_pieces(team, middle.astype(LOWER))
        cross_down_a = across(team, down_a)
        side = beside(team, [jnp.concatenate([up_b, *cross_up_b], axis=0)])
        cot_two = [cot_half, cot_one, deal_flip(team, cot_half, 1)]
        down_a, down_b, *rest = fence(
            down_a, down_b, *cot_two, *pieces, *cross_down_a, *side
        )
        cot_two, rest = rest[:3], rest[3:]
        pieces, rest = rest[:members], rest[members:]
        cross_down_a, side_b = rest[:steps], rest[steps]
    part_rows = down_a.shape[0]

    def split_side(side):
        blocks = [side[k * part_rows : (k + 1) * part_rows] for k in range(steps + 1)]
        return blocks[0], blocks[1:]

    side_up_a, far_up_a = split_side(side_a)
    side_up_b, far_up_b = split_side(side_b)
    up_mat = first_column(
        [up_a, up_b]
        + pairs(cross_up_a, cross_up_b)
        + [side_up_a, side_up_b]
        + pairs(far_up_a, far_up_b)
    )
    with jax.named_scope("c2"):
        half = stack_rows(pieces)
        other = cores(team, half)
        cross_down_b = across(team, down_b)
        side = beside(team, [jnp.concatenate([down_a, *cross_down_a], axis=0)])
        mid_parts = [half] + other
        hidden, active = [], []
        for part in mid_parts:
            hidden_part, active_part = project("gelu", [part], up_mat, tall, bias_up)
            hidden.append(hidden_part)
            active.append(active_part)
        down_b, *rest = fence(down_b, *active, *cross_down_b, *side, *cot_two)
        active, rest = rest[:ts], rest[ts:]
        cross_down_b, side, cot_two = rest[:steps], rest[steps], rest[steps + 1 :]
        side_down_a, far_down_a = split_side(side)
    with jax.named_scope("s5"):
        (side,) = beside(team, [jnp.concatenate([down_b, *cross_down_b], axis=0)])
        side_down_b, far_down_b = split_side(side)
        cot_pieces = deal_across(team, cot_two)
        down_mat = first_column(
            [down_a, down_b]
            + pairs(cross_down_a, cross_down_b)
            + [side_down_a, side_down_b]
            + pairs(far_down_a, far_down_b)
        )
        got = core_send(team, active, down_mat, half_rows, *cot_pieces)
        total, sent = core_total(team, active, down_mat, half_rows, got)
        rest = fence(*sent, *cot_pieces)
        sent, cot_pieces = rest[: members - 1], rest[members - 1 :]
    with jax.named_scope("s6"):
        cot = to_team_order(team, dealt_in(team, cot_pieces))
        cot, *got = fence(cot, *team_send_direct(team, sent))
    with jax.named_scope("s7"):
        result = team_total(total, got) + b_down
        normed, end_hat, end_rate = layer_norm(middle + result, gain_end, shift_end)
        output_own = jnp.where(query_live, normed, 0.0).astype(LOWER)
        grad_normed = jnp.where(query_live, cot.astype(WIDE), 0.0)
        grad_sum = layer_norm_back(grad_normed, gain_end, end_hat, end_rate)
        grad_result = grad_sum.astype(LOWER)
        pieces = team_pieces(team, grad_result)
        out_pieces = spread_h(team, from_team_order(team, output_own))
        rest = fence(*pieces, *out_pieces)
        pieces, out_pieces = rest[:members], rest[members:]
        grad_gend = jnp.sum(grad_normed * end_hat, axis=0)
        grad_send = jnp.sum(grad_normed, axis=0)
        grad_bdown = jnp.sum(grad_result.astype(WIDE), axis=0)
    with jax.named_scope("c3"):
        half = stack_rows(pieces)
        other = cores(team, half)
        result_parts = [half] + other
        flow_down = Grads(team, result_parts, active)
        far_down_a = beside(team, flow_down.send_half(0))
        grad_hidden = []
        for part, hidden_part in zip(result_parts, hidden):
            grad_hidden += project("slope", [part], down_mat, tall, hidden_part)
        got = core_send(team, grad_hidden, up_mat, half_rows, *far_down_a, *grad_hidden)
        total, sent = core_total(team, grad_hidden, up_mat, half_rows, got)
        cross_down = flow_down.cross_halves(0, far_down_a)
        flow_up = Grads(team, mid_parts, grad_hidden)
        rest = fence(*sent, *cross_down)
        sent, cross_down = rest[: members - 1], rest[members - 1 :]
    with jax.named_scope("s8"):
        got = team_send(team, sent)
        got_down_a = flow_down.go(cross_down)
        far_down_b = beside(team, flow_down.send_half(1))
        far_up, *far_down_b = fence(flow_up.send_far(), *far_down_b)
        (far_up,) = beside(team, [far_up])
        cross_down = flow_down.cross_halves(1, far_down_b)
        far_up, *rest = fence(far_up, *got, *got_down_a, *cross_down)
        got, rest = rest[:team_count], rest[team_count:]
        got_down_a, cross_down = rest[:steps], rest[steps:]
    with jax.named_scope("s9"):
        grad_middle = team_total(total, got) + grad_sum
        grad_inner = layer_norm_back(grad_middle, gain_mid, mid_hat, mid_rate)
        grad_branch = grad_inner.astype(LOWER)
        pieces = team_pieces(team, grad_branch)
        got_down_b = flow_down.go(cross_down)
        (near_down,) = beside(team, [flow_down.send_near()])
        grad_gmid = jnp.sum(grad_middle * mid_hat, axis=0)
        grad_smid = jnp.sum(grad_middle, axis=0)
        grad_bout = jnp.sum(grad_branch.astype(WIDE), axis=0)
        by_row = jnp.stack([grad_bout, grad_gmid, grad_smid, grad_bdown, grad_gend, grad_send])
        by_row = add_ring(team, from_team_order(team, by_row), "tp")
        out_first, out_swapped, out_second = deal(team, out_pieces)
        cross_up_a, cross_up_b = flow_up.cross_half(0, far_up), flow_up.cross_half(1, far_up)
        by_row, near_down, out_first, out_swapped, out_second, *rest = fence(
            by_row, near_down, out_first, out_swapped, out_second, *pieces, *got_down_b, *cross_up_a, *cross_up_b)
        pieces, rest = rest[:members], rest[members:]
        got_down_b, rest = rest[:steps], rest[steps:]
        cross_up_a, cross_up_b = rest[:steps], rest[steps:]
    with jax.named_scope("c4"):
        half = stack_rows(pieces)
        other = cores(team, half)
        got_up_a, got_up_b = flow_up.go(cross_up_a), flow_up.go(cross_up_b)
        out_two = [out_first, out_swapped, deal_second(out_second)]
        branch_parts = [half] + other
        attended_parts = [(attended, k) for k in range(ts)]
        flow_out = Grads(team, branch_parts, attended_parts)
        (far_out,) = beside(team, [flow_out.send_far()])
        (grad_attended,) = project("plain", branch_parts, out_mat, wide)
        grad_qkv = attend_back(qkv, grad_attended, log_sum, limits, score_scale)
        got = core_send(team, grad_qkv, qkv_mat, half_rows, far_out, *got_up_a, *out_two)
        total, sent = core_total(team, grad_qkv, qkv_mat, half_rows, got)
        grad_parts = [(grad_qkv, k) for k in range(ts)]
        flow_qkv = Grads(team, in_parts, grad_parts)
        qkv_sum = jnp.sum(grad_qkv.astype(WIDE), axis=0)
        grad_bup = sum(jnp.sum(part.astype(WIDE), axis=0) for part in grad_hidden)
        zeros = jnp.zeros((members, 1), WIDE)
        by_slot = [
            put(zeros * part[None], part[None], (my_slot, 0)).reshape(-1)
            for part in (qkv_sum[:wide], qkv_sum[2 * wide :], grad_bup)
        ]
        sums = jnp.concatenate([by_row.reshape(-1)] + by_slot).reshape(-1, 128)
        sums = add_ring(team, sums, "x")
        (far_qkv,) = beside(team, [flow_qkv.send_far()])
        cross_out = flow_out.cross(far_out)
        sums, near_down, far_qkv, *rest = fence(
            sums, near_down, far_qkv, *cross_out, *sent, *got_up_a, *got_up_b, *out_two
        )
        cross_out, rest = rest[:steps], rest[steps:]
        sent, rest = rest[: members - 1], rest[members - 1 :]
        got_up_a, got_up_b, out_two = rest[:steps], rest[steps : 2 * steps], rest[2 * steps :]
    with jax.named_scope("s10"):
        got = team_send(team, sent)
        total_down = flow_down.total(
            near_down,
            [jnp.concatenate(both, axis=0) for both in zip(got_down_a, got_down_b)],
        )
        got_qkv = flow_qkv.go(flow_qkv.cross(far_qkv))
        (near_up,) = beside(team, [flow_up.send_near()])
        sums, total_down, near_up, *rest = fence(
            sums, total_down, near_up, *out_two, *got, *got_qkv, *cross_out
        )
        out_two, rest = rest[:3], rest[3:]
        got, rest = rest[:team_count], rest[team_count:]
        got_qkv, cross_out = rest[:steps], rest[steps:]
    with jax.named_scope("s11"):
        got_out = flow_out.go(cross_out)
        home_down = home_pieces(team, total_down)
        grad_own = (team_total(total, got) + grad_inner).astype(LOWER)
        grad_own = from_team_order(team, grad_own)
        swapped = swap_home(grad_own)
        near_att = jnp.concatenate([flow_qkv.send_near(), flow_out.send_near()], axis=1)
        (near_att,) = beside(team, [near_att])
        total_up = flow_up.total(
            near_up, [jnp.concatenate(both, axis=0) for both in zip(got_up_a, got_up_b)]
        )
        total_out = flow_out.total(near_att, got_out, 3)
        total_qkv = flow_qkv.total(near_att, got_qkv, 0)
        sums, swapped, total_up, total_out, total_qkv, *rest = fence(
            sums, swapped, total_up, total_out, total_qkv, *home_down, *out_two
        )
        home_down, out_two = rest[:members], rest[members:]
        (grad_down,) = home_join(team, home_down, [tall])
    with jax.named_scope("s12"):
        grad_tokens = join_cores(team, swapped_home(team, grad_own, swapped))
        home_all = home_pieces(team, jnp.concatenate([total_up, total_qkv, total_out], axis=1))
        output = join_cores(team, dealt_out(team, out_two))
        sums = add_ring(
            team, add_ring(team, add_ring(team, sums, "l"), "h"), "y"
        ).reshape(-1)
        grad_up, grad_query, grad_key, grad_value, grad_out = home_join(
            team, home_all, [tall] + [wide] * 4
        )
    smalls = []
    first = 0
    for size in [width] * 6 + [b_query.shape[0], b_value.shape[0], b_up.shape[0]]:
        smalls.append(sums[first : first + size])
        first += size
    return (
        output,
        grad_tokens,
        grad_query,
        grad_key,
        grad_value,
        grad_out,
        smalls[6],
        smalls[7],
        smalls[0],
        smalls[1],
        smalls[2],
        grad_up,
        smalls[8],
        grad_down,
        smalls[3],
        smalls[4],
        smalls[5],
    )


def solution(mesh):
    fsdp, ctx, tp = (mesh.shape[name] for name in ("fsdp", "ctx", "tp"))
    fine = Mesh(mesh.devices.reshape(fsdp // 2, 2, 2, ctx // 2, tp), ROWS + ("tp",))
    rows, split = P(ROWS, None), P(ROWS, "tp")
    in_specs = (
        (rows, P(), P())
        + (split,) * 4
        + (P("tp"), P("tp"), P(), P(), P(), split, P("tp"), split, P(), P(), P(), rows)
    )
    out_specs = (
        (rows, rows)
        + (split,) * 4
        + (P("tp"), P("tp"), P(), P(), P(), split, P("tp"), split, P(), P(), P())
    )
    return jax.shard_map(local, mesh=fine, in_specs=in_specs, out_specs=out_specs, check_vma=False)
```

```python
import functools
import math

import jax
import jax.numpy as jnp
from jax import lax
from jax.experimental import pallas as pl
from jax.experimental.pallas import tpu as pltpu
from jax.sharding import Mesh
from jax.sharding import PartitionSpec as P

HEAD = 128
EPSILON = 1e-12
NEGATIVE = -1e30
WIDE = jnp.float32
LOWER = jnp.bfloat16

TEAM = ("l", "x")
ROWS = ("h", "l", "y", "x")


def dot(left, right, dims):
    return lax.dot_general(left, right, (dims, ((), ())), preferred_element_type=WIDE)


def mm(left, right):
    return dot(left, right, ((1,), (0,)))


def mm_nt(left, right):
    return dot(left, right, ((1,), (1,)))


def mm_tn(left, right):
    return dot(left, right, ((0,), (0,)))


def modulo(value, size):
    if isinstance(size, int) and size & (size - 1) == 0:
        return jnp.bitwise_and(value, size - 1)
    return lax.rem(value, size)


class Team:
    def __init__(self):
        self.sizes = {name: lax.axis_size(name) for name in ROWS + ("tp",)}
        self.at = {name: lax.axis_index(name) for name in ROWS + ("tp",)}
        ls, xs = self.sizes["l"], self.sizes["x"]
        self.offsets = [(dl, dx) for dl in range(ls) for dx in range(xs)]
        self.members = ls * xs

    def shift(self, value, offset, back=False):
        with jax.named_scope("team%d%d" % offset):
            return self.shift_(value, offset, back)

    def shift_(self, value, offset, back):
        ls, xs = self.sizes["l"], self.sizes["x"]
        dl, dx = offset
        if back:
            dl, dx = -dl, -dx
        perm = [
            (l * xs + x, ((l + dl) % ls) * xs + (x + dx) % xs) for l in range(ls) for x in range(xs)
        ]
        return lax.ppermute(value, TEAM, perm)

    def ring(self, value, name, step):
        size = self.sizes[name]
        with jax.named_scope("ring_" + name):
            return lax.ppermute(value, name, [(i, (i + step) % size) for i in range(size)])

    def slot(self, offset, back=True):
        return self.slots[back][self.offsets.index(offset)]

    def plan(self, dealing, home):
        hs, h, l, y = self.sizes["h"], self.at["h"], self.at["l"], self.at["y"]
        own = pick(home, h * 2 + y)
        needs = [
            modulo(pick(home, modulo(h + step, hs) * 2 + y), 2) == y for step in range(hs)
        ]
        sources = [pick(dealing, h * 2 + target) for target in (y, 1 - y)]
        steps = [modulo(h - lax.shift_right_logical(source, 1) + hs, hs) for source in sources]
        here = pick(dealing, h * 2 + l)
        return (
            [self.slot_(offset, back) for back in (False, True) for offset in self.offsets]
            + [l == y, modulo(h - lax.shift_right_logical(own, 1) + hs, hs), modulo(here, 2) == l]
            + steps
            + needs
        )

    def set_plan(self, plan):
        self.slots = {False: plan[: self.members], True: plan[self.members : 2 * self.members]}
        rest = plan[2 * self.members :]
        self.same, self.in_step, self.out_first = rest[:3]
        self.out_steps, self.needs = rest[3:5], rest[5:]

    def slot_(self, offset, back):
        ls, xs = self.sizes["l"], self.sizes["x"]
        dl, dx = offset
        if back:
            dl, dx = -dl, -dx
        return modulo(self.at["l"] + dl + ls, ls) * xs + modulo(self.at["x"] + dx + xs, xs)


def fence(*values):
    return lax.optimization_barrier(values)


def swap_home(value):
    return lax.ppermute(value, ("l", "y"), [(1, 2), (2, 1)])


def swapped_home(team, value, moved):
    return jnp.where(team.same, value, moved)


def team_pieces(team, piece):
    far = team.shift(piece, (1, 0))
    across_x = [(0, dx) for dx in range(1, team.sizes["x"])]
    return (
        [piece]
        + [team.shift(piece, offset) for offset in across_x]
        + [far]
        + [team.shift(far, offset) for offset in across_x]
    )


def cores(team, value):
    return [team.ring(value, "tp", step) for step in range(1, team.sizes["tp"])]


def row_blocks(team):
    ts = team.sizes["tp"]
    return [
        team.slot(offset) * ts + modulo(team.at["tp"] - step + ts, ts)
        for step in range(ts)
        for offset in team.offsets
    ]


def core_send(team, rows, pieces, half_rows, *others):
    sent = [spread(rows, step, pieces, half_rows) for step in range(1, team.sizes["tp"])]
    sent = fence(*sent, *others)[: len(sent)]
    return [team.ring(value, "tp", -step) for step, value in enumerate(sent, 1)]


def core_total(team, rows, pieces, half_rows, got):
    total, *sent = spread(rows, 0, pieces, half_rows, got, team.members)
    return total, sent


def team_send_direct(team, sent):
    return [
        team.shift(value, offset, back=True) for value, offset in zip(sent, team.offsets[1:])
    ]


def team_send(team, sent):
    xs = team.sizes["x"]
    across_x = [(0, dx) for dx in range(1, xs)]
    far = sent[xs - 1].astype(WIDE)
    for value, offset in zip(sent[xs:], across_x):
        far = far + team.shift(value, offset, back=True).astype(WIDE)
    got = [team.shift(value, offset, back=True) for value, offset in zip(sent, across_x)]
    return got + [team.shift(far.astype(LOWER), (1, 0), back=True)]


def team_total(own, got):
    for value in got:
        own = own + value.astype(WIDE)
    return own


def put(buffer, value, starts):
    return lax.dynamic_update_slice(buffer, value, starts)


def share_columns(team, shards):
    widths = [shard.shape[1] // team.members for shard in shards]
    pieces = []
    for j, offset in enumerate(team.offsets):
        slot = team.slot(offset, back=False)
        cuts = [
            lax.dynamic_slice_in_dim(shard, slot * each, each, 1)
            for shard, each in zip(shards, widths)
        ]
        piece = jnp.concatenate(cuts, axis=1)
        pieces.append(team.shift(piece, offset) if j > 0 else piece)
    return pieces


def place_rows_kernel(widths, slots_ref, *refs):
    pieces, outs = refs[: len(refs) - len(widths)], refs[len(refs) - len(widths) :]
    for j, piece in enumerate(pieces):
        height = piece.shape[0]
        row = pl.multiple_of(slots_ref[j] * height, height)
        first = 0
        for out, width in zip(outs, widths):
            out[pl.ds(row, height), :] = piece[:, first : first + width]
            first += width


def place_columns_kernel(widths, slots_ref, *refs):
    pieces, outs = refs[: len(refs) - len(widths)], refs[len(refs) - len(widths) :]
    for j, piece in enumerate(pieces):
        first = 0
        for out, width in zip(outs, widths):
            column = pl.multiple_of(slots_ref[j] * width, width)
            block = piece[:, first : first + width].astype(out.dtype)
            out[:, pl.ds(column, width)] = block
            first += width


def place(team, kernel, pieces, widths, shapes):
    slots = jnp.stack([team.slot(offset) for offset in team.offsets]).astype(jnp.int32)
    whole = [pl.BlockSpec(piece.shape, lambda n: (0, 0)) for piece in pieces]
    return pl.pallas_call(
        kernel if widths is None else functools.partial(kernel, widths),
        grid=(1,),
        in_specs=[pl.BlockSpec(memory_space=pltpu.SMEM)] + whole,
        out_specs=[pl.BlockSpec(shape.shape, lambda n: (0, 0)) for shape in shapes],
        out_shape=shapes,
        cost_estimate=LIGHT,
        compiler_params=KERNEL,
    )(slots, *pieces)


def stack_rows_kernel(*refs):
    height = refs[0].shape[0]
    for j, piece in enumerate(refs[:-1]):
        refs[-1][j * height : (j + 1) * height, :] = piece[...]


def stack_rows(pieces):
    height, width = pieces[0].shape
    rows = height * len(pieces)
    return pl.pallas_call(
        stack_rows_kernel,
        grid=(1,),
        in_specs=[pl.BlockSpec((height, width), lambda n: (0, 0)) for _ in pieces],
        out_specs=pl.BlockSpec((rows, width), lambda n: (0, 0)),
        out_shape=jax.ShapeDtypeStruct((rows, width), pieces[0].dtype),
        cost_estimate=LIGHT,
        compiler_params=KERNEL,
    )(*pieces)


def place_halves_kernel(slots_ref, *refs):
    pieces, outs = refs[:-2], refs[-2:]
    split = len(pieces) // 2
    for j, piece in enumerate(pieces):
        height = piece.shape[0]
        for part, out in enumerate(outs):

            @pl.when(lax.div(slots_ref[j], split) == part)
            def _():
                row = pl.multiple_of(lax.rem(slots_ref[j], split) * height, height)
                out[pl.ds(row, height), :] = piece[...]


def near_rows(team, pieces, parts=1):
    height, width = pieces[0].shape
    shape = jax.ShapeDtypeStruct((height * team.members // parts, width), LOWER)
    if parts == 1:
        return place(team, place_rows_kernel, pieces, [width], [shape])
    return place(team, place_halves_kernel, pieces, None, [shape] * 2)


def across(team, value):
    return [team.ring(value, "h", -step) for step in range(1, team.sizes["h"])]


def beside(team, values):
    return [team.ring(value, "y", 1) for value in values]


def halves(value):
    middle = value.shape[0] // 2
    return value[:middle], value[middle:]


def pairs(firsts, seconds):
    return [part for pair in zip(firsts, seconds) for part in pair]


def add_ring(team, value, name):
    return value + sum(team.ring(value, name, step) for step in range(1, team.sizes[name]))


class Grads:
    def __init__(self, team, lefts, rights):
        self.team, self.lefts, self.rights = team, lefts, rights
        self.far = lefts[0].shape[1] // 2
        self.near = self.far // team.sizes["h"]

        self.half = self.near // 2
        self.steps = range(1, team.sizes["h"])

    def rows(self, first, count, adds=(), offset=0, column=0):
        return outer(self.lefts, self.rights, first, count, adds, offset, column)

    def send_far(self):
        return self.rows(self.far + self.near, self.far - self.near)

    def send_half(self, part):
        start = self.far + part * self.half
        return [self.rows(start + step * self.near, self.half) for step in self.steps]

    def send_near(self):
        return self.rows(self.far, self.near)

    def cross(self, got):
        offsets = [(step - 1) * self.near for step in self.steps]
        return [self.rows(self.near + first, self.near, [got], first) for first in offsets]

    def cross_half(self, part, got):
        offsets = [(step - 1) * self.near + part * self.half for step in self.steps]
        return [self.rows(self.near + first, self.half, [got], first) for first in offsets]

    def cross_halves(self, part, gots):
        start = part * self.half
        return [
            self.rows(start + step * self.near, self.half, [got])
            for step, got in zip(self.steps, gots)
        ]

    def go(self, sent):
        return [self.team.ring(value, "h", step) for step, value in zip(self.steps, sent)]

    def total(self, got, crossed, column=0):
        return self.rows(0, self.near, [got, *crossed], column=column)


def home_pieces(team, total):
    height = total.shape[0] // team.members
    total = total.reshape(team.members, height, -1)
    pieces = []
    for j, offset in enumerate(team.offsets):
        piece = lax.dynamic_index_in_dim(total, team.slot(offset, back=False), 0, False)
        pieces.append(team.shift(piece, offset) if j > 0 else piece)
    return pieces


def home_join(team, pieces, widths):
    height = pieces[0].shape[0]
    shapes = [jax.ShapeDtypeStruct((height, width * team.members), WIDE) for width in widths]
    return place(team, place_columns_kernel, pieces, widths, shapes)


def permute_kernel(count, table_ref, value_ref, out_ref):
    block = value_ref.shape[1] // count
    for i in range(count):
        column = pl.multiple_of(table_ref[i] * block, block)
        out_ref[:, i * block : (i + 1) * block] = value_ref[:, pl.ds(column, block)]


def permute_columns(value, table):
    whole = pl.BlockSpec(value.shape, lambda n: (0, 0))
    return pl.pallas_call(
        functools.partial(permute_kernel, len(table)),
        grid=(1,),
        in_specs=[pl.BlockSpec(memory_space=pltpu.SMEM), whole],
        out_specs=whole,
        out_shape=jax.ShapeDtypeStruct(value.shape, value.dtype),
        cost_estimate=LIGHT,
    )(jnp.stack(table).astype(jnp.int32), value)


def to_team_order(team, value):
    hs = team.sizes["h"]
    table = []
    for dy in range(2):
        for dh in range(hs):
            for l in range(2):
                h, y = modulo(team.at["h"] + dh, hs), modulo(team.at["y"] + dy, 2)
                table.append((h * 2 + l) * 2 + y)
    return permute_columns(value, table)


def from_team_order(team, value):
    hs = team.sizes["h"]
    table = []
    for h in range(hs):
        for l in range(2):
            for y in range(2):
                dh, dy = modulo(h - team.at["h"] + hs, hs), modulo(y - team.at["y"] + 2, 2)
                table.append((dy * hs + dh) * 2 + l)
    return permute_columns(value, table)


def pick(table, index):
    ids = jnp.arange(table.shape[0], dtype=jnp.int32)
    return jnp.sum(jnp.where(ids == index, table, 0))


def choose(pieces, index):
    out = pieces[0]
    for i in range(1, len(pieces)):
        out = jnp.where(index == i, pieces[i], out)
    return out


def spread_h(team, piece):
    return [piece] + [team.ring(piece, "h", step) for step in range(1, team.sizes["h"])]


def deal_flip(team, piece, flip):
    if flip == 0:
        return swap_home(piece)
    perm = [(l * 2 + y, y * 2 + 1 - l) for l in range(2) for y in range(2)]
    with jax.named_scope("flip"):
        return lax.ppermute(piece, ("l", "y"), perm)


def deal_across(team, two):
    first = swapped_home(team, two[0], two[1])
    chosen = [jnp.where(need, first, two[2]) for need in team.needs]
    return chosen[:1] + [team.ring(value, "h", step) for step, value in enumerate(chosen) if step]


def dealt_in(team, pieces):
    return choose(pieces, team.in_step)


def deal(team, pieces):
    first, second = (choose(pieces, step) for step in team.out_steps)
    return first, swap_home(first), second


def deal_second(value):
    perm = [(l * 2 + y, (1 - y) * 2 + l) for l in range(2) for y in range(2)]
    return lax.ppermute(value, ("l", "y"), perm)


def dealt_out(team, got):
    return jnp.where(team.out_first, swapped_home(team, got[0], got[1]), got[2])


def join_cores(team, piece):
    ts = team.sizes["tp"]
    out = jnp.zeros((ts,) + piece.shape, piece.dtype)
    for step in range(ts):
        other = team.ring(piece, "tp", step) if step else piece
        out = put(out, other[None], (modulo(team.at["tp"] - step + ts, ts), 0, 0))
    return out.reshape(-1, piece.shape[-1])


def layer_norm(inputs, gain_vec, shift_vec):
    row_mean = jnp.mean(inputs, axis=-1, keepdims=True)
    centred = inputs - row_mean
    spread = jnp.mean(centred * centred, axis=-1, keepdims=True)
    rate = lax.rsqrt(spread + EPSILON)
    xhat = centred * rate
    return xhat * gain_vec + shift_vec, xhat, rate


def layer_norm_back(grad, gain_vec, xhat, rate):
    scaled = grad * gain_vec
    return rate * (
        scaled
        - jnp.mean(scaled, axis=-1, keepdims=True)
        - xhat * jnp.mean(scaled * xhat, axis=-1, keepdims=True)
    )


def gelu_tanh(inputs):
    return jax.nn.gelu(inputs, approximate=True)


def masked_scores(key_ref, query, limits_ref, scale):
    count = limits_ref.shape[0]
    height = key_ref.shape[0] // count
    blocks = []
    for j in range(count):
        block = mm_nt(key_ref[j * height : (j + 1) * height, :], query) * scale
        row = lax.broadcasted_iota(jnp.int32, block.shape, 0)
        blocks.append(jnp.where(row < limits_ref[j], block, NEGATIVE))
    return blocks


def attend_kernel(scale, limits_ref, query_ref, key_ref, value_ref, out_ref, log_ref):
    blocks = masked_scores(key_ref, query_ref[...], limits_ref, scale)
    row_max = functools.reduce(jnp.maximum, blocks)
    row_max = jnp.max(row_max, axis=0, keepdims=True)
    blocks = [jnp.exp(block - row_max) for block in blocks]
    total = jnp.sum(functools.reduce(jnp.add, blocks), axis=0, keepdims=True)
    inverse = 1.0 / total
    height = key_ref.shape[0] // len(blocks)
    out = None
    for j, block in enumerate(blocks):
        value = value_ref[j * height : (j + 1) * height, :]
        term = mm_tn(value, (block * inverse).astype(LOWER))
        out = term if out is None else out + term
    out_ref[...] = out.T.astype(LOWER)
    log_ref[0] = row_max + jnp.log(total)


def attend_back_kernel(
    scale, wide, limits_ref, query_ref, key_ref, value_ref, grad_ref, log_ref, out_ref, key_sum, value_sum
):
    head, step = pl.program_id(0), pl.program_id(1)
    query, grad = query_ref[...], grad_ref[...]
    blocks = masked_scores(key_ref, query, limits_ref, scale)
    count = len(blocks)
    height = key_ref.shape[0] // count
    part = [slice(j * height, (j + 1) * height) for j in range(count)]
    log_sum = log_ref[0]
    probs = [jnp.exp(block - log_sum) for block in blocks]
    grad_probs = [mm_nt(value_ref[rows, :], grad) for rows in part]
    delta = functools.reduce(jnp.add, [p * g for p, g in zip(probs, grad_probs)])
    delta = jnp.sum(delta, axis=0, keepdims=True)

    @pl.when(step == 0)
    def _():
        key_sum[...] = jnp.zeros_like(key_sum)
        value_sum[...] = jnp.zeros_like(value_sum)

    grad_query = None
    for j, rows in enumerate(part):
        scores = (probs[j] * (grad_probs[j] - delta)).astype(LOWER)
        term = mm_tn(key_ref[rows, :], scores)
        grad_query = term if grad_query is None else grad_query + term
        key_sum[rows, :] += mm(scores, query)
        value_sum[rows, :] += mm(probs[j].astype(LOWER), grad)
    count = query.shape[0]
    first = pl.multiple_of(step * count, count)
    column = pl.multiple_of(head * HEAD, HEAD)
    out_ref[pl.ds(first, count), pl.ds(column, HEAD)] = (grad_query.T * scale).astype(LOWER)

    @pl.when(step == pl.num_programs(1) - 1)
    def _():
        out_ref[:, pl.ds(wide + column, HEAD)] = (key_sum[...] * scale).astype(LOWER)
        out_ref[:, pl.ds(2 * wide + column, HEAD)] = value_sum[...].astype(LOWER)


LIGHT = pl.CostEstimate(flops=1000000, bytes_accessed=100000, transcendentals=0)
KERNEL = pltpu.CompilerParams(vmem_limit_bytes=16 * 1024 * 1024)


def gelu_slope(value):
    inner = math.sqrt(2.0 / math.pi)
    square = value * value
    tanh = jnp.tanh(inner * value * (1.0 + 0.044715 * square))
    return 0.5 * (1.0 + tanh) + 0.5 * value * (1.0 - tanh * tanh) * inner * (
        1.0 + 3.0 * 0.044715 * square
    )


def project_kernel(mode, part_count, piece_count, steps, *refs):
    parts, pieces = refs[:part_count], refs[part_count : part_count + piece_count]
    rest = refs[part_count + piece_count :]
    index = pl.program_id(0)

    def run(rows):
        total = None
        first = 0
        for piece in pieces:
            depth = piece.shape[0]
            term = mm(rows[:, first : first + depth], piece[...])
            total = term if total is None else total + term
            first += depth
        if mode == "bias":
            rest[1][...] = (total + rest[0][...]).astype(LOWER)
        elif mode == "gelu":
            total = total + rest[0][...]
            rest[1][...] = total
            rest[2][...] = gelu_tanh(total).astype(LOWER)
        elif mode == "slope":
            rest[1][...] = (total * gelu_slope(rest[0][...])).astype(LOWER)
        else:
            rest[0][...] = total.astype(LOWER)

    for place in range(part_count):

        @pl.when(index // steps == place)
        def _():
            run(parts[place][...])


def project(mode, parts, pieces, width, extra=None):
    half_rows, depth = parts[0].shape
    block = min(256, half_rows)
    steps = half_rows // block
    rows = half_rows * len(parts)

    def part_at(place):
        return lambda i: (jnp.clip(i - place * steps, 0, steps - 1), 0)

    in_specs = [pl.BlockSpec((block, depth), part_at(place)) for place in range(len(parts))]
    for array, column in pieces:
        in_specs.append(
            pl.BlockSpec((array.shape[0], width), functools.partial(lambda c, i: (0, c), column))
        )
    arrays = list(parts) + [array for array, _ in pieces]
    tile = pl.BlockSpec((block, width), lambda i: (i, 0))
    if mode in ("bias", "gelu"):
        in_specs.append(pl.BlockSpec((1, width), lambda i: (0, 0)))
        arrays.append(extra[None])
    elif mode == "slope":
        in_specs.append(tile)
        arrays.append(extra)
    shapes = [jax.ShapeDtypeStruct((rows, width), LOWER)]
    if mode == "gelu":
        shapes = [jax.ShapeDtypeStruct((rows, width), WIDE)] + shapes
    return pl.pallas_call(
        functools.partial(project_kernel, mode, len(parts), len(pieces), steps),
        grid=(len(parts) * steps,),
        in_specs=in_specs,
        out_specs=[tile] * len(shapes),
        out_shape=shapes,
        cost_estimate=LIGHT,
        compiler_params=KERNEL,
    )(*arrays)


def spread_kernel(piece_count, got_count, members, rows_ref, *refs):
    pieces, gots = refs[:piece_count], refs[piece_count : piece_count + got_count]
    outs = refs[piece_count + got_count :]
    rows = rows_ref[...]
    height = rows.shape[0] // members
    first = 0
    for piece in pieces:
        columns = slice(first, first + piece.shape[0])
        total = mm_nt(rows, piece[...])
        for got in gots:
            total = total + got[:, columns].astype(WIDE)
        for j, out in enumerate(outs):
            out[:, columns] = total[j * height : (j + 1) * height].astype(out.dtype)
        first += piece.shape[0]


def spread(rows, place, pieces, half_rows, got=(), members=0):
    if isinstance(rows, (list, tuple)):
        rows, place = rows[place], 0
    depth = rows.shape[1]
    width = sum(array.shape[0] for array, _ in pieces)
    in_specs = [pl.BlockSpec((half_rows, depth), lambda n: (place, 0))]
    for array, column in pieces:
        in_specs.append(
            pl.BlockSpec((array.shape[0], depth), functools.partial(lambda c, n: (0, c), column))
        )
    in_specs += [pl.BlockSpec((half_rows, width), lambda n: (0, 0))] * len(got)
    split = max(members, 1)
    height = half_rows // split
    dtypes = [WIDE] + [LOWER] * (members - 1) if members else [LOWER]
    out = pl.pallas_call(
        functools.partial(spread_kernel, len(pieces), len(got), split),
        grid=(1,),
        in_specs=in_specs,
        out_specs=[pl.BlockSpec((height, width), lambda n: (0, 0))] * split,
        out_shape=[jax.ShapeDtypeStruct((height, width), dtype) for dtype in dtypes],
        cost_estimate=LIGHT,
        compiler_params=KERNEL,
    )(rows, *[array for array, _ in pieces], *got)
    return out if members else out[0]


def outer_kernel(part_count, add_count, *refs):
    lefts, rights = refs[:part_count], refs[part_count : 2 * part_count]
    adds, out = refs[2 * part_count : 2 * part_count + add_count], refs[-1]
    total = None
    for left, right in zip(lefts, rights):
        term = mm_tn(left[...], right[...])
        total = term if total is None else total + term
    for add in adds:
        total = total + add[...].astype(WIDE)
    out[...] = total.astype(out.dtype)


def outer(lefts, rights, first, count, adds, offset, column):
    height = lefts[0].shape[0]
    rights = [right if isinstance(right, tuple) else (right, 0) for right in rights]
    width = rights[0][0].shape[1]
    block = math.gcd(256, count)
    in_specs = [pl.BlockSpec((height, block), lambda i: (0, first // block + i)) for _ in lefts]
    for _, row in rights:
        in_specs.append(
            pl.BlockSpec((height, width), functools.partial(lambda r, i: (r, 0), row))
        )
    tile = pl.BlockSpec((block, width), lambda i: (i, 0))
    add_tile = pl.BlockSpec((block, width), lambda i: (offset // block + i, 0))
    first_tile = pl.BlockSpec((block, width), lambda i: (offset // block + i, column))
    return pl.pallas_call(
        functools.partial(outer_kernel, len(lefts), len(adds)),
        grid=(count // block,),
        in_specs=in_specs + [first_tile] * len(adds[:1]) + [add_tile] * len(adds[1:]),
        out_specs=tile,
        out_shape=jax.ShapeDtypeStruct((count, width), LOWER),
        cost_estimate=LIGHT,
        compiler_params=KERNEL,
    )(*lefts, *[right for right, _ in rights], *adds)


def query_block(rows):
    return min(512, rows)


def attend(qkv, limits, scale):
    rows, wide = qkv.shape[0], qkv.shape[1] // 3
    heads, block = wide // HEAD, query_block(rows)
    return pl.pallas_call(
        functools.partial(attend_kernel, scale),
        grid=(heads, rows // block),
        in_specs=[
            pl.BlockSpec(memory_space=pltpu.SMEM),
            pl.BlockSpec((block, HEAD), lambda h, i: (i, h)),
            pl.BlockSpec((rows, HEAD), lambda h, i: (0, heads + h)),
            pl.BlockSpec((rows, HEAD), lambda h, i: (0, 2 * heads + h)),
        ],
        out_specs=[
            pl.BlockSpec((block, HEAD), lambda h, i: (i, h)),
            pl.BlockSpec((1, 1, block), lambda h, i: (h, 0, i)),
        ],
        out_shape=[
            jax.ShapeDtypeStruct((rows, wide), LOWER),
            jax.ShapeDtypeStruct((heads, 1, rows), WIDE),
        ],
        cost_estimate=LIGHT,
        compiler_params=KERNEL,
    )(limits, qkv, qkv, qkv)


def attend_back(qkv, grad, log_sum, limits, scale):
    rows, wide = grad.shape
    heads, block = wide // HEAD, query_block(rows)
    return pl.pallas_call(
        functools.partial(attend_back_kernel, scale, wide),
        grid=(heads, rows // block),
        in_specs=[
            pl.BlockSpec(memory_space=pltpu.SMEM),
            pl.BlockSpec((block, HEAD), lambda h, i: (i, h)),
            pl.BlockSpec((rows, HEAD), lambda h, i: (0, heads + h)),
            pl.BlockSpec((rows, HEAD), lambda h, i: (0, 2 * heads + h)),
            pl.BlockSpec((block, HEAD), lambda h, i: (i, h)),
            pl.BlockSpec((1, 1, block), lambda h, i: (h, 0, i)),
        ],
        out_specs=pl.BlockSpec((rows, 3 * wide), lambda h, i: (0, 0)),
        out_shape=jax.ShapeDtypeStruct((rows, 3 * wide), LOWER),
        scratch_shapes=[pltpu.VMEM((rows, HEAD), WIDE), pltpu.VMEM((rows, HEAD), WIDE)],
        cost_estimate=LIGHT,
        compiler_params=KERNEL,
    )(limits, qkv, qkv, qkv, grad, log_sum)


def local(
    tokens,
    lengths,
    dealing,
    w_query,
    w_key,
    w_value,
    w_out,
    b_query,
    b_value,
    b_out,
    gain_mid,
    shift_mid,
    w_up,
    b_up,
    w_down,
    b_down,
    gain_end,
    shift_end,
    cotangent,
):
    team = Team()
    ts, members = team.sizes["tp"], team.members
    row_count = tokens.shape[0] // ts
    wide = w_query.shape[1] // members
    tall = w_up.shape[1] // members
    width = tokens.shape[1]
    score_scale = 1.0 / math.sqrt(HEAD)
    my_slot = team.at["l"] * team.sizes["x"] + team.at["x"]
    seq_ids = jnp.arange(dealing.shape[0], dtype=jnp.int32)
    home = jnp.sum(jnp.where(dealing[None, :] == seq_ids[:, None], seq_ids[None, :], 0), axis=1)
    plan = team.plan(dealing, home)
    team.set_plan(plan)
    live_count = pick(lengths, team.at["h"] * 2 + team.at["y"])
    limits = live_count - jnp.stack(row_blocks(team)).astype(jnp.int32) * row_count
    query_live = (jnp.arange(row_count, dtype=jnp.int32) < limits[0])[:, None]
    half_at = team.at["tp"] * row_count

    half_rows = members * row_count
    vectors = jnp.stack([b_out, gain_mid, shift_mid, b_down, gain_end, shift_end])
    b_out, gain_mid, shift_mid, b_down, gain_end, shift_end = to_team_order(team, vectors)
    bias_q = lax.dynamic_slice_in_dim(b_query, my_slot * wide, wide, 0)
    bias_v = lax.dynamic_slice_in_dim(b_value, my_slot * wide, wide, 0)
    bias_up = lax.dynamic_slice_in_dim(b_up, my_slot * tall, tall, 0)
    bias_qkv = jnp.concatenate([bias_q, jnp.zeros_like(bias_q), bias_v])
    steps = team.sizes["h"] - 1
    team_count = team.sizes["x"]


    def first_column(arrays):
        return [(array, 0) for array in arrays]

    with jax.named_scope("a0"):
        mine = lax.dynamic_slice_in_dim(tokens, half_at, row_count, 0)
        own = swap_home(mine)
        share = share_columns(team, [w_query, w_key, w_value, w_out])
        own, w_up, w_down, bias_qkv, bias_up, limits, query_live, *rest = fence(
            own, w_up, w_down, bias_qkv, bias_up, limits, query_live, *share, *plan
        )
        share, plan = rest[:members], rest[members:]
        team.set_plan(plan)
    with jax.named_scope("a1"):
        own = to_team_order(team, swapped_home(team, mine, own))
        (near_att,) = near_rows(team, share)
        pieces = team_pieces(team, own)
        cross_qkv = across(team, near_att[:, : 3 * wide])
        (side_att,) = beside(team, [near_att])
        near_att, w_up, w_down, cotangent, side_att, *rest = fence(
            near_att, w_up, w_down, cotangent, side_att, *pieces, *cross_qkv
        )
        pieces, cross_qkv = rest[:members], rest[members:]
    with jax.named_scope("a2"):
        half = stack_rows(pieces)
        other = cores(team, half)
        far_qkv = beside(team, cross_qkv)
        cross_out = across(team, near_att[:, 3 * wide :])
        share = share_columns(team, [w_up])
        cotangent, w_down, *rest = fence(
            cotangent, w_down, half, *other, *share, *far_qkv, *cross_out
        )
        in_parts = rest[:ts]
        share, rest = rest[ts : ts + members], rest[ts + members :]
        far_qkv, cross_out = rest[:steps], rest[steps:]
    qkv_mat = first_column([near_att, *cross_qkv, side_att, *far_qkv])
    with jax.named_scope("c1"):
        up_a, up_b = near_rows(team, share, 2)
        cross_up_a = across(team, up_a)
        far_out = beside(team, cross_out)
        cot_half = lax.dynamic_slice_in_dim(cotangent, half_at, row_count, 0)
        share = share_columns(team, [w_down])
        (qkv,) = project("bias", in_parts, qkv_mat, 3 * wide, bias_qkv)
        attended, log_sum = attend(qkv, limits, score_scale)
        out_mat = [(near_att, 3), *first_column(cross_out), (side_att, 3), *first_column(far_out)]
        got = core_send(team, attended, out_mat, half_rows, *cross_up_a, *share)
        total, sent = core_total(team, attended, out_mat, half_rows, got)
        up_a, up_b, cot_half, *rest = fence(
            up_a, up_b, cot_half, *cross_up_a, *share, *sent
        )
        cross_up_a, rest = rest[:steps], rest[steps:]
        share, sent = rest[:members], rest[members:]
    with jax.named_scope("s3"):
        got = team_send(team, sent)
        cross_up_b = across(team, up_b)
        down_a, down_b = near_rows(team, share, 2)
        side = beside(team, [jnp.concatenate([up_a, *cross_up_a], axis=0)])
        cot_one = deal_flip(team, cot_half, 0)
        cot_half, cot_one, up_b, down_a, down_b, *rest = fence(
            cot_half, cot_one, up_b, down_a, down_b, *got, *cross_up_b, *side
        )
        got, rest = rest[:team_count], rest[team_count:]
        cross_up_b, side_a = rest[:steps], rest[steps]
    with jax.named_scope("s4"):
        branch = team_total(total, got) + b_out
        middle, mid_hat, mid_rate = layer_norm(own.astype(WIDE) + branch, gain_mid, shift_mid)
        pieces = team_pieces(team, middle.astype(LOWER))
        cross_down_a = across(team, down_a)
        side = beside(team, [jnp.concatenate([up_b, *cross_up_b], axis=0)])
        cot_two = [cot_half, cot_one, deal_flip(team, cot_half, 1)]
        down_a, down_b, *rest = fence(
            down_a, down_b, *cot_two, *pieces, *cross_down_a, *side
        )
        cot_two, rest = rest[:3], rest[3:]
        pieces, rest = rest[:members], rest[members:]
        cross_down_a, side_b = rest[:steps], rest[steps]
    part_rows = down_a.shape[0]

    def split_side(side):
        blocks = [side[k * part_rows : (k + 1) * part_rows] for k in range(steps + 1)]
        return blocks[0], blocks[1:]

    side_up_a, far_up_a = split_side(side_a)
    side_up_b, far_up_b = split_side(side_b)
    up_mat = first_column(
        [up_a, up_b]
        + pairs(cross_up_a, cross_up_b)
        + [side_up_a, side_up_b]
        + pairs(far_up_a, far_up_b)
    )
    with jax.named_scope("c2"):
        half = stack_rows(pieces)
        other = cores(team, half)
        cross_down_b = across(team, down_b)
        side = beside(team, [jnp.concatenate([down_a, *cross_down_a], axis=0)])
        mid_parts = [half] + other
        hidden, active = [], []
        for part in mid_parts:
            hidden_part, active_part = project("gelu", [part], up_mat, tall, bias_up)
            hidden.append(hidden_part)
            active.append(active_part)
        down_b, *rest = fence(down_b, *active, *cross_down_b, *side, *cot_two)
        active, rest = rest[:ts], rest[ts:]
        cross_down_b, side, cot_two = rest[:steps], rest[steps], rest[steps + 1 :]
        side_down_a, far_down_a = split_side(side)
    with jax.named_scope("s5"):
        (side,) = beside(team, [jnp.concatenate([down_b, *cross_down_b], axis=0)])
        side_down_b, far_down_b = split_side(side)
        cot_pieces = deal_across(team, cot_two)
        down_mat = first_column(
            [down_a, down_b]
            + pairs(cross_down_a, cross_down_b)
            + [side_down_a, side_down_b]
            + pairs(far_down_a, far_down_b)
        )
        got = core_send(team, active, down_mat, half_rows, *cot_pieces)
        total, sent = core_total(team, active, down_mat, half_rows, got)
        rest = fence(*sent, *cot_pieces)
        sent, cot_pieces = rest[: members - 1], rest[members - 1 :]
    with jax.named_scope("s6"):
        cot = to_team_order(team, dealt_in(team, cot_pieces))
        cot, *got = fence(cot, *team_send_direct(team, sent))
    with jax.named_scope("s7"):
        result = team_total(total, got) + b_down
        normed, end_hat, end_rate = layer_norm(middle + result, gain_end, shift_end)
        output_own = jnp.where(query_live, normed, 0.0).astype(LOWER)
        grad_normed = jnp.where(query_live, cot.astype(WIDE), 0.0)
        grad_sum = layer_norm_back(grad_normed, gain_end, end_hat, end_rate)
        grad_result = grad_sum.astype(LOWER)
        pieces = team_pieces(team, grad_result)
        out_pieces = spread_h(team, from_team_order(team, output_own))
        rest = fence(*pieces, *out_pieces)
        pieces, out_pieces = rest[:members], rest[members:]
        grad_gend = jnp.sum(grad_normed * end_hat, axis=0)
        grad_send = jnp.sum(grad_normed, axis=0)
        grad_bdown = jnp.sum(grad_result.astype(WIDE), axis=0)
    with jax.named_scope("c3"):
        half = stack_rows(pieces)
        other = cores(team, half)
        result_parts = [half] + other
        flow_down = Grads(team, result_parts, active)
        far_down_a = beside(team, flow_down.send_half(0))
        grad_hidden = []
        for part, hidden_part in zip(result_parts, hidden):
            grad_hidden += project("slope", [part], down_mat, tall, hidden_part)
        got = core_send(team, grad_hidden, up_mat, half_rows, *far_down_a, *grad_hidden)
        total, sent = core_total(team, grad_hidden, up_mat, half_rows, got)
        cross_down = flow_down.cross_halves(0, far_down_a)
        flow_up = Grads(team, mid_parts, grad_hidden)
        rest = fence(*sent, *cross_down)
        sent, cross_down = rest[: members - 1], rest[members - 1 :]
    with jax.named_scope("s8"):
        got = team_send(team, sent)
        got_down_a = flow_down.go(cross_down)
        far_down_b = beside(team, flow_down.send_half(1))
        far_up, *far_down_b = fence(flow_up.send_far(), *far_down_b)
        (far_up,) = beside(team, [far_up])
        cross_down = flow_down.cross_halves(1, far_down_b)
        far_up, *rest = fence(far_up, *got, *got_down_a, *cross_down)
        got, rest = rest[:team_count], rest[team_count:]
        got_down_a, cross_down = rest[:steps], rest[steps:]
    with jax.named_scope("s9"):
        grad_middle = team_total(total, got) + grad_sum
        grad_inner = layer_norm_back(grad_middle, gain_mid, mid_hat, mid_rate)
        grad_branch = grad_inner.astype(LOWER)
        pieces = team_pieces(team, grad_branch)
        got_down_b = flow_down.go(cross_down)
        (near_down,) = beside(team, [flow_down.send_near()])
        grad_gmid = jnp.sum(grad_middle * mid_hat, axis=0)
        grad_smid = jnp.sum(grad_middle, axis=0)
        grad_bout = jnp.sum(grad_branch.astype(WIDE), axis=0)
        by_row = jnp.stack([grad_bout, grad_gmid, grad_smid, grad_bdown, grad_gend, grad_send])
        by_row = add_ring(team, from_team_order(team, by_row), "tp")
        out_first, out_swapped, out_second = deal(team, out_pieces)
        cross_up_a, cross_up_b = flow_up.cross_half(0, far_up), flow_up.cross_half(1, far_up)
        by_row, near_down, out_first, out_swapped, out_second, *rest = fence(
            by_row, near_down, out_first, out_swapped, out_second, *pieces, *got_down_b, *cross_up_a, *cross_up_b)
        pieces, rest = rest[:members], rest[members:]
        got_down_b, rest = rest[:steps], rest[steps:]
        cross_up_a, cross_up_b = rest[:steps], rest[steps:]
    with jax.named_scope("c4"):
        half = stack_rows(pieces)
        other = cores(team, half)
        got_up_a, got_up_b = flow_up.go(cross_up_a), flow_up.go(cross_up_b)
        out_two = [out_first, out_swapped, deal_second(out_second)]
        branch_parts = [half] + other
        attended_parts = [(attended, k) for k in range(ts)]
        flow_out = Grads(team, branch_parts, attended_parts)
        (far_out,) = beside(team, [flow_out.send_far()])
        (grad_attended,) = project("plain", branch_parts, out_mat, wide)
        grad_qkv = attend_back(qkv, grad_attended, log_sum, limits, score_scale)
        got = core_send(team, grad_qkv, qkv_mat, half_rows, far_out, *got_up_a, *out_two)
        total, sent = core_total(team, grad_qkv, qkv_mat, half_rows, got)
        grad_parts = [(grad_qkv, k) for k in range(ts)]
        flow_qkv = Grads(team, in_parts, grad_parts)
        qkv_sum = jnp.sum(grad_qkv.astype(WIDE), axis=0)
        grad_bup = sum(jnp.sum(part.astype(WIDE), axis=0) for part in grad_hidden)
        zeros = jnp.zeros((members, 1), WIDE)
        by_slot = [
            put(zeros * part[None], part[None], (my_slot, 0)).reshape(-1)
            for part in (qkv_sum[:wide], qkv_sum[2 * wide :], grad_bup)
        ]
        sums = jnp.concatenate([by_row.reshape(-1)] + by_slot).reshape(-1, 128)
        sums = add_ring(team, sums, "x")
        (far_qkv,) = beside(team, [flow_qkv.send_far()])
        cross_out = flow_out.cross(far_out)
        sums, near_down, far_qkv, *rest = fence(
            sums, near_down, far_qkv, *cross_out, *sent, *got_up_a, *got_up_b, *out_two
        )
        cross_out, rest = rest[:steps], rest[steps:]
        sent, rest = rest[: members - 1], rest[members - 1 :]
        got_up_a, got_up_b, out_two = rest[:steps], rest[steps : 2 * steps], rest[2 * steps :]
    with jax.named_scope("s10"):
        got = team_send(team, sent)
        total_down = flow_down.total(
            near_down,
            [jnp.concatenate(both, axis=0) for both in zip(got_down_a, got_down_b)],
        )
        got_qkv_a = flow_qkv.go(flow_qkv.cross_half(0, far_qkv))
        cross_qkv = flow_qkv.cross_half(1, far_qkv)
        (near_up,) = beside(team, [flow_up.send_near()])
        sums, total_down, near_up, *rest = fence(
            sums, total_down, near_up, *out_two, *got, *got_qkv_a, *cross_qkv, *cross_out
        )
        out_two, rest = rest[:3], rest[3:]
        got, rest = rest[:team_count], rest[team_count:]
        got_qkv_a, cross_qkv, cross_out = rest[:steps], rest[steps : 2 * steps], rest[2 * steps :]
    with jax.named_scope("s11"):
        got_qkv_b = flow_qkv.go(cross_qkv)
        got_out = flow_out.go(cross_out)
        grad_own = (team_total(total, got) + grad_inner).astype(LOWER)
        grad_own = from_team_order(team, grad_own)
        swapped = swap_home(grad_own)
        near_att = jnp.concatenate([flow_qkv.send_near(), flow_out.send_near()], axis=1)
        (near_att,) = beside(team, [near_att])
        total_up = flow_up.total(
            near_up, [jnp.concatenate(both, axis=0) for both in zip(got_up_a, got_up_b)]
        )
        home_both = home_pieces(team, jnp.concatenate([total_down, total_up], axis=1))
        total_out = flow_out.total(near_att, got_out, 3)
        got_qkv = [jnp.concatenate(both, axis=0) for both in zip(got_qkv_a, got_qkv_b)]
        total_qkv = flow_qkv.total(near_att, got_qkv, 0)
        sums, swapped, total_out, total_qkv, *rest = fence(
            sums, swapped, total_out, total_qkv, *home_both, *out_two
        )
        home_both, out_two = rest[:members], rest[members:]
        grad_down, grad_up = home_join(team, home_both, [tall, tall])
    with jax.named_scope("s12"):
        grad_tokens = join_cores(team, swapped_home(team, grad_own, swapped))
        home_att = home_pieces(team, jnp.concatenate([total_qkv, total_out], axis=1))
        output = join_cores(team, dealt_out(team, out_two))
        sums = add_ring(
            team, add_ring(team, add_ring(team, sums, "h"), "y"), "l"
        ).reshape(-1)
        grad_query, grad_key, grad_value, grad_out = home_join(team, home_att, [wide] * 4)
    smalls = []
    first = 0
    for size in [width] * 6 + [b_query.shape[0], b_value.shape[0], b_up.shape[0]]:
        smalls.append(sums[first : first + size])
        first += size
    return (
        output,
        grad_tokens,
        grad_query,
        grad_key,
        grad_value,
        grad_out,
        smalls[6],
        smalls[7],
        smalls[0],
        smalls[1],
        smalls[2],
        grad_up,
        smalls[8],
        grad_down,
        smalls[3],
        smalls[4],
        smalls[5],
    )


def solution(mesh):
    fsdp, ctx, tp = (mesh.shape[name] for name in ("fsdp", "ctx", "tp"))
    fine = Mesh(mesh.devices.reshape(fsdp // 2, 2, 2, ctx // 2, tp), ROWS + ("tp",))
    rows, split = P(ROWS, None), P(ROWS, "tp")
    in_specs = (
        (rows, P(), P())
        + (split,) * 4
        + (P("tp"), P("tp"), P(), P(), P(), split, P("tp"), split, P(), P(), P(), rows)
    )
    out_specs = (
        (rows, rows)
        + (split,) * 4
        + (P("tp"), P("tp"), P(), P(), P(), split, P("tp"), split, P(), P(), P())
    )
    return jax.shard_map(local, mesh=fine, in_specs=in_specs, out_specs=out_specs, check_vma=False)
```

```python
import functools
import math

import jax
import jax.numpy as jnp
from jax import lax
from jax.experimental import pallas as pl
from jax.experimental.pallas import tpu as pltpu
from jax.sharding import Mesh
from jax.sharding import PartitionSpec as P

HEAD = 128
EPSILON = 1e-12
NEGATIVE = -1e30
WIDE = jnp.float32
LOWER = jnp.bfloat16

TEAM = ("l", "x")
ROWS = ("h", "l", "y", "x")


def dot(left, right, dims):
    return lax.dot_general(left, right, (dims, ((), ())), preferred_element_type=WIDE)


def mm(left, right):
    return dot(left, right, ((1,), (0,)))


def mm_nt(left, right):
    return dot(left, right, ((1,), (1,)))


def mm_tn(left, right):
    return dot(left, right, ((0,), (0,)))


def modulo(value, size):
    if isinstance(size, int) and size & (size - 1) == 0:
        return jnp.bitwise_and(value, size - 1)
    return lax.rem(value, size)


class Team:
    def __init__(self):
        self.sizes = {name: lax.axis_size(name) for name in ROWS + ("tp",)}
        self.at = {name: lax.axis_index(name) for name in ROWS + ("tp",)}
        ls, xs = self.sizes["l"], self.sizes["x"]
        self.offsets = [(dl, dx) for dl in range(ls) for dx in range(xs)]
        self.members = ls * xs

    def shift(self, value, offset, back=False):
        with jax.named_scope("team%d%d" % offset):
            return self.shift_(value, offset, back)

    def shift_(self, value, offset, back):
        ls, xs = self.sizes["l"], self.sizes["x"]
        dl, dx = offset
        if back:
            dl, dx = -dl, -dx
        perm = [
            (l * xs + x, ((l + dl) % ls) * xs + (x + dx) % xs) for l in range(ls) for x in range(xs)
        ]
        return lax.ppermute(value, TEAM, perm)

    def ring(self, value, name, step):
        size = self.sizes[name]
        with jax.named_scope("ring_" + name):
            return lax.ppermute(value, name, [(i, (i + step) % size) for i in range(size)])

    def slot(self, offset, back=True):
        return self.slots[back][self.offsets.index(offset)]

    def plan(self, dealing, home):
        hs, h, l, y = self.sizes["h"], self.at["h"], self.at["l"], self.at["y"]
        own = pick(home, h * 2 + y)
        needs = [
            modulo(pick(home, modulo(h + step, hs) * 2 + y), 2) == y for step in range(hs)
        ]
        sources = [pick(dealing, h * 2 + target) for target in (y, 1 - y)]
        steps = [modulo(h - lax.shift_right_logical(source, 1) + hs, hs) for source in sources]
        here = pick(dealing, h * 2 + l)
        return (
            [self.slot_(offset, back) for back in (False, True) for offset in self.offsets]
            + [l == y, modulo(h - lax.shift_right_logical(own, 1) + hs, hs), modulo(here, 2) == l]
            + steps
            + needs
        )

    def set_plan(self, plan):
        self.slots = {False: plan[: self.members], True: plan[self.members : 2 * self.members]}
        rest = plan[2 * self.members :]
        self.same, self.in_step, self.out_first = rest[:3]
        self.out_steps, self.needs = rest[3:5], rest[5:]

    def slot_(self, offset, back):
        ls, xs = self.sizes["l"], self.sizes["x"]
        dl, dx = offset
        if back:
            dl, dx = -dl, -dx
        return modulo(self.at["l"] + dl + ls, ls) * xs + modulo(self.at["x"] + dx + xs, xs)


def fence(*values):
    return lax.optimization_barrier(values)


def swap_home(value):
    return lax.ppermute(value, ("l", "y"), [(1, 2), (2, 1)])


def swapped_home(team, value, moved):
    return jnp.where(team.same, value, moved)


def team_pieces(team, piece):
    far = team.shift(piece, (1, 0))
    across_x = [(0, dx) for dx in range(1, team.sizes["x"])]
    return (
        [piece]
        + [team.shift(piece, offset) for offset in across_x]
        + [far]
        + [team.shift(far, offset) for offset in across_x]
    )


def cores(team, value):
    return [team.ring(value, "tp", step) for step in range(1, team.sizes["tp"])]


def row_blocks(team):
    ts = team.sizes["tp"]
    return [
        team.slot(offset) * ts + modulo(team.at["tp"] - step + ts, ts)
        for step in range(ts)
        for offset in team.offsets
    ]


def core_send(team, rows, pieces, half_rows, *others):
    sent = [spread(rows, step, pieces, half_rows) for step in range(1, team.sizes["tp"])]
    sent = fence(*sent, *others)[: len(sent)]
    return [team.ring(value, "tp", -step) for step, value in enumerate(sent, 1)]


def core_total(team, rows, pieces, half_rows, got):
    total, *sent = spread(rows, 0, pieces, half_rows, got, team.members)
    return total, sent


def team_send_direct(team, sent):
    return [
        team.shift(value, offset, back=True) for value, offset in zip(sent, team.offsets[1:])
    ]


def team_send(team, sent):
    xs = team.sizes["x"]
    across_x = [(0, dx) for dx in range(1, xs)]
    far = sent[xs - 1].astype(WIDE)
    for value, offset in zip(sent[xs:], across_x):
        far = far + team.shift(value, offset, back=True).astype(WIDE)
    got = [team.shift(value, offset, back=True) for value, offset in zip(sent, across_x)]
    return got + [team.shift(far.astype(LOWER), (1, 0), back=True)]


def team_total(own, got):
    for value in got:
        own = own + value.astype(WIDE)
    return own


def put(buffer, value, starts):
    return lax.dynamic_update_slice(buffer, value, starts)


def share_columns(team, shards):
    widths = [shard.shape[1] // team.members for shard in shards]
    pieces = []
    for j, offset in enumerate(team.offsets):
        slot = team.slot(offset, back=False)
        cuts = [
            lax.dynamic_slice_in_dim(shard, slot * each, each, 1)
            for shard, each in zip(shards, widths)
        ]
        piece = jnp.concatenate(cuts, axis=1)
        pieces.append(team.shift(piece, offset) if j > 0 else piece)
    return pieces


def place_rows_kernel(widths, slots_ref, *refs):
    pieces, outs = refs[: len(refs) - len(widths)], refs[len(refs) - len(widths) :]
    for j, piece in enumerate(pieces):
        height = piece.shape[0]
        row = pl.multiple_of(slots_ref[j] * height, height)
        first = 0
        for out, width in zip(outs, widths):
            out[pl.ds(row, height), :] = piece[:, first : first + width]
            first += width


def place_columns_kernel(widths, slots_ref, *refs):
    pieces, outs = refs[: len(refs) - len(widths)], refs[len(refs) - len(widths) :]
    for j, piece in enumerate(pieces):
        first = 0
        for out, width in zip(outs, widths):
            column = pl.multiple_of(slots_ref[j] * width, width)
            block = piece[:, first : first + width].astype(out.dtype)
            out[:, pl.ds(column, width)] = block
            first += width


def place(team, kernel, pieces, widths, shapes):
    slots = jnp.stack([team.slot(offset) for offset in team.offsets]).astype(jnp.int32)
    whole = [pl.BlockSpec(piece.shape, lambda n: (0, 0)) for piece in pieces]
    return pl.pallas_call(
        kernel if widths is None else functools.partial(kernel, widths),
        grid=(1,),
        in_specs=[pl.BlockSpec(memory_space=pltpu.SMEM)] + whole,
        out_specs=[pl.BlockSpec(shape.shape, lambda n: (0, 0)) for shape in shapes],
        out_shape=shapes,
        cost_estimate=LIGHT,
        compiler_params=KERNEL,
    )(slots, *pieces)


def stack_rows_kernel(*refs):
    height = refs[0].shape[0]
    for j, piece in enumerate(refs[:-1]):
        refs[-1][j * height : (j + 1) * height, :] = piece[...]


def stack_rows(pieces):
    height, width = pieces[0].shape
    rows = height * len(pieces)
    return pl.pallas_call(
        stack_rows_kernel,
        grid=(1,),
        in_specs=[pl.BlockSpec((height, width), lambda n: (0, 0)) for _ in pieces],
        out_specs=pl.BlockSpec((rows, width), lambda n: (0, 0)),
        out_shape=jax.ShapeDtypeStruct((rows, width), pieces[0].dtype),
        cost_estimate=LIGHT,
        compiler_params=KERNEL,
    )(*pieces)


def place_halves_kernel(slots_ref, *refs):
    pieces, outs = refs[:-2], refs[-2:]
    split = len(pieces) // 2
    for j, piece in enumerate(pieces):
        height = piece.shape[0]
        for part, out in enumerate(outs):

            @pl.when(lax.div(slots_ref[j], split) == part)
            def _():
                row = pl.multiple_of(lax.rem(slots_ref[j], split) * height, height)
                out[pl.ds(row, height), :] = piece[...]


def near_rows(team, pieces, parts=1):
    height, width = pieces[0].shape
    shape = jax.ShapeDtypeStruct((height * team.members // parts, width), LOWER)
    if parts == 1:
        return place(team, place_rows_kernel, pieces, [width], [shape])
    return place(team, place_halves_kernel, pieces, None, [shape] * 2)


def across(team, value):
    return [team.ring(value, "h", -step) for step in range(1, team.sizes["h"])]


def beside(team, values):
    return [team.ring(value, "y", 1) for value in values]


def halves(value):
    middle = value.shape[0] // 2
    return value[:middle], value[middle:]


def pairs(firsts, seconds):
    return [part for pair in zip(firsts, seconds) for part in pair]


def add_ring(team, value, name):
    return value + sum(team.ring(value, name, step) for step in range(1, team.sizes[name]))


class Grads:
    def __init__(self, team, lefts, rights):
        self.team, self.lefts, self.rights = team, lefts, rights
        self.far = lefts[0].shape[1] // 2
        self.near = self.far // team.sizes["h"]

        self.half = self.near // 2
        self.steps = range(1, team.sizes["h"])

    def rows(self, first, count, adds=(), offset=0, column=0):
        return outer(self.lefts, self.rights, first, count, adds, offset, column)

    def send_far(self):
        return self.rows(self.far + self.near, self.far - self.near)

    def send_half(self, part):
        start = self.far + part * self.half
        return [self.rows(start + step * self.near, self.half) for step in self.steps]

    def send_near(self):
        return self.rows(self.far, self.near)

    def cross(self, got):
        offsets = [(step - 1) * self.near for step in self.steps]
        return [self.rows(self.near + first, self.near, [got], first) for first in offsets]

    def cross_half(self, part, got):
        offsets = [(step - 1) * self.near + part * self.half for step in self.steps]
        return [self.rows(self.near + first, self.half, [got], first) for first in offsets]

    def cross_halves(self, part, gots):
        start = part * self.half
        return [
            self.rows(start + step * self.near, self.half, [got])
            for step, got in zip(self.steps, gots)
        ]

    def go(self, sent):
        return [self.team.ring(value, "h", step) for step, value in zip(self.steps, sent)]

    def total(self, got, crossed, column=0):
        return self.rows(0, self.near, [got, *crossed], column=column)


def home_pieces(team, total):
    height = total.shape[0] // team.members
    total = total.reshape(team.members, height, -1)
    pieces = []
    for j, offset in enumerate(team.offsets):
        piece = lax.dynamic_index_in_dim(total, team.slot(offset, back=False), 0, False)
        pieces.append(team.shift(piece, offset) if j > 0 else piece)
    return pieces


def home_join(team, pieces, widths):
    height = pieces[0].shape[0]
    shapes = [jax.ShapeDtypeStruct((height, width * team.members), WIDE) for width in widths]
    return place(team, place_columns_kernel, pieces, widths, shapes)


def permute_kernel(count, table_ref, value_ref, out_ref):
    block = value_ref.shape[1] // count
    for i in range(count):
        column = pl.multiple_of(table_ref[i] * block, block)
        out_ref[:, i * block : (i + 1) * block] = value_ref[:, pl.ds(column, block)]


def permute_columns(value, table):
    whole = pl.BlockSpec(value.shape, lambda n: (0, 0))
    return pl.pallas_call(
        functools.partial(permute_kernel, len(table)),
        grid=(1,),
        in_specs=[pl.BlockSpec(memory_space=pltpu.SMEM), whole],
        out_specs=whole,
        out_shape=jax.ShapeDtypeStruct(value.shape, value.dtype),
        cost_estimate=LIGHT,
    )(jnp.stack(table).astype(jnp.int32), value)


def to_team_order(team, value):
    hs = team.sizes["h"]
    table = []
    for dy in range(2):
        for dh in range(hs):
            for l in range(2):
                h, y = modulo(team.at["h"] + dh, hs), modulo(team.at["y"] + dy, 2)
                table.append((h * 2 + l) * 2 + y)
    return permute_columns(value, table)


def from_team_order(team, value):
    hs = team.sizes["h"]
    table = []
    for h in range(hs):
        for l in range(2):
            for y in range(2):
                dh, dy = modulo(h - team.at["h"] + hs, hs), modulo(y - team.at["y"] + 2, 2)
                table.append((dy * hs + dh) * 2 + l)
    return permute_columns(value, table)


def pick(table, index):
    ids = jnp.arange(table.shape[0], dtype=jnp.int32)
    return jnp.sum(jnp.where(ids == index, table, 0))


def choose(pieces, index):
    out = pieces[0]
    for i in range(1, len(pieces)):
        out = jnp.where(index == i, pieces[i], out)
    return out


def spread_h(team, piece):
    return [piece] + [team.ring(piece, "h", step) for step in range(1, team.sizes["h"])]


def deal_flip(team, piece, flip):
    if flip == 0:
        return swap_home(piece)
    perm = [(l * 2 + y, y * 2 + 1 - l) for l in range(2) for y in range(2)]
    with jax.named_scope("flip"):
        return lax.ppermute(piece, ("l", "y"), perm)


def deal_across(team, two):
    first = swapped_home(team, two[0], two[1])
    chosen = [jnp.where(need, first, two[2]) for need in team.needs]
    return chosen[:1] + [team.ring(value, "h", step) for step, value in enumerate(chosen) if step]


def dealt_in(team, pieces):
    return choose(pieces, team.in_step)


def deal(team, pieces):
    first, second = (choose(pieces, step) for step in team.out_steps)
    return first, swap_home(first), second


def deal_second(value):
    perm = [(l * 2 + y, (1 - y) * 2 + l) for l in range(2) for y in range(2)]
    return lax.ppermute(value, ("l", "y"), perm)


def dealt_out(team, got):
    return jnp.where(team.out_first, swapped_home(team, got[0], got[1]), got[2])


def join_cores(team, piece):
    ts = team.sizes["tp"]
    out = jnp.zeros((ts,) + piece.shape, piece.dtype)
    for step in range(ts):
        other = team.ring(piece, "tp", step) if step else piece
        out = put(out, other[None], (modulo(team.at["tp"] - step + ts, ts), 0, 0))
    return out.reshape(-1, piece.shape[-1])


def layer_norm(inputs, gain_vec, shift_vec):
    row_mean = jnp.mean(inputs, axis=-1, keepdims=True)
    centred = inputs - row_mean
    spread = jnp.mean(centred * centred, axis=-1, keepdims=True)
    rate = lax.rsqrt(spread + EPSILON)
    xhat = centred * rate
    return xhat * gain_vec + shift_vec, xhat, rate


def layer_norm_back(grad, gain_vec, xhat, rate):
    scaled = grad * gain_vec
    return rate * (
        scaled
        - jnp.mean(scaled, axis=-1, keepdims=True)
        - xhat * jnp.mean(scaled * xhat, axis=-1, keepdims=True)
    )


def gelu_tanh(inputs):
    return jax.nn.gelu(inputs, approximate=True)


def masked_scores(key_ref, query, limits_ref, scale):
    count = limits_ref.shape[0]
    height = key_ref.shape[0] // count
    blocks = []
    for j in range(count):
        block = mm_nt(key_ref[j * height : (j + 1) * height, :], query) * scale
        row = lax.broadcasted_iota(jnp.int32, block.shape, 0)
        blocks.append(jnp.where(row < limits_ref[j], block, NEGATIVE))
    return blocks


def attend_kernel(scale, limits_ref, query_ref, key_ref, value_ref, out_ref, log_ref):
    blocks = masked_scores(key_ref, query_ref[...], limits_ref, scale)
    row_max = functools.reduce(jnp.maximum, blocks)
    row_max = jnp.max(row_max, axis=0, keepdims=True)
    blocks = [jnp.exp(block - row_max) for block in blocks]
    total = jnp.sum(functools.reduce(jnp.add, blocks), axis=0, keepdims=True)
    inverse = 1.0 / total
    height = key_ref.shape[0] // len(blocks)
    out = None
    for j, block in enumerate(blocks):
        value = value_ref[j * height : (j + 1) * height, :]
        term = mm_tn(value, (block * inverse).astype(LOWER))
        out = term if out is None else out + term
    out_ref[...] = out.T.astype(LOWER)
    log_ref[0] = row_max + jnp.log(total)


def attend_back_kernel(
    scale, wide, limits_ref, query_ref, key_ref, value_ref, grad_ref, log_ref, out_ref, key_sum, value_sum
):
    head, step = pl.program_id(0), pl.program_id(1)
    query, grad = query_ref[...], grad_ref[...]
    blocks = masked_scores(key_ref, query, limits_ref, scale)
    count = len(blocks)
    height = key_ref.shape[0] // count
    part = [slice(j * height, (j + 1) * height) for j in range(count)]
    log_sum = log_ref[0]
    probs = [jnp.exp(block - log_sum) for block in blocks]
    grad_probs = [mm_nt(value_ref[rows, :], grad) for rows in part]
    delta = functools.reduce(jnp.add, [p * g for p, g in zip(probs, grad_probs)])
    delta = jnp.sum(delta, axis=0, keepdims=True)

    @pl.when(step == 0)
    def _():
        key_sum[...] = jnp.zeros_like(key_sum)
        value_sum[...] = jnp.zeros_like(value_sum)

    grad_query = None
    for j, rows in enumerate(part):
        scores = (probs[j] * (grad_probs[j] - delta)).astype(LOWER)
        term = mm_tn(key_ref[rows, :], scores)
        grad_query = term if grad_query is None else grad_query + term
        key_sum[rows, :] += mm(scores, query)
        value_sum[rows, :] += mm(probs[j].astype(LOWER), grad)
    count = query.shape[0]
    first = pl.multiple_of(step * count, count)
    column = pl.multiple_of(head * HEAD, HEAD)
    out_ref[pl.ds(first, count), pl.ds(column, HEAD)] = (grad_query.T * scale).astype(LOWER)

    @pl.when(step == pl.num_programs(1) - 1)
    def _():
        out_ref[:, pl.ds(wide + column, HEAD)] = (key_sum[...] * scale).astype(LOWER)
        out_ref[:, pl.ds(2 * wide + column, HEAD)] = value_sum[...].astype(LOWER)


LIGHT = pl.CostEstimate(flops=1000000, bytes_accessed=100000, transcendentals=0)
KERNEL = pltpu.CompilerParams(vmem_limit_bytes=16 * 1024 * 1024)


def gelu_slope(value):
    inner = math.sqrt(2.0 / math.pi)
    square = value * value
    tanh = jnp.tanh(inner * value * (1.0 + 0.044715 * square))
    return 0.5 * (1.0 + tanh) + 0.5 * value * (1.0 - tanh * tanh) * inner * (
        1.0 + 3.0 * 0.044715 * square
    )


def project_kernel(mode, part_count, piece_count, steps, *refs):
    parts, pieces = refs[:part_count], refs[part_count : part_count + piece_count]
    rest = refs[part_count + piece_count :]
    index = pl.program_id(0)

    def run(rows):
        total = None
        first = 0
        for piece in pieces:
            depth = piece.shape[0]
            term = mm(rows[:, first : first + depth], piece[...])
            total = term if total is None else total + term
            first += depth
        if mode == "bias":
            rest[1][...] = (total + rest[0][...]).astype(LOWER)
        elif mode == "gelu":
            total = total + rest[0][...]
            rest[1][...] = total
            rest[2][...] = gelu_tanh(total).astype(LOWER)
        elif mode == "slope":
            rest[1][...] = (total * gelu_slope(rest[0][...])).astype(LOWER)
        else:
            rest[0][...] = total.astype(LOWER)

    for place in range(part_count):

        @pl.when(index // steps == place)
        def _():
            run(parts[place][...])


def project(mode, parts, pieces, width, extra=None):
    half_rows, depth = parts[0].shape
    block = min(256, half_rows)
    steps = half_rows // block
    rows = half_rows * len(parts)

    def part_at(place):
        return lambda i: (jnp.clip(i - place * steps, 0, steps - 1), 0)

    in_specs = [pl.BlockSpec((block, depth), part_at(place)) for place in range(len(parts))]
    for array, column in pieces:
        in_specs.append(
            pl.BlockSpec((array.shape[0], width), functools.partial(lambda c, i: (0, c), column))
        )
    arrays = list(parts) + [array for array, _ in pieces]
    tile = pl.BlockSpec((block, width), lambda i: (i, 0))
    if mode in ("bias", "gelu"):
        in_specs.append(pl.BlockSpec((1, width), lambda i: (0, 0)))
        arrays.append(extra[None])
    elif mode == "slope":
        in_specs.append(tile)
        arrays.append(extra)
    shapes = [jax.ShapeDtypeStruct((rows, width), LOWER)]
    if mode == "gelu":
        shapes = [jax.ShapeDtypeStruct((rows, width), WIDE)] + shapes
    return pl.pallas_call(
        functools.partial(project_kernel, mode, len(parts), len(pieces), steps),
        grid=(len(parts) * steps,),
        in_specs=in_specs,
        out_specs=[tile] * len(shapes),
        out_shape=shapes,
        cost_estimate=LIGHT,
        compiler_params=KERNEL,
    )(*arrays)


def spread_kernel(piece_count, got_count, members, rows_ref, *refs):
    pieces, gots = refs[:piece_count], refs[piece_count : piece_count + got_count]
    outs = refs[piece_count + got_count :]
    rows = rows_ref[...]
    height = rows.shape[0] // members
    first = 0
    for piece in pieces:
        columns = slice(first, first + piece.shape[0])
        total = mm_nt(rows, piece[...])
        for got in gots:
            total = total + got[:, columns].astype(WIDE)
        for j, out in enumerate(outs):
            out[:, columns] = total[j * height : (j + 1) * height].astype(out.dtype)
        first += piece.shape[0]


def spread(rows, place, pieces, half_rows, got=(), members=0):
    if isinstance(rows, (list, tuple)):
        rows, place = rows[place], 0
    depth = rows.shape[1]
    width = sum(array.shape[0] for array, _ in pieces)
    in_specs = [pl.BlockSpec((half_rows, depth), lambda n: (place, 0))]
    for array, column in pieces:
        in_specs.append(
            pl.BlockSpec((array.shape[0], depth), functools.partial(lambda c, n: (0, c), column))
        )
    in_specs += [pl.BlockSpec((half_rows, width), lambda n: (0, 0))] * len(got)
    split = max(members, 1)
    height = half_rows // split
    dtypes = [WIDE] + [LOWER] * (members - 1) if members else [LOWER]
    out = pl.pallas_call(
        functools.partial(spread_kernel, len(pieces), len(got), split),
        grid=(1,),
        in_specs=in_specs,
        out_specs=[pl.BlockSpec((height, width), lambda n: (0, 0))] * split,
        out_shape=[jax.ShapeDtypeStruct((height, width), dtype) for dtype in dtypes],
        cost_estimate=LIGHT,
        compiler_params=KERNEL,
    )(rows, *[array for array, _ in pieces], *got)
    return out if members else out[0]


def outer_kernel(part_count, add_count, *refs):
    lefts, rights = refs[:part_count], refs[part_count : 2 * part_count]
    adds, out = refs[2 * part_count : 2 * part_count + add_count], refs[-1]
    total = None
    for left, right in zip(lefts, rights):
        term = mm_tn(left[...], right[...])
        total = term if total is None else total + term
    for add in adds:
        total = total + add[...].astype(WIDE)
    out[...] = total.astype(out.dtype)


def outer(lefts, rights, first, count, adds, offset, column):
    height = lefts[0].shape[0]
    rights = [right if isinstance(right, tuple) else (right, 0) for right in rights]
    width = rights[0][0].shape[1]
    block = math.gcd(256, count)
    in_specs = [pl.BlockSpec((height, block), lambda i: (0, first // block + i)) for _ in lefts]
    for _, row in rights:
        in_specs.append(
            pl.BlockSpec((height, width), functools.partial(lambda r, i: (r, 0), row))
        )
    tile = pl.BlockSpec((block, width), lambda i: (i, 0))
    add_tile = pl.BlockSpec((block, width), lambda i: (offset // block + i, 0))
    first_tile = pl.BlockSpec((block, width), lambda i: (offset // block + i, column))
    return pl.pallas_call(
        functools.partial(outer_kernel, len(lefts), len(adds)),
        grid=(count // block,),
        in_specs=in_specs + [first_tile] * len(adds[:1]) + [add_tile] * len(adds[1:]),
        out_specs=tile,
        out_shape=jax.ShapeDtypeStruct((count, width), LOWER),
        cost_estimate=LIGHT,
        compiler_params=KERNEL,
    )(*lefts, *[right for right, _ in rights], *adds)


def query_block(rows):
    return min(512, rows)


def attend(qkv, limits, scale):
    rows, wide = qkv.shape[0], qkv.shape[1] // 3
    heads, block = wide // HEAD, query_block(rows)
    return pl.pallas_call(
        functools.partial(attend_kernel, scale),
        grid=(heads, rows // block),
        in_specs=[
            pl.BlockSpec(memory_space=pltpu.SMEM),
            pl.BlockSpec((block, HEAD), lambda h, i: (i, h)),
            pl.BlockSpec((rows, HEAD), lambda h, i: (0, heads + h)),
            pl.BlockSpec((rows, HEAD), lambda h, i: (0, 2 * heads + h)),
        ],
        out_specs=[
            pl.BlockSpec((block, HEAD), lambda h, i: (i, h)),
            pl.BlockSpec((1, 1, block), lambda h, i: (h, 0, i)),
        ],
        out_shape=[
            jax.ShapeDtypeStruct((rows, wide), LOWER),
            jax.ShapeDtypeStruct((heads, 1, rows), WIDE),
        ],
        cost_estimate=LIGHT,
        compiler_params=KERNEL,
    )(limits, qkv, qkv, qkv)


def attend_back(qkv, grad, log_sum, limits, scale):
    rows, wide = grad.shape
    heads, block = wide // HEAD, query_block(rows)
    return pl.pallas_call(
        functools.partial(attend_back_kernel, scale, wide),
        grid=(heads, rows // block),
        in_specs=[
            pl.BlockSpec(memory_space=pltpu.SMEM),
            pl.BlockSpec((block, HEAD), lambda h, i: (i, h)),
            pl.BlockSpec((rows, HEAD), lambda h, i: (0, heads + h)),
            pl.BlockSpec((rows, HEAD), lambda h, i: (0, 2 * heads + h)),
            pl.BlockSpec((block, HEAD), lambda h, i: (i, h)),
            pl.BlockSpec((1, 1, block), lambda h, i: (h, 0, i)),
        ],
        out_specs=pl.BlockSpec((rows, 3 * wide), lambda h, i: (0, 0)),
        out_shape=jax.ShapeDtypeStruct((rows, 3 * wide), LOWER),
        scratch_shapes=[pltpu.VMEM((rows, HEAD), WIDE), pltpu.VMEM((rows, HEAD), WIDE)],
        cost_estimate=LIGHT,
        compiler_params=KERNEL,
    )(limits, qkv, qkv, qkv, grad, log_sum)


def local(
    tokens,
    lengths,
    dealing,
    w_query,
    w_key,
    w_value,
    w_out,
    b_query,
    b_value,
    b_out,
    gain_mid,
    shift_mid,
    w_up,
    b_up,
    w_down,
    b_down,
    gain_end,
    shift_end,
    cotangent,
):
    team = Team()
    ts, members = team.sizes["tp"], team.members
    row_count = tokens.shape[0] // ts
    wide = w_query.shape[1] // members
    tall = w_up.shape[1] // members
    width = tokens.shape[1]
    score_scale = 1.0 / math.sqrt(HEAD)
    my_slot = team.at["l"] * team.sizes["x"] + team.at["x"]
    seq_ids = jnp.arange(dealing.shape[0], dtype=jnp.int32)
    home = jnp.sum(jnp.where(dealing[None, :] == seq_ids[:, None], seq_ids[None, :], 0), axis=1)
    plan = team.plan(dealing, home)
    team.set_plan(plan)
    live_count = pick(lengths, team.at["h"] * 2 + team.at["y"])
    limits = live_count - jnp.stack(row_blocks(team)).astype(jnp.int32) * row_count
    query_live = (jnp.arange(row_count, dtype=jnp.int32) < limits[0])[:, None]
    half_at = team.at["tp"] * row_count

    half_rows = members * row_count
    vectors = jnp.stack([b_out, gain_mid, shift_mid, b_down, gain_end, shift_end])
    b_out, gain_mid, shift_mid, b_down, gain_end, shift_end = to_team_order(team, vectors)
    bias_q = lax.dynamic_slice_in_dim(b_query, my_slot * wide, wide, 0)
    bias_v = lax.dynamic_slice_in_dim(b_value, my_slot * wide, wide, 0)
    bias_up = lax.dynamic_slice_in_dim(b_up, my_slot * tall, tall, 0)
    bias_qkv = jnp.concatenate([bias_q, jnp.zeros_like(bias_q), bias_v])
    steps = team.sizes["h"] - 1
    team_count = team.sizes["x"]


    def first_column(arrays):
        return [(array, 0) for array in arrays]

    with jax.named_scope("a0"):
        mine = lax.dynamic_slice_in_dim(tokens, half_at, row_count, 0)
        own = swap_home(mine)
        w_query, w_key, w_value, w_out = fence(w_query, w_key, w_value, w_out, mine)[:4]
        share = share_columns(team, [w_query, w_key, w_value, w_out])
        own, w_up, w_down, bias_qkv, bias_up, limits, query_live, *rest = fence(
            own, w_up, w_down, bias_qkv, bias_up, limits, query_live, *share, *plan
        )
        share, plan = rest[:members], rest[members:]
        team.set_plan(plan)
    with jax.named_scope("a1"):
        own = to_team_order(team, swapped_home(team, mine, own))
        (near_att,) = near_rows(team, share)
        pieces = team_pieces(team, own)
        cross_qkv = across(team, near_att[:, : 3 * wide])
        (side_att,) = beside(team, [near_att])
        near_att, w_up, w_down, cotangent, side_att, *rest = fence(
            near_att, w_up, w_down, cotangent, side_att, *pieces, *cross_qkv
        )
        pieces, cross_qkv = rest[:members], rest[members:]
    with jax.named_scope("a2"):
        half = stack_rows(pieces)
        other = cores(team, half)
        far_qkv = beside(team, cross_qkv)
        cross_out = across(team, near_att[:, 3 * wide :])
        share = share_columns(team, [w_up])
        cotangent, w_down, *rest = fence(
            cotangent, w_down, half, *other, *share, *far_qkv, *cross_out
        )
        in_parts = rest[:ts]
        share, rest = rest[ts : ts + members], rest[ts + members :]
        far_qkv, cross_out = rest[:steps], rest[steps:]
    qkv_mat = first_column([near_att, *cross_qkv, side_att, *far_qkv])
    with jax.named_scope("c1"):
        up_a, up_b = near_rows(team, share, 2)
        cross_up_a = across(team, up_a)
        far_out = beside(team, cross_out)
        cot_half = lax.dynamic_slice_in_dim(cotangent, half_at, row_count, 0)
        share = share_columns(team, [w_down])
        (qkv,) = project("bias", in_parts, qkv_mat, 3 * wide, bias_qkv)
        attended, log_sum = attend(qkv, limits, score_scale)
        out_mat = [(near_att, 3), *first_column(cross_out), (side_att, 3), *first_column(far_out)]
        got = core_send(team, attended, out_mat, half_rows, *cross_up_a, *share)
        total, sent = core_total(team, attended, out_mat, half_rows, got)
        up_a, up_b, cot_half, *rest = fence(
            up_a, up_b, cot_half, *cross_up_a, *share, *sent
        )
        cross_up_a, rest = rest[:steps], rest[steps:]
        share, sent = rest[:members], rest[members:]
    with jax.named_scope("s3"):
        got = team_send(team, sent)
        cross_up_b = across(team, up_b)
        down_a, down_b = near_rows(team, share, 2)
        side = beside(team, [jnp.concatenate([up_a, *cross_up_a], axis=0)])
        cot_one = deal_flip(team, cot_half, 0)
        cot_half, cot_one, up_b, down_a, down_b, *rest = fence(
            cot_half, cot_one, up_b, down_a, down_b, *got, *cross_up_b, *side
        )
        got, rest = rest[:team_count], rest[team_count:]
        cross_up_b, side_a = rest[:steps], rest[steps]
    with jax.named_scope("s4"):
        branch = team_total(total, got) + b_out
        middle, mid_hat, mid_rate = layer_norm(own.astype(WIDE) + branch, gain_mid, shift_mid)
        pieces = team_pieces(team, middle.astype(LOWER))
        cross_down_a = across(team, down_a)
        side = beside(team, [jnp.concatenate([up_b, *cross_up_b], axis=0)])
        cot_two = [cot_half, cot_one, deal_flip(team, cot_half, 1)]
        down_a, down_b, *rest = fence(
            down_a, down_b, *cot_two, *pieces, *cross_down_a, *side
        )
        cot_two, rest = rest[:3], rest[3:]
        pieces, rest = rest[:members], rest[members:]
        cross_down_a, side_b = rest[:steps], rest[steps]
    part_rows = down_a.shape[0]

    def split_side(side):
        blocks = [side[k * part_rows : (k + 1) * part_rows] for k in range(steps + 1)]
        return blocks[0], blocks[1:]

    side_up_a, far_up_a = split_side(side_a)
    side_up_b, far_up_b = split_side(side_b)
    up_mat = first_column(
        [up_a, up_b]
        + pairs(cross_up_a, cross_up_b)
        + [side_up_a, side_up_b]
        + pairs(far_up_a, far_up_b)
    )
    with jax.named_scope("c2"):
        half = stack_rows(pieces)
        other = cores(team, half)
        cross_down_b = across(team, down_b)
        side = beside(team, [jnp.concatenate([down_a, *cross_down_a], axis=0)])
        mid_parts = [half] + other
        hidden, active = [], []
        for part in mid_parts:
            hidden_part, active_part = project("gelu", [part], up_mat, tall, bias_up)
            hidden.append(hidden_part)
            active.append(active_part)
        down_b, *rest = fence(down_b, *active, *cross_down_b, *side, *cot_two)
        active, rest = rest[:ts], rest[ts:]
        cross_down_b, side, cot_two = rest[:steps], rest[steps], rest[steps + 1 :]
        side_down_a, far_down_a = split_side(side)
    with jax.named_scope("s5"):
        (side,) = beside(team, [jnp.concatenate([down_b, *cross_down_b], axis=0)])
        side_down_b, far_down_b = split_side(side)
        cot_pieces = deal_across(team, cot_two)
        down_mat = first_column(
            [down_a, down_b]
            + pairs(cross_down_a, cross_down_b)
            + [side_down_a, side_down_b]
            + pairs(far_down_a, far_down_b)
        )
        got = core_send(team, active, down_mat, half_rows, *cot_pieces)
        total, sent = core_total(team, active, down_mat, half_rows, got)
        rest = fence(*sent, *cot_pieces)
        sent, cot_pieces = rest[: members - 1], rest[members - 1 :]
    with jax.named_scope("s6"):
        cot = to_team_order(team, dealt_in(team, cot_pieces))
        cot, *got = fence(cot, *team_send_direct(team, sent))
    with jax.named_scope("s7"):
        result = team_total(total, got) + b_down
        normed, end_hat, end_rate = layer_norm(middle + result, gain_end, shift_end)
        output_own = jnp.where(query_live, normed, 0.0).astype(LOWER)
        grad_normed = jnp.where(query_live, cot.astype(WIDE), 0.0)
        grad_sum = layer_norm_back(grad_normed, gain_end, end_hat, end_rate)
        grad_result = grad_sum.astype(LOWER)
        pieces = team_pieces(team, grad_result)
        out_pieces = spread_h(team, from_team_order(team, output_own))
        rest = fence(*pieces, *out_pieces)
        pieces, out_pieces = rest[:members], rest[members:]
        grad_gend = jnp.sum(grad_normed * end_hat, axis=0)
        grad_send = jnp.sum(grad_normed, axis=0)
        grad_bdown = jnp.sum(grad_result.astype(WIDE), axis=0)
    with jax.named_scope("c3"):
        half = stack_rows(pieces)
        other = cores(team, half)
        result_parts = [half] + other
        flow_down = Grads(team, result_parts, active)
        far_down_a = beside(team, flow_down.send_half(0))
        grad_hidden = []
        for part, hidden_part in zip(result_parts, hidden):
            grad_hidden += project("slope", [part], down_mat, tall, hidden_part)
        got = core_send(team, grad_hidden, up_mat, half_rows, *far_down_a, *grad_hidden)
        total, sent = core_total(team, grad_hidden, up_mat, half_rows, got)
        cross_down = flow_down.cross_halves(0, far_down_a)
        flow_up = Grads(team, mid_parts, grad_hidden)
        rest = fence(*sent, *cross_down)
        sent, cross_down = rest[: members - 1], rest[members - 1 :]
    with jax.named_scope("s8"):
        got = team_send(team, sent)
        got_down_a = flow_down.go(cross_down)
        far_down_b = beside(team, flow_down.send_half(1))
        far_up, *far_down_b = fence(flow_up.send_far(), *far_down_b)
        (far_up,) = beside(team, [far_up])
        cross_down = flow_down.cross_halves(1, far_down_b)
        far_up, *rest = fence(far_up, *got, *got_down_a, *cross_down)
        got, rest = rest[:team_count], rest[team_count:]
        got_down_a, cross_down = rest[:steps], rest[steps:]
    with jax.named_scope("s9"):
        grad_middle = team_total(total, got) + grad_sum
        grad_inner = layer_norm_back(grad_middle, gain_mid, mid_hat, mid_rate)
        grad_branch = grad_inner.astype(LOWER)
        pieces = team_pieces(team, grad_branch)
        got_down_b = flow_down.go(cross_down)
        (near_down,) = beside(team, [flow_down.send_near()])
        grad_gmid = jnp.sum(grad_middle * mid_hat, axis=0)
        grad_smid = jnp.sum(grad_middle, axis=0)
        grad_bout = jnp.sum(grad_branch.astype(WIDE), axis=0)
        by_row = jnp.stack([grad_bout, grad_gmid, grad_smid, grad_bdown, grad_gend, grad_send])
        by_row = add_ring(team, from_team_order(team, by_row), "tp")
        out_first, out_swapped, out_second = deal(team, out_pieces)
        cross_up_a, cross_up_b = flow_up.cross_half(0, far_up), flow_up.cross_half(1, far_up)
        by_row, near_down, out_first, out_swapped, out_second, *rest = fence(
            by_row, near_down, out_first, out_swapped, out_second, *pieces, *got_down_b, *cross_up_a, *cross_up_b)
        pieces, rest = rest[:members], rest[members:]
        got_down_b, rest = rest[:steps], rest[steps:]
        cross_up_a, cross_up_b = rest[:steps], rest[steps:]
    with jax.named_scope("c4"):
        half = stack_rows(pieces)
        other = cores(team, half)
        got_up_a, got_up_b = flow_up.go(cross_up_a), flow_up.go(cross_up_b)
        out_two = [out_first, out_swapped, deal_second(out_second)]
        branch_parts = [half] + other
        attended_parts = [(attended, k) for k in range(ts)]
        flow_out = Grads(team, branch_parts, attended_parts)
        (far_out,) = beside(team, [flow_out.send_far()])
        (grad_attended,) = project("plain", branch_parts, out_mat, wide)
        grad_qkv = attend_back(qkv, grad_attended, log_sum, limits, score_scale)
        got = core_send(team, grad_qkv, qkv_mat, half_rows, far_out, *got_up_a, *out_two)
        total, sent = core_total(team, grad_qkv, qkv_mat, half_rows, got)
        grad_parts = [(grad_qkv, k) for k in range(ts)]
        flow_qkv = Grads(team, in_parts, grad_parts)
        qkv_sum = jnp.sum(grad_qkv.astype(WIDE), axis=0)
        grad_bup = sum(jnp.sum(part.astype(WIDE), axis=0) for part in grad_hidden)
        zeros = jnp.zeros((members, 1), WIDE)
        by_slot = [
            put(zeros * part[None], part[None], (my_slot, 0)).reshape(-1)
            for part in (qkv_sum[:wide], qkv_sum[2 * wide :], grad_bup)
        ]
        sums = jnp.concatenate([by_row.reshape(-1)] + by_slot).reshape(-1, 128)
        sums = add_ring(team, sums, "x")
        (far_qkv,) = beside(team, [flow_qkv.send_far()])
        cross_out = flow_out.cross(far_out)
        sums, near_down, far_qkv, *rest = fence(
            sums, near_down, far_qkv, *cross_out, *sent, *got_up_a, *got_up_b, *out_two
        )
        cross_out, rest = rest[:steps], rest[steps:]
        sent, rest = rest[: members - 1], rest[members - 1 :]
        got_up_a, got_up_b, out_two = rest[:steps], rest[steps : 2 * steps], rest[2 * steps :]
    with jax.named_scope("s10"):
        got = team_send(team, sent)
        total_down = flow_down.total(
            near_down,
            [jnp.concatenate(both, axis=0) for both in zip(got_down_a, got_down_b)],
        )
        got_qkv_a = flow_qkv.go(flow_qkv.cross_half(0, far_qkv))
        cross_qkv = flow_qkv.cross_half(1, far_qkv)
        (near_up,) = beside(team, [flow_up.send_near()])
        sums, total_down, near_up, *rest = fence(
            sums, total_down, near_up, *out_two, *got, *got_qkv_a, *cross_qkv, *cross_out
        )
        out_two, rest = rest[:3], rest[3:]
        got, rest = rest[:team_count], rest[team_count:]
        got_qkv_a, cross_qkv, cross_out = rest[:steps], rest[steps : 2 * steps], rest[2 * steps :]
    with jax.named_scope("s11"):
        got_qkv_b = flow_qkv.go(cross_qkv)
        got_out = flow_out.go(cross_out)
        grad_own = (team_total(total, got) + grad_inner).astype(LOWER)
        grad_own = from_team_order(team, grad_own)
        swapped = swap_home(grad_own)
        near_att = jnp.concatenate([flow_qkv.send_near(), flow_out.send_near()], axis=1)
        (near_att,) = beside(team, [near_att])
        total_up = flow_up.total(
            near_up, [jnp.concatenate(both, axis=0) for both in zip(got_up_a, got_up_b)]
        )
        home_both = home_pieces(team, jnp.concatenate([total_down, total_up], axis=1))
        total_out = flow_out.total(near_att, got_out, 3)
        got_qkv = [jnp.concatenate(both, axis=0) for both in zip(got_qkv_a, got_qkv_b)]
        total_qkv = flow_qkv.total(near_att, got_qkv, 0)
        sums, swapped, total_out, total_qkv, *rest = fence(
            sums, swapped, total_out, total_qkv, *home_both, *out_two
        )
        home_both, out_two = rest[:members], rest[members:]
        grad_down, grad_up = home_join(team, home_both, [tall, tall])
    with jax.named_scope("s12"):
        grad_tokens = join_cores(team, swapped_home(team, grad_own, swapped))
        home_att = home_pieces(team, jnp.concatenate([total_qkv, total_out], axis=1))
        output = join_cores(team, dealt_out(team, out_two))
        sums = add_ring(
            team, add_ring(team, add_ring(team, sums, "h"), "y"), "l"
        ).reshape(-1)
        grad_query, grad_key, grad_value, grad_out = home_join(team, home_att, [wide] * 4)
    smalls = []
    first = 0
    for size in [width] * 6 + [b_query.shape[0], b_value.shape[0], b_up.shape[0]]:
        smalls.append(sums[first : first + size])
        first += size
    return (
        output,
        grad_tokens,
        grad_query,
        grad_key,
        grad_value,
        grad_out,
        smalls[6],
        smalls[7],
        smalls[0],
        smalls[1],
        smalls[2],
        grad_up,
        smalls[8],
        grad_down,
        smalls[3],
        smalls[4],
        smalls[5],
    )


def solution(mesh):
    fsdp, ctx, tp = (mesh.shape[name] for name in ("fsdp", "ctx", "tp"))
    fine = Mesh(mesh.devices.reshape(fsdp // 2, 2, 2, ctx // 2, tp), ROWS + ("tp",))
    rows, split = P(ROWS, None), P(ROWS, "tp")
    in_specs = (
        (rows, P(), P())
        + (split,) * 4
        + (P("tp"), P("tp"), P(), P(), P(), split, P("tp"), split, P(), P(), P(), rows)
    )
    out_specs = (
        (rows, rows)
        + (split,) * 4
        + (P("tp"), P("tp"), P(), P(), P(), split, P("tp"), split, P(), P(), P())
    )
    return jax.shard_map(local, mesh=fine, in_specs=in_specs, out_specs=out_specs, check_vma=False)
```

```python
import functools
import math

import jax
import jax.numpy as jnp
from jax import lax
from jax.experimental import pallas as pl
from jax.experimental.pallas import tpu as pltpu
from jax.sharding import Mesh
from jax.sharding import PartitionSpec as P

HEAD = 128
EPSILON = 1e-12
NEGATIVE = -1e30
WIDE = jnp.float32
LOWER = jnp.bfloat16

TEAM = ("l", "x")
ROWS = ("h", "l", "y", "x")


def dot(left, right, dims):
    return lax.dot_general(left, right, (dims, ((), ())), preferred_element_type=WIDE)


def mm(left, right):
    return dot(left, right, ((1,), (0,)))


def mm_nt(left, right):
    return dot(left, right, ((1,), (1,)))


def mm_tn(left, right):
    return dot(left, right, ((0,), (0,)))


def modulo(value, size):
    if isinstance(size, int) and size & (size - 1) == 0:
        return jnp.bitwise_and(value, size - 1)
    return lax.rem(value, size)


class Team:
    def __init__(self):
        self.sizes = {name: lax.axis_size(name) for name in ROWS + ("tp",)}
        self.at = {name: lax.axis_index(name) for name in ROWS + ("tp",)}
        ls, xs = self.sizes["l"], self.sizes["x"]
        self.offsets = [(dl, dx) for dl in range(ls) for dx in range(xs)]
        self.members = ls * xs

    def shift(self, value, offset, back=False):
        with jax.named_scope("team%d%d" % offset):
            return self.shift_(value, offset, back)

    def shift_(self, value, offset, back):
        ls, xs = self.sizes["l"], self.sizes["x"]
        dl, dx = offset
        if back:
            dl, dx = -dl, -dx
        perm = [
            (l * xs + x, ((l + dl) % ls) * xs + (x + dx) % xs) for l in range(ls) for x in range(xs)
        ]
        return lax.ppermute(value, TEAM, perm)

    def ring(self, value, name, step):
        size = self.sizes[name]
        with jax.named_scope("ring_" + name):
            return lax.ppermute(value, name, [(i, (i + step) % size) for i in range(size)])

    def slot(self, offset, back=True):
        return self.slots[back][self.offsets.index(offset)]

    def plan(self, dealing, home):
        hs, h, l, y = self.sizes["h"], self.at["h"], self.at["l"], self.at["y"]
        own = pick(home, h * 2 + y)
        needs = [
            modulo(pick(home, modulo(h + step, hs) * 2 + y), 2) == y for step in range(hs)
        ]
        sources = [pick(dealing, h * 2 + target) for target in (y, 1 - y)]
        steps = [modulo(h - lax.shift_right_logical(source, 1) + hs, hs) for source in sources]
        here = pick(dealing, h * 2 + l)
        return (
            [self.slot_(offset, back) for back in (False, True) for offset in self.offsets]
            + [l == y, modulo(h - lax.shift_right_logical(own, 1) + hs, hs), modulo(here, 2) == l]
            + steps
            + needs
        )

    def set_plan(self, plan):
        self.slots = {False: plan[: self.members], True: plan[self.members : 2 * self.members]}
        rest = plan[2 * self.members :]
        self.same, self.in_step, self.out_first = rest[:3]
        self.out_steps, self.needs = rest[3:5], rest[5:]

    def slot_(self, offset, back):
        ls, xs = self.sizes["l"], self.sizes["x"]
        dl, dx = offset
        if back:
            dl, dx = -dl, -dx
        return modulo(self.at["l"] + dl + ls, ls) * xs + modulo(self.at["x"] + dx + xs, xs)


def fence(*values):
    return lax.optimization_barrier(values)


def swap_home(value):
    return lax.ppermute(value, ("l", "y"), [(1, 2), (2, 1)])


def swapped_home(team, value, moved):
    return jnp.where(team.same, value, moved)


def team_pieces(team, piece):
    far = team.shift(piece, (1, 0))
    across_x = [(0, dx) for dx in range(1, team.sizes["x"])]
    return (
        [piece]
        + [team.shift(piece, offset) for offset in across_x]
        + [far]
        + [team.shift(far, offset) for offset in across_x]
    )


def cores(team, value):
    return [team.ring(value, "tp", step) for step in range(1, team.sizes["tp"])]


def row_blocks(team):
    ts = team.sizes["tp"]
    return [
        team.slot(offset) * ts + modulo(team.at["tp"] - step + ts, ts)
        for step in range(ts)
        for offset in team.offsets
    ]


def core_send(team, rows, pieces, half_rows, *others):
    sent = [spread(rows, step, pieces, half_rows) for step in range(1, team.sizes["tp"])]
    sent = fence(*sent, *others)[: len(sent)]
    return [team.ring(value, "tp", -step) for step, value in enumerate(sent, 1)]


def core_total(team, rows, pieces, half_rows, got):
    total, *sent = spread(rows, 0, pieces, half_rows, got, team.members)
    return total, sent


def team_send_direct(team, sent):
    return [
        team.shift(value, offset, back=True) for value, offset in zip(sent, team.offsets[1:])
    ]


def team_send(team, sent):
    xs = team.sizes["x"]
    across_x = [(0, dx) for dx in range(1, xs)]
    far = sent[xs - 1].astype(WIDE)
    for value, offset in zip(sent[xs:], across_x):
        far = far + team.shift(value, offset, back=True).astype(WIDE)
    got = [team.shift(value, offset, back=True) for value, offset in zip(sent, across_x)]
    return got + [team.shift(far.astype(LOWER), (1, 0), back=True)]


def team_total(own, got):
    for value in got:
        own = own + value.astype(WIDE)
    return own


def put(buffer, value, starts):
    return lax.dynamic_update_slice(buffer, value, starts)


def share_columns(team, shards):
    widths = [shard.shape[1] // team.members for shard in shards]
    pieces = []
    for j, offset in enumerate(team.offsets):
        slot = team.slot(offset, back=False)
        cuts = [
            lax.dynamic_slice_in_dim(shard, slot * each, each, 1)
            for shard, each in zip(shards, widths)
        ]
        piece = jnp.concatenate(cuts, axis=1)
        pieces.append(team.shift(piece, offset) if j > 0 else piece)
    return pieces


def place_rows_kernel(widths, slots_ref, *refs):
    pieces, outs = refs[: len(refs) - len(widths)], refs[len(refs) - len(widths) :]
    for j, piece in enumerate(pieces):
        height = piece.shape[0]
        row = pl.multiple_of(slots_ref[j] * height, height)
        first = 0
        for out, width in zip(outs, widths):
            out[pl.ds(row, height), :] = piece[:, first : first + width]
            first += width


def place_columns_kernel(widths, slots_ref, *refs):
    pieces, outs = refs[: len(refs) - len(widths)], refs[len(refs) - len(widths) :]
    for j, piece in enumerate(pieces):
        first = 0
        for out, width in zip(outs, widths):
            column = pl.multiple_of(slots_ref[j] * width, width)
            block = piece[:, first : first + width].astype(out.dtype)
            out[:, pl.ds(column, width)] = block
            first += width


def place(team, kernel, pieces, widths, shapes):
    slots = jnp.stack([team.slot(offset) for offset in team.offsets]).astype(jnp.int32)
    whole = [pl.BlockSpec(piece.shape, lambda n: (0, 0)) for piece in pieces]
    return pl.pallas_call(
        kernel if widths is None else functools.partial(kernel, widths),
        grid=(1,),
        in_specs=[pl.BlockSpec(memory_space=pltpu.SMEM)] + whole,
        out_specs=[pl.BlockSpec(shape.shape, lambda n: (0, 0)) for shape in shapes],
        out_shape=shapes,
        cost_estimate=LIGHT,
        compiler_params=KERNEL,
    )(slots, *pieces)


def stack_rows_kernel(*refs):
    height = refs[0].shape[0]
    for j, piece in enumerate(refs[:-1]):
        refs[-1][j * height : (j + 1) * height, :] = piece[...]


def stack_rows(pieces):
    height, width = pieces[0].shape
    rows = height * len(pieces)
    return pl.pallas_call(
        stack_rows_kernel,
        grid=(1,),
        in_specs=[pl.BlockSpec((height, width), lambda n: (0, 0)) for _ in pieces],
        out_specs=pl.BlockSpec((rows, width), lambda n: (0, 0)),
        out_shape=jax.ShapeDtypeStruct((rows, width), pieces[0].dtype),
        cost_estimate=LIGHT,
        compiler_params=KERNEL,
    )(*pieces)


def place_halves_kernel(slots_ref, *refs):
    pieces, outs = refs[:-2], refs[-2:]
    split = len(pieces) // 2
    for j, piece in enumerate(pieces):
        height = piece.shape[0]
        for part, out in enumerate(outs):

            @pl.when(lax.div(slots_ref[j], split) == part)
            def _():
                row = pl.multiple_of(lax.rem(slots_ref[j], split) * height, height)
                out[pl.ds(row, height), :] = piece[...]


def near_rows(team, pieces, parts=1):
    height, width = pieces[0].shape
    shape = jax.ShapeDtypeStruct((height * team.members // parts, width), LOWER)
    if parts == 1:
        return place(team, place_rows_kernel, pieces, [width], [shape])
    return place(team, place_halves_kernel, pieces, None, [shape] * 2)


def across(team, value):
    return [team.ring(value, "h", -step) for step in range(1, team.sizes["h"])]


def beside(team, values):
    return [team.ring(value, "y", 1) for value in values]


def halves(value):
    middle = value.shape[0] // 2
    return value[:middle], value[middle:]


def pairs(firsts, seconds):
    return [part for pair in zip(firsts, seconds) for part in pair]


def add_ring(team, value, name):
    return value + sum(team.ring(value, name, step) for step in range(1, team.sizes[name]))


class Grads:
    def __init__(self, team, lefts, rights):
        self.team, self.lefts, self.rights = team, lefts, rights
        self.far = lefts[0].shape[1] // 2
        self.near = self.far // team.sizes["h"]

        self.half = self.near // 2
        self.steps = range(1, team.sizes["h"])

    def rows(self, first, count, adds=(), offset=0, column=0):
        return outer(self.lefts, self.rights, first, count, adds, offset, column)

    def send_far(self):
        return self.rows(self.far + self.near, self.far - self.near)

    def send_half(self, part):
        start = self.far + part * self.half
        return [self.rows(start + step * self.near, self.half) for step in self.steps]

    def send_near(self):
        return self.rows(self.far, self.near)

    def cross(self, got):
        offsets = [(step - 1) * self.near for step in self.steps]
        return [self.rows(self.near + first, self.near, [got], first) for first in offsets]

    def cross_half(self, part, got):
        offsets = [(step - 1) * self.near + part * self.half for step in self.steps]
        return [self.rows(self.near + first, self.half, [got], first) for first in offsets]

    def cross_halves(self, part, gots):
        start = part * self.half
        return [
            self.rows(start + step * self.near, self.half, [got])
            for step, got in zip(self.steps, gots)
        ]

    def go(self, sent):
        return [self.team.ring(value, "h", step) for step, value in zip(self.steps, sent)]

    def total(self, got, crossed, column=0):
        return self.rows(0, self.near, [got, *crossed], column=column)


def home_pieces(team, total):
    height = total.shape[0] // team.members
    total = total.reshape(team.members, height, -1)
    pieces = []
    for j, offset in enumerate(team.offsets):
        piece = lax.dynamic_index_in_dim(total, team.slot(offset, back=False), 0, False)
        pieces.append(team.shift(piece, offset) if j > 0 else piece)
    return pieces


def home_join(team, pieces, widths):
    height = pieces[0].shape[0]
    shapes = [jax.ShapeDtypeStruct((height, width * team.members), WIDE) for width in widths]
    return place(team, place_columns_kernel, pieces, widths, shapes)


def permute_kernel(count, table_ref, value_ref, out_ref):
    block = value_ref.shape[1] // count
    for i in range(count):
        column = pl.multiple_of(table_ref[i] * block, block)
        out_ref[:, i * block : (i + 1) * block] = value_ref[:, pl.ds(column, block)]


def permute_columns(value, table):
    whole = pl.BlockSpec(value.shape, lambda n: (0, 0))
    return pl.pallas_call(
        functools.partial(permute_kernel, len(table)),
        grid=(1,),
        in_specs=[pl.BlockSpec(memory_space=pltpu.SMEM), whole],
        out_specs=whole,
        out_shape=jax.ShapeDtypeStruct(value.shape, value.dtype),
        cost_estimate=LIGHT,
    )(jnp.stack(table).astype(jnp.int32), value)


def to_team_order(team, value):
    hs = team.sizes["h"]
    table = []
    for dy in range(2):
        for dh in range(hs):
            for l in range(2):
                h, y = modulo(team.at["h"] + dh, hs), modulo(team.at["y"] + dy, 2)
                table.append((h * 2 + l) * 2 + y)
    return permute_columns(value, table)


def from_team_order(team, value):
    hs = team.sizes["h"]
    table = []
    for h in range(hs):
        for l in range(2):
            for y in range(2):
                dh, dy = modulo(h - team.at["h"] + hs, hs), modulo(y - team.at["y"] + 2, 2)
                table.append((dy * hs + dh) * 2 + l)
    return permute_columns(value, table)


def pick(table, index):
    ids = jnp.arange(table.shape[0], dtype=jnp.int32)
    return jnp.sum(jnp.where(ids == index, table, 0))


def choose(pieces, index):
    out = pieces[0]
    for i in range(1, len(pieces)):
        out = jnp.where(index == i, pieces[i], out)
    return out


def spread_h(team, piece):
    return [piece] + [team.ring(piece, "h", step) for step in range(1, team.sizes["h"])]


def deal_flip(team, piece, flip):
    if flip == 0:
        return swap_home(piece)
    perm = [(l * 2 + y, y * 2 + 1 - l) for l in range(2) for y in range(2)]
    with jax.named_scope("flip"):
        return lax.ppermute(piece, ("l", "y"), perm)


def deal_across(team, two):
    first = swapped_home(team, two[0], two[1])
    chosen = [jnp.where(need, first, two[2]) for need in team.needs]
    return chosen[:1] + [team.ring(value, "h", step) for step, value in enumerate(chosen) if step]


def dealt_in(team, pieces):
    return choose(pieces, team.in_step)


def deal(team, pieces):
    first, second = (choose(pieces, step) for step in team.out_steps)
    return first, swap_home(first), second


def deal_second(value):
    perm = [(l * 2 + y, (1 - y) * 2 + l) for l in range(2) for y in range(2)]
    return lax.ppermute(value, ("l", "y"), perm)


def dealt_out(team, got):
    return jnp.where(team.out_first, swapped_home(team, got[0], got[1]), got[2])


def join_cores(team, piece):
    ts = team.sizes["tp"]
    out = jnp.zeros((ts,) + piece.shape, piece.dtype)
    for step in range(ts):
        other = team.ring(piece, "tp", step) if step else piece
        out = put(out, other[None], (modulo(team.at["tp"] - step + ts, ts), 0, 0))
    return out.reshape(-1, piece.shape[-1])


def layer_norm(inputs, gain_vec, shift_vec):
    row_mean = jnp.mean(inputs, axis=-1, keepdims=True)
    centred = inputs - row_mean
    spread = jnp.mean(centred * centred, axis=-1, keepdims=True)
    rate = lax.rsqrt(spread + EPSILON)
    xhat = centred * rate
    return xhat * gain_vec + shift_vec, xhat, rate


def layer_norm_back(grad, gain_vec, xhat, rate):
    scaled = grad * gain_vec
    return rate * (
        scaled
        - jnp.mean(scaled, axis=-1, keepdims=True)
        - xhat * jnp.mean(scaled * xhat, axis=-1, keepdims=True)
    )


def gelu_tanh(inputs):
    return jax.nn.gelu(inputs, approximate=True)


def masked_scores(key_ref, query, limits_ref, scale):
    count = limits_ref.shape[0]
    height = key_ref.shape[0] // count
    blocks = []
    for j in range(count):
        block = mm_nt(key_ref[j * height : (j + 1) * height, :], query) * scale
        row = lax.broadcasted_iota(jnp.int32, block.shape, 0)
        blocks.append(jnp.where(row < limits_ref[j], block, NEGATIVE))
    return blocks


def attend_kernel(scale, limits_ref, query_ref, key_ref, value_ref, out_ref, log_ref):
    blocks = masked_scores(key_ref, query_ref[...], limits_ref, scale)
    row_max = functools.reduce(jnp.maximum, blocks)
    row_max = jnp.max(row_max, axis=0, keepdims=True)
    blocks = [jnp.exp(block - row_max) for block in blocks]
    total = jnp.sum(functools.reduce(jnp.add, blocks), axis=0, keepdims=True)
    inverse = 1.0 / total
    height = key_ref.shape[0] // len(blocks)
    out = None
    for j, block in enumerate(blocks):
        value = value_ref[j * height : (j + 1) * height, :]
        term = mm_tn(value, (block * inverse).astype(LOWER))
        out = term if out is None else out + term
    out_ref[...] = out.T.astype(LOWER)
    log_ref[0] = row_max + jnp.log(total)


def attend_back_kernel(
    scale, wide, limits_ref, query_ref, key_ref, value_ref, grad_ref, log_ref, out_ref, key_sum, value_sum
):
    head, step = pl.program_id(0), pl.program_id(1)
    query, grad = query_ref[...], grad_ref[...]
    blocks = masked_scores(key_ref, query, limits_ref, scale)
    count = len(blocks)
    height = key_ref.shape[0] // count
    part = [slice(j * height, (j + 1) * height) for j in range(count)]
    log_sum = log_ref[0]
    probs = [jnp.exp(block - log_sum) for block in blocks]
    grad_probs = [mm_nt(value_ref[rows, :], grad) for rows in part]
    delta = functools.reduce(jnp.add, [p * g for p, g in zip(probs, grad_probs)])
    delta = jnp.sum(delta, axis=0, keepdims=True)

    @pl.when(step == 0)
    def _():
        key_sum[...] = jnp.zeros_like(key_sum)
        value_sum[...] = jnp.zeros_like(value_sum)

    grad_query = None
    for j, rows in enumerate(part):
        scores = (probs[j] * (grad_probs[j] - delta)).astype(LOWER)
        term = mm_tn(key_ref[rows, :], scores)
        grad_query = term if grad_query is None else grad_query + term
        key_sum[rows, :] += mm(scores, query)
        value_sum[rows, :] += mm(probs[j].astype(LOWER), grad)
    count = query.shape[0]
    first = pl.multiple_of(step * count, count)
    column = pl.multiple_of(head * HEAD, HEAD)
    out_ref[pl.ds(first, count), pl.ds(column, HEAD)] = (grad_query.T * scale).astype(LOWER)

    @pl.when(step == pl.num_programs(1) - 1)
    def _():
        out_ref[:, pl.ds(wide + column, HEAD)] = (key_sum[...] * scale).astype(LOWER)
        out_ref[:, pl.ds(2 * wide + column, HEAD)] = value_sum[...].astype(LOWER)


LIGHT = pl.CostEstimate(flops=1000000, bytes_accessed=100000, transcendentals=0)
KERNEL = pltpu.CompilerParams(vmem_limit_bytes=12 * 1024 * 1024)


def gelu_slope(value):
    inner = math.sqrt(2.0 / math.pi)
    square = value * value
    tanh = jnp.tanh(inner * value * (1.0 + 0.044715 * square))
    return 0.5 * (1.0 + tanh) + 0.5 * value * (1.0 - tanh * tanh) * inner * (
        1.0 + 3.0 * 0.044715 * square
    )


def project_kernel(mode, part_count, piece_count, steps, *refs):
    parts, pieces = refs[:part_count], refs[part_count : part_count + piece_count]
    rest = refs[part_count + piece_count :]
    index = pl.program_id(0)

    def run(rows):
        total = None
        first = 0
        for piece in pieces:
            depth = piece.shape[0]
            term = mm(rows[:, first : first + depth], piece[...])
            total = term if total is None else total + term
            first += depth
        if mode == "bias":
            rest[1][...] = (total + rest[0][...]).astype(LOWER)
        elif mode == "gelu":
            total = total + rest[0][...]
            rest[1][...] = total
            rest[2][...] = gelu_tanh(total).astype(LOWER)
        elif mode == "slope":
            rest[1][...] = (total * gelu_slope(rest[0][...])).astype(LOWER)
        else:
            rest[0][...] = total.astype(LOWER)

    for place in range(part_count):

        @pl.when(index // steps == place)
        def _():
            run(parts[place][...])


def project(mode, parts, pieces, width, extra=None):
    half_rows, depth = parts[0].shape
    block = min(256, half_rows)
    steps = half_rows // block
    rows = half_rows * len(parts)

    def part_at(place):
        return lambda i: (jnp.clip(i - place * steps, 0, steps - 1), 0)

    in_specs = [pl.BlockSpec((block, depth), part_at(place)) for place in range(len(parts))]
    for array, column in pieces:
        in_specs.append(
            pl.BlockSpec((array.shape[0], width), functools.partial(lambda c, i: (0, c), column))
        )
    arrays = list(parts) + [array for array, _ in pieces]
    tile = pl.BlockSpec((block, width), lambda i: (i, 0))
    if mode in ("bias", "gelu"):
        in_specs.append(pl.BlockSpec((1, width), lambda i: (0, 0)))
        arrays.append(extra[None])
    elif mode == "slope":
        in_specs.append(tile)
        arrays.append(extra)
    shapes = [jax.ShapeDtypeStruct((rows, width), LOWER)]
    if mode == "gelu":
        shapes = [jax.ShapeDtypeStruct((rows, width), WIDE)] + shapes
    return pl.pallas_call(
        functools.partial(project_kernel, mode, len(parts), len(pieces), steps),
        grid=(len(parts) * steps,),
        in_specs=in_specs,
        out_specs=[tile] * len(shapes),
        out_shape=shapes,
        cost_estimate=LIGHT,
        compiler_params=KERNEL,
    )(*arrays)


def spread_kernel(piece_count, got_count, members, rows_ref, *refs):
    pieces, gots = refs[:piece_count], refs[piece_count : piece_count + got_count]
    outs = refs[piece_count + got_count :]
    rows = rows_ref[...]
    height = rows.shape[0] // members
    first = 0
    for piece in pieces:
        columns = slice(first, first + piece.shape[0])
        total = mm_nt(rows, piece[...])
        for got in gots:
            total = total + got[:, columns].astype(WIDE)
        for j, out in enumerate(outs):
            out[:, columns] = total[j * height : (j + 1) * height].astype(out.dtype)
        first += piece.shape[0]


def spread(rows, place, pieces, half_rows, got=(), members=0):
    if isinstance(rows, (list, tuple)):
        rows, place = rows[place], 0
    depth = rows.shape[1]
    width = sum(array.shape[0] for array, _ in pieces)
    in_specs = [pl.BlockSpec((half_rows, depth), lambda n: (place, 0))]
    for array, column in pieces:
        in_specs.append(
            pl.BlockSpec((array.shape[0], depth), functools.partial(lambda c, n: (0, c), column))
        )
    in_specs += [pl.BlockSpec((half_rows, width), lambda n: (0, 0))] * len(got)
    split = max(members, 1)
    height = half_rows // split
    dtypes = [WIDE] + [LOWER] * (members - 1) if members else [LOWER]
    out = pl.pallas_call(
        functools.partial(spread_kernel, len(pieces), len(got), split),
        grid=(1,),
        in_specs=in_specs,
        out_specs=[pl.BlockSpec((height, width), lambda n: (0, 0))] * split,
        out_shape=[jax.ShapeDtypeStruct((height, width), dtype) for dtype in dtypes],
        cost_estimate=LIGHT,
        compiler_params=KERNEL,
    )(rows, *[array for array, _ in pieces], *got)
    return out if members else out[0]


def outer_kernel(part_count, add_count, *refs):
    lefts, rights = refs[:part_count], refs[part_count : 2 * part_count]
    adds, out = refs[2 * part_count : 2 * part_count + add_count], refs[-1]
    total = None
    for left, right in zip(lefts, rights):
        term = mm_tn(left[...], right[...])
        total = term if total is None else total + term
    for add in adds:
        total = total + add[...].astype(WIDE)
    out[...] = total.astype(out.dtype)


def outer(lefts, rights, first, count, adds, offset, column):
    height = lefts[0].shape[0]
    rights = [right if isinstance(right, tuple) else (right, 0) for right in rights]
    width = rights[0][0].shape[1]
    block = math.gcd(256, count)
    in_specs = [pl.BlockSpec((height, block), lambda i: (0, first // block + i)) for _ in lefts]
    for _, row in rights:
        in_specs.append(
            pl.BlockSpec((height, width), functools.partial(lambda r, i: (r, 0), row))
        )
    tile = pl.BlockSpec((block, width), lambda i: (i, 0))
    add_tile = pl.BlockSpec((block, width), lambda i: (offset // block + i, 0))
    first_tile = pl.BlockSpec((block, width), lambda i: (offset // block + i, column))
    return pl.pallas_call(
        functools.partial(outer_kernel, len(lefts), len(adds)),
        grid=(count // block,),
        in_specs=in_specs + [first_tile] * len(adds[:1]) + [add_tile] * len(adds[1:]),
        out_specs=tile,
        out_shape=jax.ShapeDtypeStruct((count, width), LOWER),
        cost_estimate=LIGHT,
        compiler_params=KERNEL,
    )(*lefts, *[right for right, _ in rights], *adds)


def query_block(rows):
    return min(512, rows)


def attend(qkv, limits, scale):
    rows, wide = qkv.shape[0], qkv.shape[1] // 3
    heads, block = wide // HEAD, query_block(rows)
    return pl.pallas_call(
        functools.partial(attend_kernel, scale),
        grid=(heads, rows // block),
        in_specs=[
            pl.BlockSpec(memory_space=pltpu.SMEM),
            pl.BlockSpec((block, HEAD), lambda h, i: (i, h)),
            pl.BlockSpec((rows, HEAD), lambda h, i: (0, heads + h)),
            pl.BlockSpec((rows, HEAD), lambda h, i: (0, 2 * heads + h)),
        ],
        out_specs=[
            pl.BlockSpec((block, HEAD), lambda h, i: (i, h)),
            pl.BlockSpec((1, 1, block), lambda h, i: (h, 0, i)),
        ],
        out_shape=[
            jax.ShapeDtypeStruct((rows, wide), LOWER),
            jax.ShapeDtypeStruct((heads, 1, rows), WIDE),
        ],
        cost_estimate=LIGHT,
        compiler_params=KERNEL,
    )(limits, qkv, qkv, qkv)


def attend_back(qkv, grad, log_sum, limits, scale):
    rows, wide = grad.shape
    heads, block = wide // HEAD, query_block(rows)
    return pl.pallas_call(
        functools.partial(attend_back_kernel, scale, wide),
        grid=(heads, rows // block),
        in_specs=[
            pl.BlockSpec(memory_space=pltpu.SMEM),
            pl.BlockSpec((block, HEAD), lambda h, i: (i, h)),
            pl.BlockSpec((rows, HEAD), lambda h, i: (0, heads + h)),
            pl.BlockSpec((rows, HEAD), lambda h, i: (0, 2 * heads + h)),
            pl.BlockSpec((block, HEAD), lambda h, i: (i, h)),
            pl.BlockSpec((1, 1, block), lambda h, i: (h, 0, i)),
        ],
        out_specs=pl.BlockSpec((rows, 3 * wide), lambda h, i: (0, 0)),
        out_shape=jax.ShapeDtypeStruct((rows, 3 * wide), LOWER),
        scratch_shapes=[pltpu.VMEM((rows, HEAD), WIDE), pltpu.VMEM((rows, HEAD), WIDE)],
        cost_estimate=LIGHT,
        compiler_params=KERNEL,
    )(limits, qkv, qkv, qkv, grad, log_sum)


def local(
    tokens,
    lengths,
    dealing,
    w_query,
    w_key,
    w_value,
    w_out,
    b_query,
    b_value,
    b_out,
    gain_mid,
    shift_mid,
    w_up,
    b_up,
    w_down,
    b_down,
    gain_end,
    shift_end,
    cotangent,
):
    team = Team()
    ts, members = team.sizes["tp"], team.members
    row_count = tokens.shape[0] // ts
    wide = w_query.shape[1] // members
    tall = w_up.shape[1] // members
    width = tokens.shape[1]
    score_scale = 1.0 / math.sqrt(HEAD)
    my_slot = team.at["l"] * team.sizes["x"] + team.at["x"]
    seq_ids = jnp.arange(dealing.shape[0], dtype=jnp.int32)
    home = jnp.sum(jnp.where(dealing[None, :] == seq_ids[:, None], seq_ids[None, :], 0), axis=1)
    plan = team.plan(dealing, home)
    team.set_plan(plan)
    live_count = pick(lengths, team.at["h"] * 2 + team.at["y"])
    limits = live_count - jnp.stack(row_blocks(team)).astype(jnp.int32) * row_count
    query_live = (jnp.arange(row_count, dtype=jnp.int32) < limits[0])[:, None]
    half_at = team.at["tp"] * row_count

    half_rows = members * row_count
    vectors = jnp.stack([b_out, gain_mid, shift_mid, b_down, gain_end, shift_end])
    b_out, gain_mid, shift_mid, b_down, gain_end, shift_end = to_team_order(team, vectors)
    bias_q = lax.dynamic_slice_in_dim(b_query, my_slot * wide, wide, 0)
    bias_v = lax.dynamic_slice_in_dim(b_value, my_slot * wide, wide, 0)
    bias_up = lax.dynamic_slice_in_dim(b_up, my_slot * tall, tall, 0)
    bias_qkv = jnp.concatenate([bias_q, jnp.zeros_like(bias_q), bias_v])
    steps = team.sizes["h"] - 1
    team_count = team.sizes["x"]


    def first_column(arrays):
        return [(array, 0) for array in arrays]

    with jax.named_scope("a0"):
        mine = lax.dynamic_slice_in_dim(tokens, half_at, row_count, 0)
        own = swap_home(mine)
        w_query, w_key, w_value, w_out = fence(w_query, w_key, w_value, w_out, mine)[:4]
        share = share_columns(team, [w_query, w_key, w_value, w_out])
        own, w_up, w_down, bias_qkv, bias_up, limits, query_live, *rest = fence(
            own, w_up, w_down, bias_qkv, bias_up, limits, query_live, *share, *plan
        )
        share, plan = rest[:members], rest[members:]
        team.set_plan(plan)
    with jax.named_scope("a1"):
        own = to_team_order(team, swapped_home(team, mine, own))
        (near_att,) = near_rows(team, share)
        pieces = team_pieces(team, own)
        cross_qkv = across(team, near_att[:, : 3 * wide])
        (side_att,) = beside(team, [near_att])
        near_att, w_up, w_down, cotangent, side_att, *rest = fence(
            near_att, w_up, w_down, cotangent, side_att, *pieces, *cross_qkv
        )
        pieces, cross_qkv = rest[:members], rest[members:]
    with jax.named_scope("a2"):
        half = stack_rows(pieces)
        other = cores(team, half)
        far_qkv = beside(team, cross_qkv)
        cross_out = across(team, near_att[:, 3 * wide :])
        share = share_columns(team, [w_up])
        cotangent, w_down, *rest = fence(
            cotangent, w_down, half, *other, *share, *far_qkv, *cross_out
        )
        in_parts = rest[:ts]
        share, rest = rest[ts : ts + members], rest[ts + members :]
        far_qkv, cross_out = rest[:steps], rest[steps:]
    qkv_mat = first_column([near_att, *cross_qkv, side_att, *far_qkv])
    with jax.named_scope("c1"):
        up_a, up_b = near_rows(team, share, 2)
        cross_up_a = across(team, up_a)
        far_out = beside(team, cross_out)
        cot_half = lax.dynamic_slice_in_dim(cotangent, half_at, row_count, 0)
        share = share_columns(team, [w_down])
        (qkv,) = project("bias", in_parts, qkv_mat, 3 * wide, bias_qkv)
        attended, log_sum = attend(qkv, limits, score_scale)
        out_mat = [(near_att, 3), *first_column(cross_out), (side_att, 3), *first_column(far_out)]
        got = core_send(team, attended, out_mat, half_rows, *cross_up_a, *share)
        total, sent = core_total(team, attended, out_mat, half_rows, got)
        up_a, up_b, cot_half, *rest = fence(
            up_a, up_b, cot_half, *cross_up_a, *share, *sent
        )
        cross_up_a, rest = rest[:steps], rest[steps:]
        share, sent = rest[:members], rest[members:]
    with jax.named_scope("s3"):
        got = team_send(team, sent)
        cross_up_b = across(team, up_b)
        down_a, down_b = near_rows(team, share, 2)
        side = beside(team, [jnp.concatenate([up_a, *cross_up_a], axis=0)])
        cot_one = deal_flip(team, cot_half, 0)
        cot_half, cot_one, up_b, down_a, down_b, *rest = fence(
            cot_half, cot_one, up_b, down_a, down_b, *got, *cross_up_b, *side
        )
        got, rest = rest[:team_count], rest[team_count:]
        cross_up_b, side_a = rest[:steps], rest[steps]
    with jax.named_scope("s4"):
        branch = team_total(total, got) + b_out
        middle, mid_hat, mid_rate = layer_norm(own.astype(WIDE) + branch, gain_mid, shift_mid)
        pieces = team_pieces(team, middle.astype(LOWER))
        cross_down_a = across(team, down_a)
        side = beside(team, [jnp.concatenate([up_b, *cross_up_b], axis=0)])
        cot_two = [cot_half, cot_one, deal_flip(team, cot_half, 1)]
        down_a, down_b, *rest = fence(
            down_a, down_b, *cot_two, *pieces, *cross_down_a, *side
        )
        cot_two, rest = rest[:3], rest[3:]
        pieces, rest = rest[:members], rest[members:]
        cross_down_a, side_b = rest[:steps], rest[steps]
    part_rows = down_a.shape[0]

    def split_side(side):
        blocks = [side[k * part_rows : (k + 1) * part_rows] for k in range(steps + 1)]
        return blocks[0], blocks[1:]

    side_up_a, far_up_a = split_side(side_a)
    side_up_b, far_up_b = split_side(side_b)
    up_mat = first_column(
        [up_a, up_b]
        + pairs(cross_up_a, cross_up_b)
        + [side_up_a, side_up_b]
        + pairs(far_up_a, far_up_b)
    )
    with jax.named_scope("c2"):
        half = stack_rows(pieces)
        other = cores(team, half)
        cross_down_b = across(team, down_b)
        side = beside(team, [jnp.concatenate([down_a, *cross_down_a], axis=0)])
        mid_parts = [half] + other
        hidden, active = [], []
        for part in mid_parts:
            hidden_part, active_part = project("gelu", [part], up_mat, tall, bias_up)
            hidden.append(hidden_part)
            active.append(active_part)
        down_b, *rest = fence(down_b, *active, *cross_down_b, *side, *cot_two)
        active, rest = rest[:ts], rest[ts:]
        cross_down_b, side, cot_two = rest[:steps], rest[steps], rest[steps + 1 :]
        side_down_a, far_down_a = split_side(side)
    with jax.named_scope("s5"):
        (side,) = beside(team, [jnp.concatenate([down_b, *cross_down_b], axis=0)])
        side_down_b, far_down_b = split_side(side)
        cot_pieces = deal_across(team, cot_two)
        down_mat = first_column(
            [down_a, down_b]
            + pairs(cross_down_a, cross_down_b)
            + [side_down_a, side_down_b]
            + pairs(far_down_a, far_down_b)
        )
        got = core_send(team, active, down_mat, half_rows, *cot_pieces)
        total, sent = core_total(team, active, down_mat, half_rows, got)
        rest = fence(*sent, *cot_pieces)
        sent, cot_pieces = rest[: members - 1], rest[members - 1 :]
    with jax.named_scope("s6"):
        cot = to_team_order(team, dealt_in(team, cot_pieces))
        cot, *got = fence(cot, *team_send_direct(team, sent))
    with jax.named_scope("s7"):
        result = team_total(total, got) + b_down
        normed, end_hat, end_rate = layer_norm(middle + result, gain_end, shift_end)
        output_own = jnp.where(query_live, normed, 0.0).astype(LOWER)
        grad_normed = jnp.where(query_live, cot.astype(WIDE), 0.0)
        grad_sum = layer_norm_back(grad_normed, gain_end, end_hat, end_rate)
        grad_result = grad_sum.astype(LOWER)
        pieces = team_pieces(team, grad_result)
        out_pieces = spread_h(team, from_team_order(team, output_own))
        rest = fence(*pieces, *out_pieces)
        pieces, out_pieces = rest[:members], rest[members:]
        grad_gend = jnp.sum(grad_normed * end_hat, axis=0)
        grad_send = jnp.sum(grad_normed, axis=0)
        grad_bdown = jnp.sum(grad_result.astype(WIDE), axis=0)
    with jax.named_scope("c3"):
        half = stack_rows(pieces)
        other = cores(team, half)
        result_parts = [half] + other
        flow_down = Grads(team, result_parts, active)
        far_down_a = beside(team, flow_down.send_half(0))
        grad_hidden = []
        for part, hidden_part in zip(result_parts, hidden):
            grad_hidden += project("slope", [part], down_mat, tall, hidden_part)
        got = core_send(team, grad_hidden, up_mat, half_rows, *far_down_a, *grad_hidden)
        total, sent = core_total(team, grad_hidden, up_mat, half_rows, got)
        cross_down = flow_down.cross_halves(0, far_down_a)
        flow_up = Grads(team, mid_parts, grad_hidden)
        rest = fence(*sent, *cross_down)
        sent, cross_down = rest[: members - 1], rest[members - 1 :]
    with jax.named_scope("s8"):
        got = team_send(team, sent)
        got_down_a = flow_down.go(cross_down)
        far_down_b = beside(team, flow_down.send_half(1))
        far_up, *far_down_b = fence(flow_up.send_far(), *far_down_b)
        (far_up,) = beside(team, [far_up])
        cross_down = flow_down.cross_halves(1, far_down_b)
        far_up, *rest = fence(far_up, *got, *got_down_a, *cross_down)
        got, rest = rest[:team_count], rest[team_count:]
        got_down_a, cross_down = rest[:steps], rest[steps:]
    with jax.named_scope("s9"):
        grad_middle = team_total(total, got) + grad_sum
        grad_inner = layer_norm_back(grad_middle, gain_mid, mid_hat, mid_rate)
        grad_branch = grad_inner.astype(LOWER)
        pieces = team_pieces(team, grad_branch)
        got_down_b = flow_down.go(cross_down)
        (near_down,) = beside(team, [flow_down.send_near()])
        grad_gmid = jnp.sum(grad_middle * mid_hat, axis=0)
        grad_smid = jnp.sum(grad_middle, axis=0)
        grad_bout = jnp.sum(grad_branch.astype(WIDE), axis=0)
        by_row = jnp.stack([grad_bout, grad_gmid, grad_smid, grad_bdown, grad_gend, grad_send])
        by_row = add_ring(team, from_team_order(team, by_row), "tp")
        out_first, out_swapped, out_second = deal(team, out_pieces)
        cross_up_a, cross_up_b = flow_up.cross_half(0, far_up), flow_up.cross_half(1, far_up)
        by_row, near_down, out_first, out_swapped, out_second, *rest = fence(
            by_row, near_down, out_first, out_swapped, out_second, *pieces, *got_down_b, *cross_up_a, *cross_up_b)
        pieces, rest = rest[:members], rest[members:]
        got_down_b, rest = rest[:steps], rest[steps:]
        cross_up_a, cross_up_b = rest[:steps], rest[steps:]
    with jax.named_scope("c4"):
        half = stack_rows(pieces)
        other = cores(team, half)
        got_up_a, got_up_b = flow_up.go(cross_up_a), flow_up.go(cross_up_b)
        out_two = [out_first, out_swapped, deal_second(out_second)]
        branch_parts = [half] + other
        attended_parts = [(attended, k) for k in range(ts)]
        flow_out = Grads(team, branch_parts, attended_parts)
        (far_out,) = beside(team, [flow_out.send_far()])
        (grad_attended,) = project("plain", branch_parts, out_mat, wide)
        grad_qkv = attend_back(qkv, grad_attended, log_sum, limits, score_scale)
        got = core_send(team, grad_qkv, qkv_mat, half_rows, far_out, *got_up_a, *out_two)
        total, sent = core_total(team, grad_qkv, qkv_mat, half_rows, got)
        grad_parts = [(grad_qkv, k) for k in range(ts)]
        flow_qkv = Grads(team, in_parts, grad_parts)
        qkv_sum = jnp.sum(grad_qkv.astype(WIDE), axis=0)
        grad_bup = sum(jnp.sum(part.astype(WIDE), axis=0) for part in grad_hidden)
        zeros = jnp.zeros((members, 1), WIDE)
        by_slot = [
            put(zeros * part[None], part[None], (my_slot, 0)).reshape(-1)
            for part in (qkv_sum[:wide], qkv_sum[2 * wide :], grad_bup)
        ]
        sums = jnp.concatenate([by_row.reshape(-1)] + by_slot).reshape(-1, 128)
        sums = add_ring(team, sums, "x")
        (far_qkv,) = beside(team, [flow_qkv.send_far()])
        cross_out = flow_out.cross(far_out)
        sums, near_down, far_qkv, *rest = fence(
            sums, near_down, far_qkv, *cross_out, *sent, *got_up_a, *got_up_b, *out_two
        )
        cross_out, rest = rest[:steps], rest[steps:]
        sent, rest = rest[: members - 1], rest[members - 1 :]
        got_up_a, got_up_b, out_two = rest[:steps], rest[steps : 2 * steps], rest[2 * steps :]
    with jax.named_scope("s10"):
        got = team_send(team, sent)
        total_down = flow_down.total(
            near_down,
            [jnp.concatenate(both, axis=0) for both in zip(got_down_a, got_down_b)],
        )
        got_qkv_a = flow_qkv.go(flow_qkv.cross_half(0, far_qkv))
        cross_qkv = flow_qkv.cross_half(1, far_qkv)
        (near_up,) = beside(team, [flow_up.send_near()])
        sums, total_down, near_up, *rest = fence(
            sums, total_down, near_up, *out_two, *got, *got_qkv_a, *cross_qkv, *cross_out
        )
        out_two, rest = rest[:3], rest[3:]
        got, rest = rest[:team_count], rest[team_count:]
        got_qkv_a, cross_qkv, cross_out = rest[:steps], rest[steps : 2 * steps], rest[2 * steps :]
    with jax.named_scope("s11"):
        got_qkv_b = flow_qkv.go(cross_qkv)
        got_out = flow_out.go(cross_out)
        grad_own = (team_total(total, got) + grad_inner).astype(LOWER)
        grad_own = from_team_order(team, grad_own)
        swapped = swap_home(grad_own)
        near_att = jnp.concatenate([flow_qkv.send_near(), flow_out.send_near()], axis=1)
        (near_att,) = beside(team, [near_att])
        total_up = flow_up.total(
            near_up, [jnp.concatenate(both, axis=0) for both in zip(got_up_a, got_up_b)]
        )
        home_both = home_pieces(team, jnp.concatenate([total_down, total_up], axis=1))
        total_out = flow_out.total(near_att, got_out, 3)
        got_qkv = [jnp.concatenate(both, axis=0) for both in zip(got_qkv_a, got_qkv_b)]
        total_qkv = flow_qkv.total(near_att, got_qkv, 0)
        sums, swapped, total_out, total_qkv, *rest = fence(
            sums, swapped, total_out, total_qkv, *home_both, *out_two
        )
        home_both, out_two = rest[:members], rest[members:]
        grad_down, grad_up = home_join(team, home_both, [tall, tall])
    with jax.named_scope("s12"):
        grad_tokens = join_cores(team, swapped_home(team, grad_own, swapped))
        home_att = home_pieces(team, jnp.concatenate([total_qkv, total_out], axis=1))
        output = join_cores(team, dealt_out(team, out_two))
        sums = add_ring(
            team, add_ring(team, add_ring(team, sums, "h"), "y"), "l"
        ).reshape(-1)
        grad_query, grad_key, grad_value, grad_out = home_join(team, home_att, [wide] * 4)
    smalls = []
    first = 0
    for size in [width] * 6 + [b_query.shape[0], b_value.shape[0], b_up.shape[0]]:
        smalls.append(sums[first : first + size])
        first += size
    return (
        output,
        grad_tokens,
        grad_query,
        grad_key,
        grad_value,
        grad_out,
        smalls[6],
        smalls[7],
        smalls[0],
        smalls[1],
        smalls[2],
        grad_up,
        smalls[8],
        grad_down,
        smalls[3],
        smalls[4],
        smalls[5],
    )


def solution(mesh):
    fsdp, ctx, tp = (mesh.shape[name] for name in ("fsdp", "ctx", "tp"))
    fine = Mesh(mesh.devices.reshape(fsdp // 2, 2, 2, ctx // 2, tp), ROWS + ("tp",))
    rows, split = P(ROWS, None), P(ROWS, "tp")
    in_specs = (
        (rows, P(), P())
        + (split,) * 4
        + (P("tp"), P("tp"), P(), P(), P(), split, P("tp"), split, P(), P(), P(), rows)
    )
    out_specs = (
        (rows, rows)
        + (split,) * 4
        + (P("tp"), P("tp"), P(), P(), P(), split, P("tp"), split, P(), P(), P())
    )
    return jax.shard_map(local, mesh=fine, in_specs=in_specs, out_specs=out_specs, check_vma=False)
```
